32 devices in a mesh: seq: 8 (over y, x, core), pos: 4 (over z).
Axes of the slice: x: 2, y: 2, z: 4, core: 2. Of those that a mesh axis runs over, the one named last changes fastest.
Arguments:
- block_input: bfloat16 [8192, 1024], P(('seq', 'pos')), may hold values from -6 to 6
- cotangent: bfloat16 [8192, 1024], P(('seq', 'pos')), may hold values from -6 to 6
- lengths: int32 [8], P('seq'), may hold values from 769 to 1024, as said below
- in_proj: bfloat16 [1024, 3, 1024], P('seq', None, 'pos'), may hold values from -0.1875 to 0.1875
- out_proj: bfloat16 [1024, 1024], P('pos', 'seq'), may hold values from -0.1875 to 0.1875
- up_proj: bfloat16 [1024, 4096], P('seq', 'pos'), may hold values from -0.1875 to 0.1875
- down_proj: bfloat16 [4096, 1024], P('pos', 'seq'), may hold values from -0.09375 to 0.09375
- first_gain: float32 [1024], replicated, may hold values from 0.1 to 1.9
- second_gain: float32 [1024], replicated, may hold values from 0.1 to 1.9
- short_filter: float32 [3, 3072], replicated, may hold values from -3 to 3
- skip_bias: float32 [1024], replicated, may hold values from -4 to 4
- filter_in: float32 [33, 64], replicated, may hold values from -1 to 1
- filter_in_bias: float32 [64], replicated, may hold values from -3.140625 to 3.140625
- filter_mid: float32 [64, 64], replicated, may hold values from -0.75 to 0.75
- filter_mid_bias: float32 [64], replicated, may hold values from -3.140625 to 3.140625
- filter_out: float32 [64, 1024], replicated, may hold values from -0.0625 to 0.0625
Outputs:
- block_output: bfloat16 [8192, 1024], P(('seq', 'pos'))
- input_grad: bfloat16 [8192, 1024], P(('seq', 'pos'))
- in_proj_grad: float32 [1024, 3, 1024], P('seq', None, 'pos')
- out_proj_grad: float32 [1024, 1024], P('pos', 'seq')
- up_proj_grad: float32 [1024, 4096], P('seq', 'pos')
- down_proj_grad: float32 [4096, 1024], P('pos', 'seq')
- first_gain_grad: float32 [1024], replicated
- second_gain_grad: float32 [1024], replicated
- short_filter_grad: float32 [3, 3072], replicated
- skip_bias_grad: float32 [1024], replicated
- filter_in_grad: float32 [33, 64], replicated
- filter_in_bias_grad: float32 [64], replicated
- filter_mid_grad: float32 [64, 64], replicated
- filter_mid_bias_grad: float32 [64], replicated
- filter_out_grad: float32 [64, 1024], replicated
The draws below stay inside these ranges and needn't reach their ends.
Inputs may be any that keep to these rules, and one draw needn't show every extreme that they name: `lengths`: the largest entry is exactly 1024.
All inputs are finite; a program needn't handle non-finite values.
Results may differ from the reference program's by a relative error of at most 0.014.
Values may be sent and summed in bfloat16 or wider, within the bound.
No kernel may reach another device: no remote copies, remote signals or barrier semaphores. Data moves between devices by JAX's collectives and lax.ppermute only.
A program may use at most 192 MiB of HBM per device.

```python
import math
import jax
import jax.numpy as jnp
from jax import lax

D = 1024
FF = 4096
EMB = 33
FH = 64
LSEQ = 1024
SLOTS = 1
SEQS = 8
TOKENS = 8192


def draw_lengths(key, part):
    key = jax.random.fold_in(key, 11)
    first_key, second_key = jax.random.split(key)
    drawn = jax.random.randint(first_key, (SEQS,), 3 * LSEQ // 4 + 1, LSEQ + 1)
    chosen = jax.random.randint(second_key, (), 0, SEQS)
    seq_ids = jnp.arange(SEQS, dtype=jnp.int32)
    return jnp.where(seq_ids == chosen, LSEQ, drawn).astype(jnp.int32)


def steps_of(stream_key, shape, shards, smallest, high):
    factor_of = 1.0
    for dim, parts in shards:
        draws = jax.random.uniform(jax.random.fold_in(jax.random.fold_in(stream_key, 6), dim), (parts,), jnp.float32, smallest / len(shards), high / len(shards))
        factor_of = factor_of * jnp.repeat(jnp.exp(draws), shape[dim] // parts).reshape((-1,) + (1,) * (len(shape) - 1 - dim))
    return factor_of


def bell_draw(stream_key, dims, spread, limit, shards=(), kind=jnp.bfloat16):
    level = steps_of(stream_key, dims, shards, -0.22, 0.18) if shards else 1.0
    values = jax.random.normal(stream_key, dims, jnp.float32) * spread * level
    return jnp.minimum(jnp.maximum(values, -limit), limit).astype(kind)


def setup_inputs(seed: int = 0) -> dict:
    arg_keys = jax.random.split(jax.random.key(seed), 17)
    block_input = bell_draw(arg_keys[0], (TOKENS, D), 1.0, 6.0, ((0, 32),))
    cotangent = bell_draw(arg_keys[1], (TOKENS, D), 1.0, 6.0, ((0, 32),))
    lengths = draw_lengths(jax.random.fold_in(arg_keys[16], 71), 0)
    in_proj = bell_draw(arg_keys[3], (D, 3, D), D ** -0.5, 0.1875, ((0, 8), (2, 4)))
    out_proj = bell_draw(arg_keys[4], (D, D), D ** -0.5, 0.1875, ((0, 4), (1, 8)))
    up_proj = bell_draw(arg_keys[5], (D, FF), D ** -0.5, 0.1875, ((0, 8), (1, 4)))
    down_proj = bell_draw(arg_keys[6], (FF, D), FF ** -0.5, 0.09375, ((0, 4), (1, 8)))
    first_gain = jnp.clip(1.0 + 0.18 * jax.random.normal(arg_keys[7], (D,), jnp.float32), 0.1, 1.9)
    second_gain = jnp.clip(1.0 + 0.18 * jax.random.normal(arg_keys[8], (D,), jnp.float32), 0.1, 1.9)
    short_filter = bell_draw(arg_keys[9], (3, 3 * D), 0.6, 3.0, (), jnp.float32)
    skip_bias = bell_draw(arg_keys[10], (D,), 1.0, 4.0, (), jnp.float32)
    filter_in = bell_draw(arg_keys[11], (EMB, FH), EMB ** -0.5, 1.0, (), jnp.float32)
    filter_in_bias = jnp.clip(jax.random.uniform(arg_keys[12], (FH,), jnp.float32, -3.140625, 3.140625), -3.140625, 3.140625)
    filter_mid = bell_draw(arg_keys[13], (FH, FH), FH ** -0.5, 0.75, (), jnp.float32)
    filter_mid_bias = jnp.clip(jax.random.uniform(arg_keys[14], (FH,), jnp.float32, -3.140625, 3.140625), -3.140625, 3.140625)
    filter_out = bell_draw(arg_keys[15], (FH, D), (FH * LSEQ // 8) ** -0.5, 0.0625, (), jnp.float32)
    return dict(block_input=block_input, cotangent=cotangent, lengths=lengths, in_proj=in_proj, out_proj=out_proj, up_proj=up_proj, down_proj=down_proj, first_gain=first_gain, second_gain=second_gain, short_filter=short_filter, skip_bias=skip_bias, filter_in=filter_in, filter_in_bias=filter_in_bias, filter_mid=filter_mid, filter_mid_bias=filter_mid_bias, filter_out=filter_out)


epsilon = 1e-05
highest = lax.Precision.HIGHEST

@jax.custom_vjp
def low(v):
    return lax.optimization_barrier(v.astype(jnp.bfloat16)).astype(jnp.float32)

@jax.custom_vjp
def low_back(v):
    return v

def low_keep(v):
    return (low(v), None)

def low_pass(kept, grad):
    return (grad,)

def back_keep(v):
    return (v, None)

def back_low(kept, grad):
    return (low(grad),)
low.defvjp(low_keep, low_pass)
low_back.defvjp(back_keep, back_low)

def layer_norm(values, gain_vector):
    row_mean = lax.optimization_barrier(jnp.mean(values, axis=-1, keepdims=True))
    centred = values - row_mean
    scaling = lax.rsqrt(lax.optimization_barrier(jnp.mean(centred * centred, axis=-1, keepdims=True)) + epsilon)
    return centred * scaling * gain_vector

def filter_values(positions, seq_len, channel_start, total_width, filter_in, in_bias, filter_mid, mid_bias, filter_out):
    timeline = positions / (seq_len - 1)
    band_count = (EMB - 1) // 2
    bands = jnp.linspace(0.0001, band_count - 1, band_count)
    angles = 2.0 * math.pi / seq_len * positions
    phases = angles[:, None] * bands[None, :]
    embedded = jnp.concatenate([timeline[:, None], jnp.cos(phases), -jnp.sin(phases)], axis=1)
    hidden = jnp.sin(jnp.dot(embedded, filter_in, precision=highest) + in_bias)
    hidden = jnp.sin(jnp.dot(hidden, filter_mid, precision=highest) + mid_bias)
    raw_taps = jnp.dot(hidden, filter_out, precision=highest)
    channels = (channel_start + jnp.arange(raw_taps.shape[1], dtype=jnp.int32)).astype(positions.dtype)
    slowest = math.log(0.01) / 1.5
    fastest = math.log(0.01) / 0.3
    rates = jnp.abs(slowest + (fastest - slowest) * channels / (total_width - 1))
    return raw_taps * jnp.exp(-timeline[:, None] * rates[None, :])

def block(row_values, seq_lengths, in_proj, out_proj, up_proj, down_proj, first_gain, second_gain, short_filter, skip_bias, filter_in, filter_in_bias, filter_mid, filter_mid_bias, filter_out):
    normed = low(layer_norm(row_values, first_gain))
    projected = low_back(low(jnp.dot(normed, in_proj.reshape(D, 3 * D), precision=highest)))
    streams = projected.reshape(SLOTS, LSEQ, 3, D)
    taps = short_filter.reshape(3, 3, D)
    padded = jnp.pad(streams, ((0, 0), (2, 0), (0, 0), (0, 0)))
    mixed = taps[0] * streams + taps[1] * padded[:, 1:LSEQ + 1] + taps[2] * padded[:, :LSEQ]
    gate_outer = mixed[:, :, 0]
    gate_inner = mixed[:, :, 1]
    stream_values = mixed[:, :, 2]
    valid = (jnp.arange(LSEQ, dtype=jnp.int32)[None, :] < seq_lengths[:, None]).astype(row_values.dtype)
    driven = stream_values * gate_inner * valid[:, :, None]
    positions = jnp.arange(LSEQ, dtype=jnp.int32).astype(row_values.dtype)
    filter_taps = filter_values(positions, LSEQ, 0, D, filter_in, filter_in_bias, filter_mid, filter_mid_bias, filter_out)
    spectrum = jnp.fft.rfft(driven, n=2 * LSEQ, axis=1) * jnp.fft.rfft(filter_taps, n=2 * LSEQ, axis=0)[None]
    long_conv = jnp.fft.irfft(spectrum, n=2 * LSEQ, axis=1)[:, :LSEQ] + skip_bias * driven
    gated = low_back(low(long_conv * gate_outer)).reshape(SLOTS * LSEQ, D)
    residual = row_values + low_back(jnp.dot(gated, out_proj, precision=highest))
    second = low(layer_norm(residual, second_gain))
    pre_act = low_back(jnp.dot(second, up_proj, precision=highest))
    activated = low(jax.nn.gelu(pre_act, approximate=False))
    return residual + low_back(jnp.dot(activated, down_proj, precision=highest))

def reference(block_input, cotangent, lengths, in_proj, out_proj, up_proj, down_proj, first_gain, second_gain, short_filter, skip_bias, filter_in, filter_in_bias, filter_mid, filter_mid_bias, filter_out):
    group_count = SEQS // SLOTS
    group_rows = SLOTS * LSEQ
    weights = (in_proj.astype(jnp.float32), out_proj.astype(jnp.float32), up_proj.astype(jnp.float32), down_proj.astype(jnp.float32), first_gain.astype(jnp.float32), second_gain.astype(jnp.float32), short_filter.astype(jnp.float32), skip_bias.astype(jnp.float32), filter_in.astype(jnp.float32), filter_in_bias.astype(jnp.float32), filter_mid.astype(jnp.float32), filter_mid_bias.astype(jnp.float32), filter_out.astype(jnp.float32))
    inputs = block_input.astype(jnp.float32).reshape(group_count, group_rows, D)
    grads_in = cotangent.astype(jnp.float32).reshape(group_count, group_rows, D)
    group_lengths = lengths.reshape(group_count, SLOTS)

    def each_group(carry, item):
        group_input, group_grad, group_len = item

        def forward(row_values, *params):
            return block(row_values, group_len, *params)
        result, pullback = jax.vjp(forward, group_input, *weights)
        grads = pullback(group_grad)
        summed = tuple((total + piece for total, piece in zip(carry, grads[1:])))
        return (summed, (result.astype(jnp.bfloat16), grads[0].astype(jnp.bfloat16)))
    start = tuple((jnp.zeros_like(weight) for weight in weights))
    totals, (results, input_grads) = lax.scan(each_group, start, (inputs, grads_in, group_lengths))
    return (results.reshape(TOKENS, D), input_grads.reshape(TOKENS, D), totals[0], totals[1], totals[2], totals[3], totals[4], totals[5], totals[6], totals[7], totals[8], totals[9], totals[10], totals[11], totals[12])
```

```python
import math

import jax
import jax.numpy as jnp
import numpy as np
from jax import lax
from jax.sharding import PartitionSpec as P

EMB = 33
LSEQ = 1024
RING = 4
CUBE = 8

epsilon = 1e-05
highest = lax.Precision.HIGHEST
high = lax.Precision.HIGH
f32 = jnp.float32
bf16 = jnp.bfloat16


def row_scale(values):
    row_mean = jnp.mean(values, axis=-1, keepdims=True)
    centred = values - row_mean
    return centred * lax.rsqrt(jnp.mean(centred * centred, axis=-1, keepdims=True) + epsilon)


def exact_gelu(values):
    return jax.nn.gelu(values, approximate=False)


def filter_values(positions, seq_len, rates, filter_in, in_bias, filter_mid, mid_bias, filter_out):
    timeline = positions / (seq_len - 1)
    band_count = (EMB - 1) // 2
    bands = jnp.linspace(0.0001, band_count - 1, band_count)
    angles = 2.0 * math.pi / seq_len * positions
    phases = angles[:, None] * bands[None, :]
    embedded = jnp.concatenate([timeline[:, None], jnp.cos(phases), -jnp.sin(phases)], axis=1)
    hidden = jnp.sin(jnp.dot(embedded, filter_in, precision=highest) + in_bias)
    hidden = jnp.sin(jnp.dot(hidden, filter_mid, precision=highest) + mid_bias)
    raw_taps = jnp.dot(hidden, filter_out, precision=highest)
    return raw_taps * jnp.exp(-timeline[:, None] * rates[None, :])


def spectral_matrix(length):
    steps = 2 * np.arange(length) + 1
    angle = (steps[:, None] * steps[None, :]) % (8 * length) * (math.pi / (4 * length))
    return np.concatenate([np.cos(angle), -np.sin(angle)]).astype(np.float32)


def nt_dot(left, right):
    return lax.dot_general(left, right, (((1,), (1,)), ((), ())), preferred_element_type=f32)


def tn_dot(left, right):
    return lax.dot_general(left, right, (((0,), (0,)), ((), ())), preferred_element_type=f32)


def nn_dot(left, right):
    return jnp.dot(left, right, preferred_element_type=f32)


def on_device(
    block_input,
    cotangent,
    lengths,
    in_proj,
    out_proj,
    up_proj,
    down_proj,
    first_gain,
    second_gain,
    short_filter,
    skip_bias,
    filter_in,
    filter_in_bias,
    filter_mid,
    filter_mid_bias,
    filter_out,
):
    seq_size = lax.axis_size("seq")
    fold = seq_size // CUBE
    member = lax.axis_index("seq") // fold
    core, plane = member % 2, member // 2
    ring_place = lax.axis_index("pos")
    rows, width = block_input.shape
    channels = width // RING
    span = width // 4
    lane = width // CUBE
    hidden = up_proj.shape[1]
    seq_len = LSEQ
    bundles = [list(range(i * fold, (i + 1) * fold)) for i in range(CUBE)]

    def hop(value, bit):
        pairs = [(i, ((i // fold) ^ bit) * fold + i % fold) for i in range(seq_size)]
        return lax.ppermute(value, "seq", pairs)

    def ring(value, shift):
        return lax.ppermute(value, "pos", [(i, (i + shift) % RING) for i in range(RING)])

    def in_order(mine, other, axis):
        return jnp.where(
            core == 0,
            jnp.concatenate([mine, other], axis),
            jnp.concatenate([other, mine], axis),
        )

    def plane_order(value):
        pieces = [
            lax.dynamic_slice_in_dim(value, (plane ^ r) * span, span, value.ndim - 1)
            for r in range(4)
        ]
        return jnp.concatenate(pieces, -1)

    def plane_gather(block):
        half = block.shape[0] // 2
        across = hop(block, 2)
        along = hop(block, 4)
        top = hop(along[:half], 2)
        low = hop(across[half:], 4)
        return jnp.concatenate([block, across, along, jnp.concatenate([top, low], 0)], 1)

    def plane_scatter(value):
        half = value.shape[0] // 2
        parts = [value[:, r * span : (r + 1) * span] for r in range(4)]
        top = hop(parts[3][:half].astype(bf16), 2)
        low = hop(parts[3][half:].astype(bf16), 4)
        across = jnp.concatenate([parts[1][:half], parts[1][half:] + low.astype(f32)], 0)
        along = jnp.concatenate([parts[2][:half] + top.astype(f32), parts[2][half:]], 0)
        across = hop(across.astype(bf16), 2)
        along = hop(along.astype(bf16), 4)
        return parts[0] + across.astype(f32) + along.astype(f32)

    def ring_gather(value):
        slots = [value]
        for _ in range(RING - 1):
            slots.append(ring(slots[-1], -1))
        return slots

    def ring_scatter(slots):
        total = slots[RING - 1]
        for j in range(RING - 2, -1, -1):
            total = slots[j] + ring(total.astype(bf16), 1).astype(f32)
        return total

    def to_sequence(slots):
        twice = jnp.concatenate(slots + slots, 0)
        return lax.dynamic_slice_in_dim(twice, (RING - ring_place) % RING * rows, RING * rows, 0)

    def to_slots(value):
        twice = jnp.concatenate([value, value], 0)
        return lax.dynamic_slice_in_dim(twice, ring_place * rows, RING * rows, 0)

    def unpair(total):
        sides = total.reshape(total.shape[0], 2, lane)
        kept = lax.dynamic_index_in_dim(sides, core, 1, False)
        given = hop(lax.dynamic_index_in_dim(sides, 1 - core, 1, False), 1)
        return jnp.where(core == 0, jnp.stack([kept, given]), jnp.stack([given, kept]))

    def settle(value, axis):
        if fold == 1:
            return value
        return lax.psum_scatter(
            value, "seq", scatter_dimension=axis, axis_index_groups=bundles, tiled=True
        )

    def widen(value):
        if fold == 1:
            return value
        return lax.all_gather(value, "seq", axis=1, axis_index_groups=bundles, tiled=True)

    in_rows = widen(in_proj.reshape(in_proj.shape[0], -1).T)
    up_rows = widen(up_proj.T)
    weights = [in_rows, widen(out_proj), up_rows, widen(down_proj)]
    sizes = [w.shape[0] // 2 for w in weights]
    stacked = jnp.concatenate([w[h * n : (h + 1) * n] for h in range(2) for w, n in zip(weights, sizes)])
    stacked = stacked.reshape(2, sum(sizes), lane)
    mine = lax.dynamic_index_in_dim(stacked, core, 0, False)
    other = hop(lax.dynamic_index_in_dim(stacked, 1 - core, 0, False), 1)
    paired = in_order(mine, other, 1)
    in_half, out_half, forward_half = jnp.split(paired, [sizes[0], sizes[0] + sizes[1]])

    inputs = plane_order(block_input).astype(f32)
    cot = plane_order(cotangent)
    gain_one = plane_order(first_gain)
    gain_two = plane_order(second_gain)
    unit_one = row_scale(inputs)
    normed = (unit_one * gain_one).astype(bf16)
    normed_slots = ring_gather(normed)
    normed_full = jnp.concatenate(normed_slots, 0)

    in_part = plane_gather(in_half)
    in_full = in_order(in_part, hop(in_part, 1), 0)

    channel_start = ring_place * channels
    positions = jnp.arange(seq_len, dtype=jnp.int32).astype(f32)
    channel_ids = (channel_start + jnp.arange(channels, dtype=jnp.int32)).astype(f32)
    slowest = math.log(0.01) / 1.5
    fastest = math.log(0.01) / 0.3
    rates = jnp.abs(slowest + (fastest - slowest) * channel_ids / (width - 1))
    last_layer = lax.dynamic_slice_in_dim(filter_out, channel_start, channels, 1)
    taps, filter_back = jax.vjp(
        lambda *layers: filter_values(positions, seq_len, rates, *layers),
        filter_in,
        filter_in_bias,
        filter_mid,
        filter_mid_bias,
        last_layer,
    )
    matrix = jnp.asarray(spectral_matrix(seq_len))
    turn = (2.0 * np.arange(seq_len) + 1.0) * (math.pi / (4 * seq_len))
    turn_cos = jnp.asarray(np.cos(turn).astype(np.float32))[:, None]
    turn_sin = jnp.asarray(np.sin(turn).astype(np.float32))[:, None]

    def transform(value):
        both = jnp.dot(matrix, value, precision=high)
        return both[:seq_len], both[seq_len:]

    def restore(real, imag):
        both = jnp.concatenate([real, imag], 0)
        total = lax.dot_general(matrix, both, (((0,), (0,)), ((), ())), precision=high)
        return total * (1.0 / seq_len)

    raw_real, raw_imag = transform(taps)
    taps_real = raw_real * turn_cos - raw_imag * turn_sin
    taps_imag = raw_real * turn_sin + raw_imag * turn_cos

    projected = to_sequence([nt_dot(slot, in_full).astype(bf16) for slot in normed_slots])
    streams = projected.astype(f32)
    short_local = lax.dynamic_slice_in_dim(
        short_filter.reshape(3, 3, width), channel_start, channels, 2
    ).reshape(3, 3 * channels)
    skip_local = lax.dynamic_slice_in_dim(skip_bias, channel_start, channels, 0)
    valid = (jnp.arange(seq_len, dtype=jnp.int32) < lengths[0]).astype(f32)[:, None]

    def delayed(value, steps):
        return jnp.pad(value, ((steps, 0), (0, 0)))[:seq_len]

    def advanced(value, steps):
        return jnp.pad(value, ((0, steps), (0, 0)))[steps:]

    mixed = (
        short_local[0] * streams
        + short_local[1] * delayed(streams, 1)
        + short_local[2] * delayed(streams, 2)
    )
    gate_outer = mixed[:, :channels]
    gate_inner = mixed[:, channels : 2 * channels]
    stream_values = mixed[:, 2 * channels :]
    driven = stream_values * gate_inner * valid
    driven_real, driven_imag = transform(driven)
    long_conv = skip_local * driven + restore(
        driven_real * taps_real - driven_imag * taps_imag,
        driven_real * taps_imag + driven_imag * taps_real,
    )
    gated = (long_conv * gate_outer).astype(bf16)

    gated_out = to_slots(gated)
    gated_slots = [gated_out[:rows]] + [None] * (RING - 1)
    for j in range(1, RING):
        gated_slots[RING - j] = ring(gated_out[j * rows : (j + 1) * rows], j)
    gated_rows = jnp.concatenate(gated_slots, 1)

    out_part = plane_gather(jnp.concatenate(ring_gather(out_half), 0))
    out_part = out_part.reshape(RING, channels // 2, width)
    out_full = in_order(out_part, hop(out_part, 1), 1).reshape(width, width)
    residual = inputs + nn_dot(gated_rows, out_full)
    unit_two = row_scale(residual)
    second = (unit_two * gain_two).astype(bf16)

    second_pair = jnp.concatenate([second, hop(second, 1)], 0)
    cot_pair = jnp.concatenate([cot, hop(cot, 1)], 0)
    forward_slots = ring_gather(forward_half)
    units = hidden // 2
    out_sum = 0.0
    back_sum = 0.0
    grad_slots = []
    for slot in forward_slots:
        layer = plane_gather(slot)
        up_part, down_part = layer[:units], layer[units:]
        pre_act = nt_dot(second_pair, up_part)
        activated, gelu_back = jax.vjp(exact_gelu, pre_act)
        activated = activated.astype(bf16)
        grad_pre = gelu_back(nt_dot(cot_pair, down_part))[0].astype(bf16)
        out_sum = out_sum + nn_dot(activated, down_part)
        back_sum = back_sum + nn_dot(grad_pre, up_part)
        grad_layer = jnp.concatenate([tn_dot(grad_pre, second_pair), tn_dot(activated, cot_pair)], 0)
        grad_slots.append(plane_scatter(grad_layer))
    out_sum = out_sum[:rows] + hop(out_sum[rows:].astype(bf16), 1).astype(f32)
    back_sum = back_sum[:rows] + hop(back_sum[rows:].astype(bf16), 1).astype(f32)
    block_output = plane_order(residual + out_sum).astype(bf16)
    forward_grad = unpair(ring_scatter(grad_slots)).reshape(2, 2, units, lane)
    up_grad = forward_grad[:, 0].reshape(hidden, lane).T
    down_grad = forward_grad[:, 1].reshape(hidden, lane)

    def scale_back(values, unit, gain_vector, grad):
        weighted = grad * gain_vector
        centred = values - jnp.mean(values, axis=-1, keepdims=True)
        scaling = lax.rsqrt(jnp.mean(centred * centred, axis=-1, keepdims=True) + epsilon)
        return scaling * (
            weighted
            - jnp.mean(weighted, axis=-1, keepdims=True)
            - unit * jnp.mean(weighted * unit, axis=-1, keepdims=True)
        )

    second_gain_grad = jnp.sum(back_sum * unit_two, axis=0)
    grad_res = cot.astype(f32) + scale_back(residual, unit_two, gain_two, back_sum)
    branch = grad_res.astype(bf16)

    out_grad = tn_dot(gated_rows, branch).reshape(RING, 2, channels // 2, width)
    out_kept = lax.dynamic_index_in_dim(out_grad, core, 1, False)
    out_given = hop(lax.dynamic_index_in_dim(out_grad, 1 - core, 1, False).astype(bf16), 1)
    out_grad = plane_scatter((out_kept + out_given.astype(f32)).reshape(width // 2, width))
    out_grad = ring_scatter(list(out_grad.reshape(RING, channels // 2, span)))
    out_grad = unpair(out_grad).reshape(channels, lane)

    grad_rows = nt_dot(branch, out_full).astype(bf16)
    grad_slots = [grad_rows[:, :channels]] + [None] * (RING - 1)
    for j in range(1, RING):
        grad_slots[RING - j] = ring(grad_rows[:, j * channels : (j + 1) * channels], j)
    grad_gated = to_sequence(grad_slots).astype(f32)
    grad_conv = grad_gated * gate_outer
    grad_outer = grad_gated * long_conv
    conv_real, conv_imag = transform(grad_conv)
    grad_driven = skip_local * grad_conv + restore(
        conv_real * taps_real + conv_imag * taps_imag,
        conv_imag * taps_real - conv_real * taps_imag,
    )
    skip_grad = jnp.sum(grad_conv * driven, axis=0)
    cross_real = conv_real * driven_real + conv_imag * driven_imag
    cross_imag = conv_imag * driven_real - conv_real * driven_imag
    grad_taps = restore(
        cross_real * turn_cos + cross_imag * turn_sin,
        cross_imag * turn_cos - cross_real * turn_sin,
    )
    grad_product = grad_driven * valid
    grad_mixed = jnp.concatenate(
        [grad_outer, grad_product * stream_values, grad_product * gate_inner], 1
    )
    short_grad = jnp.stack(
        [jnp.sum(grad_mixed * delayed(streams, k), axis=0) for k in range(3)]
    )
    grad_streams = (
        short_local[0] * grad_mixed
        + short_local[1] * advanced(grad_mixed, 1)
        + short_local[2] * advanced(grad_mixed, 2)
    )
    grad_projected = to_slots(grad_streams.astype(bf16))
    grad_partial = nn_dot(grad_projected, in_full)
    first_gain_grad = jnp.sum(grad_partial * normed_full.astype(f32), axis=0) / gain_one
    grad_normed = ring_scatter([grad_partial[j * rows : (j + 1) * rows] for j in range(RING)])
    in_grad = tn_dot(grad_projected, normed_full).reshape(2, -1, width)
    in_kept = lax.dynamic_index_in_dim(in_grad, core, 0, False)
    in_given = hop(lax.dynamic_index_in_dim(in_grad, 1 - core, 0, False).astype(bf16), 1)
    in_grad = unpair(plane_scatter(in_kept + in_given.astype(f32)))
    in_grad = in_grad.reshape(3 * channels, lane).T
    grad_inputs = scale_back(inputs, unit_one, gain_one, grad_normed)
    input_grad = plane_order(grad_res + grad_inputs).astype(bf16)

    filter_grads = filter_back(grad_taps)
    shared = [plane_order(first_gain_grad), plane_order(second_gain_grad), *filter_grads[:4]]
    owned = [short_grad, skip_grad, filter_grads[4]]
    pack = [jnp.pad(v.reshape(-1), (0, -v.size % lane)).reshape(-1, lane) for v in shared + owned]
    counts = [v.shape[0] for v in pack]
    small = jnp.concatenate(pack, 0)
    if fold > 1:
        small = lax.psum(small, "seq", axis_index_groups=bundles)
    for bit in (1, 2, 4):
        small = small + hop(small, bit)
    slots = [small] + [ring(small, -j) for j in range(1, RING)]
    shared_rows = sum(counts[: len(shared)])
    kept = jnp.stack(slots + slots)
    kept = lax.dynamic_slice_in_dim(kept, (RING - ring_place) % RING, RING, 0)
    total = (kept[0, :shared_rows] + kept[1, :shared_rows]) + (kept[2, :shared_rows] + kept[3, :shared_rows])
    kept = kept[:, shared_rows:]
    results = []
    start = 0
    for value, count in zip(shared, counts):
        results.append(total[start : start + count].reshape(-1)[: value.size].reshape(value.shape))
        start += count
    start = 0
    for value, count in zip(owned, counts[len(shared) :]):
        piece = kept[:, start : start + count].reshape((RING,) + value.shape)
        results.append(jnp.moveaxis(piece, 0, -2).reshape(value.shape[:-1] + (-1,)))
        start += count
    short_total = jnp.moveaxis(results[6].reshape(3, RING, 3, channels), 1, 2)
    return (
        block_output,
        input_grad,
        settle(in_grad, 0).reshape(in_proj.shape),
        settle(out_grad, 1),
        settle(up_grad, 0),
        settle(down_grad, 1),
        results[0],
        results[1],
        short_total.reshape(3, 3 * width),
        results[7],
        results[2],
        results[3],
        results[4],
        results[5],
        results[8],
    )


def solution(mesh):
    rows = P(("seq", "pos"), None)
    in_place, down_place, up_place = P("seq", None, "pos"), P("pos", "seq"), P("seq", "pos")
    return jax.shard_map(
        on_device,
        mesh=mesh,
        in_specs=(rows, rows, P("seq"), in_place, down_place, up_place, down_place) + (P(),) * 9,
        out_specs=(rows, rows, in_place, down_place, up_place, down_place) + (P(),) * 9,
        check_vma=False,
    )
```

```python
import functools
import math

import jax
import jax.numpy as jnp
import ml_dtypes
import numpy as np
from jax import lax
from jax.experimental import pallas as pl
from jax.experimental.pallas import tpu as pltpu
from jax.sharding import PartitionSpec as P

EMB = 33
LSEQ = 1024
RING = 4
CUBE = 8
PLANE = 4
SCALE = 1.0

epsilon = 1e-05
highest = lax.Precision.HIGHEST
f32 = jnp.float32
bf16 = jnp.bfloat16

OWNED = 80
GAINS = 8
SHARED = 64
PACKED = OWNED + GAINS + SHARED


def nt_dot(left, right):
    return lax.dot_general(left, right, (((1,), (1,)), ((), ())), preferred_element_type=f32)


def tn_dot(left, right):
    return lax.dot_general(left, right, (((0,), (0,)), ((), ())), preferred_element_type=f32)


def nn_dot(left, right):
    return jnp.dot(left, right, preferred_element_type=f32)


def full_dot(left, right, dims=((1,), (0,))):
    return lax.dot_general(left, right, (dims, ((), ())), precision=highest, preferred_element_type=f32)


def embedding(seq_len):
    positions = np.concatenate([np.arange(0, seq_len, 2), np.arange(1, seq_len, 2)])
    timeline = positions / (seq_len - 1)
    band_count = (EMB - 1) // 2
    bands = np.linspace(0.0001, band_count - 1, band_count)
    phases = (2.0 * math.pi / seq_len * positions)[:, None] * bands[None, :]
    features = np.concatenate([timeline[:, None], np.cos(phases), -np.sin(phases)], 1)
    return features.astype(np.float32), timeline.astype(np.float32)[:, None]


def spectral_tables(length):
    half = length // 2
    freq = 2 * np.arange(half) + 1
    tables = []
    for offset in (1, 3):
        angle = (freq[:, None] * (4 * np.arange(half) + offset)[None, :]) % (8 * length)
        angle = angle * (math.pi / (4 * length))
        tables.append(np.concatenate([np.cos(angle), np.sin(angle)]))
    tables += [tables[0].T / length, tables[1].T / length]
    split = []
    for table in tables:
        top = table.astype(ml_dtypes.bfloat16)
        split += [top, (table - top.astype(np.float64)).astype(ml_dtypes.bfloat16)]
    order = np.concatenate([np.arange(half), length - 1 - np.arange(half)])
    turn = (2.0 * order + 1.0) * (math.pi / (4 * length))
    turns = np.stack([np.cos(turn), np.sin(turn)]).astype(np.float32)[:, :, None]
    return split, turns


def split_dot(table_top, table_low, value):
    top = value.astype(bf16)
    low = (value - top.astype(f32)).astype(bf16)
    return nn_dot(table_top, top) + nn_dot(table_top, low) + nn_dot(table_low, top)


def transform(tables, even, odd):
    half = even.shape[0]
    even_sums = split_dot(tables[0][...], tables[1][...], even)
    odd_sums = split_dot(tables[2][...], tables[3][...], odd)
    even_cos, even_sin = even_sums[:half], even_sums[half:]
    odd_cos, odd_sin = odd_sums[:half], odd_sums[half:]
    real = jnp.concatenate([even_cos + odd_cos, even_sin - odd_sin], 0)
    imag = jnp.concatenate([-(even_sin + odd_sin), odd_cos - even_cos], 0)
    return real, imag


def restore(tables, real, imag):
    half = real.shape[0] // 2
    real_low, real_up, imag_low, imag_up = real[:half], real[half:], imag[:half], imag[half:]
    even = jnp.concatenate([real_low - imag_up, real_up - imag_low], 0)
    odd = jnp.concatenate([real_low + imag_up, -(real_up + imag_low)], 0)
    return (
        split_dot(tables[4][...], tables[5][...], even),
        split_dot(tables[6][...], tables[7][...], odd),
    )


def later(value):
    row = lax.broadcasted_iota(jnp.int32, value.shape, 0)
    return jnp.where(row == 0, 0.0, pltpu.roll(value, 1, 0))


def sooner(value):
    row = lax.broadcasted_iota(jnp.int32, value.shape, 0)
    last = value.shape[0] - 1
    return jnp.where(row == last, 0.0, pltpu.roll(value, last, 0))


def mix_streams(even, odd, lags):
    mixed_even = lags[0] * even + lags[1] * later(odd) + lags[2] * later(even)
    mixed_odd = lags[0] * odd + lags[1] * even + lags[2] * later(odd)
    return mixed_even, mixed_odd


def valid_rows(length, half, offset):
    place = 2 * lax.broadcasted_iota(jnp.int32, (half, 1), 0) + offset
    return jnp.where(place < length, 1.0, 0.0)


def row_order(rows, dtype):
    left = lax.broadcasted_iota(jnp.int32, (rows, rows), 0)
    right = lax.broadcasted_iota(jnp.int32, (rows, rows), 1)
    half = rows // 2
    source = jnp.where(left < half, 2 * left, 2 * (left - half) + 1)
    return jnp.where(right == source, 1.0, 0.0).astype(dtype)


def standardize(values):
    centred = values - jnp.mean(values, axis=-1, keepdims=True)
    scaling = lax.rsqrt(jnp.mean(centred * centred, axis=-1, keepdims=True) + epsilon)
    return centred * scaling, scaling


def scale_back(unit, scaling, weighted):
    return scaling * (
        weighted
        - jnp.mean(weighted, axis=-1, keepdims=True)
        - unit * jnp.mean(weighted * unit, axis=-1, keepdims=True)
    )


def piece(place, size):
    return pl.ds(pl.multiple_of(place * size, size), size)


def rows_kernel(rows_in, cot_in, gains, normed, inputs, cot):
    order = row_order(rows_in.shape[0], bf16)
    inputs[...] = nn_dot(order, rows_in[...]).astype(bf16)
    cot[...] = nn_dot(order, cot_in[...]).astype(bf16)
    unit, _ = standardize(inputs[...].astype(f32))
    normed[...] = (unit * gains[...]).astype(bf16)


def weights_kernel(in_w, up_w, down_w, in_rows, layer_rows):
    streams, channels = in_w.shape[0], in_w.shape[2]
    for k in range(streams):
        in_rows[pl.ds(k * channels, channels), :] = in_w[k].T
    turned = up_w[...].T
    part = turned.shape[0] // CUBE
    for m in range(CUBE):
        layer_rows[pl.ds(2 * m * part, part), :] = turned[m * part : (m + 1) * part]
        layer_rows[pl.ds((2 * m + 1) * part, part), :] = down_w[pl.ds(m * part, part), :]


def side_by_side(ref, out):
    count, lane = ref.shape[0] // CUBE, ref.shape[1]
    for m in range(CUBE):
        out[:, pl.ds(m * lane, lane)] = ref[pl.ds(m * count, count), :]


def decay_of(info, times, channels, width):
    lanes = lax.broadcasted_iota(jnp.int32, (1, channels), 1) + info[2] * channels
    slowest = math.log(0.01) / 1.5
    fastest = math.log(0.01) / 0.3
    rates = jnp.abs(slowest + (fastest - slowest) * lanes.astype(f32) / (width - 1))
    return jnp.exp(-times[...] * rates)


def pair_dot(left, right):
    half = left.shape[0] // 2
    return jnp.concatenate([full_dot(left[:half], right), full_dot(left[half:], right)], 1)


def unpair(value):
    lanes = value.shape[1] // 2
    return jnp.concatenate([value[:, :lanes], value[:, lanes:]], 0)


def hidden_kernel(features, first, bias_one, middle, bias_two, hidden):
    inner = middle.shape[0]
    twice = lambda ref: jnp.concatenate([ref[...], ref[...]], 1)
    angle = pair_dot(features[...], first[...]) + twice(bias_one)
    one = unpair(jnp.sin(angle))
    hidden[:, pl.ds(0, inner)] = one
    hidden[:, pl.ds(inner, inner)] = unpair(jnp.cos(angle))
    angle = pair_dot(one, middle[...]) + twice(bias_two)
    hidden[:, pl.ds(2 * inner, inner)] = unpair(jnp.sin(angle))
    hidden[:, pl.ds(3 * inner, inner)] = unpair(jnp.cos(angle))


def taps_kernel(info, width, hidden, times, last, turns, *refs):
    tables, (spectrum,) = refs[:8], refs[8:]
    half = hidden.shape[0] // 2
    inner = last.shape[0]
    taps = full_dot(hidden[:, pl.ds(2 * inner, inner)], last[...]) * decay_of(info, times, last.shape[1], width)
    real, imag = transform(tables, taps[:half], taps[half:])
    spectrum[0] = real * turns[0] - imag * turns[1]
    spectrum[1] = real * turns[1] + imag * turns[0]


def ring_blocks(info, count):
    return [piece((info[2] + j) & (RING - 1), count) for j in range(RING)]


def conv_kernel(info, *refs):
    slots, (in_all, lags, skip, spectrum), refs = refs[:4], refs[4:8], refs[8:]
    tables = refs[:8]
    projected, long_conv, driven_spectrum, gated, in_full = refs[8:]
    length = info[3]
    half_rows = slots[0].shape[0] // 2
    half = projected.shape[0] // 2
    channels = skip.shape[1]
    side_by_side(in_all, in_full)
    for j, slot in enumerate(slots):
        total = nt_dot(slot[...], in_full[...]).astype(bf16)
        block = (info[2] + j) & (RING - 1)
        projected[piece(block, half_rows), :] = total[:half_rows]
        projected[pl.ds(pl.multiple_of(half + block * half_rows, half_rows), half_rows), :] = total[half_rows:]
    streams = []
    for k in range(3):
        lanes = pl.ds(k * channels, channels)
        streams.append(
            mix_streams(
                projected[pl.ds(0, half), lanes].astype(f32),
                projected[pl.ds(half, half), lanes].astype(f32),
                [lags[pl.ds(i, 1), lanes] for i in range(3)],
            )
        )
    (outer_even, outer_odd), (inner_even, inner_odd), (value_even, value_odd) = streams
    even = value_even * inner_even * valid_rows(length, half, 0)
    odd = value_odd * inner_odd * valid_rows(length, half, 1)
    real, imag = transform(tables, even, odd)
    driven_spectrum[0] = real
    driven_spectrum[1] = imag
    taps_real, taps_imag = spectrum[0], spectrum[1]
    back_even, back_odd = restore(
        tables, real * taps_real - imag * taps_imag, real * taps_imag + imag * taps_real
    )
    back_even += skip[...] * even
    back_odd += skip[...] * odd
    long_conv[pl.ds(0, half), :] = back_even
    long_conv[pl.ds(half, half), :] = back_odd
    even, odd = (back_even * outer_even).astype(bf16), (back_odd * outer_odd).astype(bf16)
    for z in range(RING):
        here = slice(z * half_rows, (z + 1) * half_rows)
        gated[pl.ds(2 * z * half_rows, half_rows), :] = even[here]
        gated[pl.ds((2 * z + 1) * half_rows, half_rows), :] = odd[here]


def out_kernel(info, gated, out_all, inputs, gains, residual, second):
    rows, width = inputs.shape
    lane = out_all.shape[1]
    wide = jnp.concatenate([gated[block, :] for block in ring_blocks(info, rows)], 1)
    for m in range(CUBE):
        lanes = pl.ds(m * lane, lane)
        residual[:, lanes] = inputs[:, lanes].astype(f32) + nn_dot(wide, out_all[pl.ds(m * width, width), :])
    unit, _ = standardize(residual[...])
    second[...] = (unit * gains[...]).astype(bf16)


def layer_kernel(info, *refs):
    rows_in, (cot_all, *slots), refs = refs[:10], refs[10:15], refs[15:]
    out_kept, out_given, back_kept, back_given, grads, up_sum, down_sum = refs
    own, sib, across, across_sib, along, along_sib, top, low, top_sib, low_sib = rows_in
    rows = own.shape[0]
    part = slots[0].shape[0] // 2
    ups = jnp.concatenate([slot[pl.ds(0, part), :] for slot in slots], 0)
    downs = jnp.concatenate([slot[pl.ds(part, part), :] for slot in slots], 0)
    chips = ((own, sib), (across, across_sib), (along, along_sib), (top, low, top_sib, low_sib))
    for r, parts in enumerate(chips):
        second = jnp.concatenate([ref[...] for ref in parts], 0)
        cot = jnp.concatenate([cot_all[piece(info[1] ^ (2 * r + i), rows), :] for i in range(2)], 0)
        pre_act = nt_dot(second, ups)
        grad_act = nt_dot(cot, downs)
        lower = 0.5 * (1.0 + lax.erf(pre_act * math.sqrt(0.5)))
        density = jnp.exp(-0.5 * pre_act * pre_act) * (1.0 / math.sqrt(2.0 * math.pi))
        activated = (pre_act * lower).astype(bf16)
        grad_pre = (grad_act * (lower + pre_act * density)).astype(bf16)
        here = pl.ds(r * rows, rows)
        out = nn_dot(activated, downs)
        out_kept[here, :] = out[:rows].astype(bf16)
        out_given[here, :] = out[rows:].astype(bf16)
        back = nn_dot(grad_pre, ups)
        back_kept[here, :] = back[:rows].astype(bf16)
        back_given[here, :] = back[rows:].astype(bf16)
        up_grad = tn_dot(grad_pre, second)
        down_grad = tn_dot(activated, cot)
        up_sum[...] = up_grad if r == 0 else up_sum[...] + up_grad
        down_sum[...] = down_grad if r == 0 else down_sum[...] + down_grad
    for j, block in enumerate(ring_blocks(info, 2 * part)):
        here = pl.ds(j * part, part)
        both = jnp.concatenate([up_sum[here, :], down_sum[here, :]], 0)
        grads[block, :] = both.astype(bf16)


def share_kernel(kept, got, own, across, along, top, low):
    rows = own.shape[0]
    for r, ref in enumerate((own, across, along)):
        here = pl.ds(r * rows, rows)
        ref[...] = (kept[here, :].astype(f32) + got[here, :].astype(f32)).astype(bf16)
    for i, ref in enumerate((top, low)):
        here = pl.ds(3 * rows + i * rows // 2, rows // 2)
        ref[...] = (kept[here, :].astype(f32) + got[here, :].astype(f32)).astype(bf16)


def turn_kernel(across, along, top, low, across_sum, along_sum):
    half = top.shape[0]
    first, second = pl.ds(0, half), pl.ds(half, half)
    across_sum[first, :] = across[first, :]
    across_sum[second, :] = (across[second, :].astype(f32) + low[...].astype(f32)).astype(bf16)
    along_sum[first, :] = (along[first, :].astype(f32) + top[...].astype(f32)).astype(bf16)
    along_sum[second, :] = along[second, :]


def branch_kernel(
    info, own, across, along, residual, gains, cot, out_all, grad_res, branch, gain_grad, grad_gated
):
    rows, width = residual.shape
    lane = out_all.shape[1]
    channels = grad_gated.shape[1]
    back = own[...].astype(f32) + across[...].astype(f32) + along[...].astype(f32)
    unit, scaling = standardize(residual[...])
    gain_grad[...] = jnp.sum(back * unit, axis=0, keepdims=True)
    total = cot[...].astype(f32) + scale_back(unit, scaling, back * gains[...])
    grad_res[...] = total
    branch[...] = total.astype(bf16)
    total = None
    for m in range(CUBE):
        part = nt_dot(branch[:, pl.ds(m * lane, lane)], out_all[pl.ds(m * width, width), :])
        total = part if m == 0 else total + part
    total = total.astype(bf16)
    for j, block in enumerate(ring_blocks(info, rows)):
        grad_gated[block, :] = total[:, j * channels : (j + 1) * channels]


def finish_kernel(residual, own, across, along, block_output):
    total = own[...].astype(f32) + across[...].astype(f32) + along[...].astype(f32)
    total = (residual[...] + total).astype(bf16)
    block_output[...] = tn_dot(row_order(total.shape[0], bf16), total).astype(bf16)


def below(total, out):
    count, lane = total.shape[0], total.shape[1] // CUBE
    for m in range(CUBE):
        out[pl.ds(m * count, count), :] = total[:, m * lane : (m + 1) * lane].astype(out.dtype)


def below_kernel(total, out):
    below(total[...], out)


def out_grad_kernel(gated, branch, out_grad):
    rows = branch.shape[0]
    parts = [tn_dot(gated[pl.ds(z * rows, rows), :], branch[...]) for z in range(RING)]
    below(jnp.concatenate(parts, 0).astype(bf16), out_grad)


def back_kernel(
    info, grad_gated, projected, long_conv, driven_spectrum, lags, skip, spectrum, turns, *refs
):
    tables = refs[:8]
    grad_projected, grad_taps, small = refs[8:]
    length = info[3]
    channels = grad_gated.shape[1]
    half = projected.shape[0] // 2
    half_rows = half // RING
    plain, mixed = [], []
    for k in range(3):
        lanes = pl.ds(k * channels, channels)
        even = projected[pl.ds(0, half), lanes].astype(f32)
        odd = projected[pl.ds(half, half), lanes].astype(f32)
        plain.append((even, odd))
        mixed.append(mix_streams(even, odd, [lags[pl.ds(i, 1), lanes] for i in range(3)]))
    (outer_even, outer_odd), (inner_even, inner_odd), (value_even, value_odd) = mixed
    valid_even, valid_odd = valid_rows(length, half, 0), valid_rows(length, half, 1)
    gated_even, gated_odd = (
        jnp.concatenate([grad_gated[pl.ds((2 * z + i) * half_rows, half_rows), :] for z in range(RING)], 0).astype(f32)
        for i in range(2)
    )
    conv_even, conv_odd = gated_even * outer_even, gated_odd * outer_odd
    real, imag = transform(tables, conv_even, conv_odd)
    taps_real, taps_imag = spectrum[0], spectrum[1]
    driven_even, driven_odd = restore(
        tables, real * taps_real + imag * taps_imag, imag * taps_real - real * taps_imag
    )
    driven_even = (driven_even + skip[...] * conv_even) * valid_even
    driven_odd = (driven_odd + skip[...] * conv_odd) * valid_odd
    small[pl.ds(9, 1), :] = jnp.sum(
        conv_even * value_even * inner_even * valid_even + conv_odd * value_odd * inner_odd * valid_odd,
        axis=0,
        keepdims=True,
    )
    small[pl.ds(10, 6), :] = jnp.zeros((6, channels), f32)
    grads = (
        (gated_even * long_conv[pl.ds(0, half), :], gated_odd * long_conv[pl.ds(half, half), :]),
        (driven_even * value_even, driven_odd * value_odd),
        (driven_even * inner_even, driven_odd * inner_odd),
    )
    for k, (even, odd) in enumerate(grads):
        lanes = pl.ds(k * channels, channels)
        lag = [lags[pl.ds(i, 1), lanes] for i in range(3)]
        plain_even, plain_odd = plain[k]
        sums = (
            even * plain_even + odd * plain_odd,
            even * later(plain_odd) + odd * plain_even,
            even * later(plain_even) + odd * later(plain_odd),
        )
        for i in range(3):
            small[pl.ds(3 * i + k, 1), :] = jnp.sum(sums[i], axis=0, keepdims=True)
        next_even, next_odd = sooner(even), sooner(odd)
        stream_even = (lag[0] * even + lag[1] * odd + lag[2] * next_even).astype(bf16)
        stream_odd = (lag[0] * odd + lag[1] * next_even + lag[2] * next_odd).astype(bf16)
        for z in range(RING):
            here = slice(z * half_rows, (z + 1) * half_rows)
            grad_projected[pl.ds(2 * z * half_rows, half_rows), lanes] = stream_even[here]
            grad_projected[pl.ds((2 * z + 1) * half_rows, half_rows), lanes] = stream_odd[here]
    base_real, base_imag = driven_spectrum[0], driven_spectrum[1]
    cross_real = real * base_real + imag * base_imag
    cross_imag = imag * base_real - real * base_imag
    taps_even, taps_odd = restore(
        tables,
        cross_real * turns[0] + cross_imag * turns[1],
        cross_imag * turns[0] - cross_real * turns[1],
    )
    grad_taps[pl.ds(0, half), :] = taps_even
    grad_taps[pl.ds(half, half), :] = taps_odd


def normed_kernel(info, grad_projected, in_full, n0, n1, n2, n3, gains, partial, gain_grad):
    rows = n0.shape[0]
    total_gain = None
    for j, (slot, block) in enumerate(zip((n0, n1, n2, n3), ring_blocks(info, rows))):
        total = nn_dot(grad_projected[block, :], in_full[...])
        partial[block, :] = total.astype(bf16)
        part = jnp.sum(total * slot[...].astype(f32), axis=0, keepdims=True)
        total_gain = part if j == 0 else total_gain + part
    gain_grad[...] = total_gain / gains[...]


def in_grad_kernel(info, grad_projected, n0, n1, n2, n3, in_grad):
    normed = jnp.concatenate([n0[...], n1[...], n2[...], n3[...]], 0)
    grad = jnp.concatenate([grad_projected[block, :] for block in ring_blocks(info, n0.shape[0])], 0)
    below(tn_dot(grad, normed).astype(bf16), in_grad)


def end_kernel(grad_normed, inputs, gains, grad_res, input_grad):
    grad = grad_normed[...].astype(f32)
    unit, scaling = standardize(inputs[...].astype(f32))
    total = (grad_res[...] + scale_back(unit, scaling, grad * gains[...])).astype(bf16)
    input_grad[...] = tn_dot(row_order(total.shape[0], bf16), total).astype(bf16)


def layer_end_kernel(parts, up_grad, down_grad):
    part = parts.shape[0] // CUBE // 2
    for m in range(CUBE):
        here = pl.ds(m * part, part)
        up_grad[:, here] = parts[pl.ds(2 * m * part, part), :].astype(f32).T
        down_grad[here, :] = parts[pl.ds((2 * m + 1) * part, part), :].astype(f32)


def out_sum_kernel(info, parts, own, p1, p2, p3):
    rows = parts.shape[0] // CUBE
    count = own.shape[0]
    for j, ref in enumerate((own, p1, p2, p3)):
        place = ((info[2] + j) & (RING - 1)) * count
        total = None
        for m in range(CUBE):
            here = pl.ds(pl.multiple_of(m * rows + place, count), count)
            part = parts[here, :].astype(f32)
            total = part if m == 0 else total + part
        ref[...] = total.astype(ref.dtype)


def out_end_kernel(own, p1, p2, p3, total):
    total[...] = own[...] + p1[...].astype(f32) + p2[...].astype(f32) + p3[...].astype(f32)


def in_end_kernel(parts, in_grad):
    channels = in_grad.shape[2]
    rows = parts.shape[0] // CUBE
    for k in range(in_grad.shape[0]):
        total = None
        for m in range(CUBE):
            part = parts[pl.ds(m * rows + k * channels, channels), :].astype(f32)
            total = part if m == 0 else total + part
        in_grad[k] = total.T


def pack_kernel(
    info, width, grad_taps, hidden, features, times, middle, last, small, gain_one, gain_two, packed
):
    inner = middle.shape[0]
    span = packed.shape[1]
    one, slope_one, two, slope_two = (hidden[:, pl.ds(i * inner, inner)] for i in range(4))
    grad_raw = grad_taps[...] * decay_of(info, times, span, width)
    rows = ((0,), (0,))
    packed[pl.ds(0, inner), :] = full_dot(two, grad_raw, rows)
    grad_two = full_dot(grad_raw, last[...], ((1,), (1,))) * slope_two
    grad_one = full_dot(grad_two, middle[...], ((1,), (1,))) * slope_one
    packed[pl.ds(64, 16), :] = small[...]
    for r in range(PLANE):
        lanes = pl.ds(r * span, span)
        packed[pl.ds(OWNED + r, 1), :] = gain_one[:, lanes]
        packed[pl.ds(OWNED + PLANE + r, 1), :] = gain_two[:, lanes]
    start = OWNED + GAINS
    packed[pl.ds(start, SHARED), :] = jnp.zeros((SHARED, span), f32)
    packed[pl.ds(start, inner), pl.ds(0, inner)] = full_dot(one, grad_two, rows)
    packed[pl.ds(start, EMB), pl.ds(inner, inner)] = full_dot(features[...], grad_one, rows)
    packed[pl.ds(start, 1), pl.ds(2 * inner, inner)] = jnp.sum(grad_one, axis=0, keepdims=True)
    packed[pl.ds(start, 1), pl.ds(3 * inner, inner)] = jnp.sum(grad_two, axis=0, keepdims=True)


def unpack_kernel(
    info, s0, s1, s2, s3, gain_one, gain_two, short, skip, first, bias_one, middle, bias_two, last, slots
):
    place = info[2]
    for j, ref in enumerate((s0, s1, s2, s3)):
        slots[place ^ j] = ref[...]
    channels = s0.shape[1]
    inner = middle.shape[0]
    for z in range(RING):
        lanes = pl.ds(z * channels, channels)
        last[:, lanes] = slots[z, pl.ds(0, 64), :]
        for i in range(3):
            for k in range(3):
                here = pl.ds((k * RING + z) * channels, channels)
                short[pl.ds(i, 1), here] = slots[z, pl.ds(64 + 3 * i + k, 1), :]
        skip[:, lanes] = slots[z, pl.ds(64 + 9, 1), :]
    count = GAINS + SHARED
    total = slots[0, pl.ds(OWNED, count), :] + slots[1, pl.ds(OWNED, count), :]
    total += slots[2, pl.ds(OWNED, count), :] + slots[3, pl.ds(OWNED, count), :]
    for b in range(PLANE):
        lanes = pl.ds(b * channels, channels)
        gain_one[:, lanes] = total[b : b + 1]
        gain_two[:, lanes] = total[PLANE + b : PLANE + b + 1]
    total = total[GAINS:]
    middle[...] = total[:, :inner]
    first[...] = total[:EMB, inner : 2 * inner]
    bias_one[...] = total[:1, 2 * inner : 3 * inner]
    bias_two[...] = total[:1, 3 * inner :]


def tick_kernel(count, *refs):
    refs[count][...] = jnp.zeros_like(refs[count])


def run(kernel, outs, *args, scratch=(), name, micros=2.0, limit=56, after=()):
    place = lambda a: pltpu.SMEM if a.dtype == jnp.int32 else pltpu.VMEM
    shapes = [jax.ShapeDtypeStruct(*o) for o in outs]
    count = len(args)

    def body(*refs):
        kernel(*refs[:count], *refs[count + len(after) :])

    return pl.pallas_call(
        body,
        out_shape=shapes,
        in_specs=[pl.BlockSpec(memory_space=place(a)) for a in args]
        + [pl.BlockSpec(memory_space=pl.ANY) for _ in after],
        out_specs=[pl.BlockSpec(memory_space=pltpu.VMEM)] * len(shapes),
        scratch_shapes=[pltpu.VMEM(*s) for s in scratch],
        compiler_params=pltpu.CompilerParams(vmem_limit_bytes=limit * 2**20),
        cost_estimate=pl.CostEstimate(
            flops=int(SCALE * micros * 1e9), bytes_accessed=int(SCALE * micros * 3e6), transcendentals=0
        ),
        name=name,
    )(*args, *after)


def on_device(
    block_input,
    cotangent,
    lengths,
    in_proj,
    out_proj,
    up_proj,
    down_proj,
    first_gain,
    second_gain,
    short_filter,
    skip_bias,
    filter_in,
    filter_in_bias,
    filter_mid,
    filter_mid_bias,
    filter_out,
):
    seq_size = lax.axis_size("seq")
    fold = seq_size // CUBE
    member = lax.axis_index("seq") // fold
    ring_place = lax.axis_index("pos")
    rows, width = block_input.shape
    channels = width // RING
    lane = width // CUBE
    hidden = up_proj.shape[1]
    seq_len = LSEQ
    members = [[i * fold + o for i in range(CUBE)] for o in range(fold)]
    bundles = [list(range(i * fold, (i + 1) * fold)) for i in range(CUBE)]

    def hop(value, bit):
        pairs = [(i, ((i // fold) ^ bit) * fold + i % fold) for i in range(seq_size)]
        return lax.ppermute(value, "seq", pairs)

    def ring(value, shift):
        return lax.ppermute(value, "pos", [(i, (i + shift) % RING) for i in range(RING)])

    def near_ring(value, bit):
        return lax.ppermute(value, "pos", [(i, i ^ bit) for i in range(RING)])

    def to_rows(value):
        return lax.all_to_all(value, "pos", 0, 0, tiled=True)

    def swap(value):
        return lax.all_to_all(value, "seq", 0, 0, axis_index_groups=members, tiled=True)

    def gather(value):
        return lax.all_gather(value, "seq", axis=0, axis_index_groups=members, tiled=True)

    def scatter(value):
        return lax.psum_scatter(value, "seq", scatter_dimension=0, axis_index_groups=members, tiled=True)

    def settle(value, axis):
        if fold == 1:
            return value
        return lax.psum_scatter(
            value, "seq", scatter_dimension=axis, axis_index_groups=bundles, tiled=True
        )

    def widen(value, axis):
        if fold == 1:
            return value
        return lax.all_gather(value, "seq", axis=axis, axis_index_groups=bundles, tiled=True)

    info = jnp.stack([member % 2, member, ring_place, lengths[0]]).astype(jnp.int32)
    waiting = []
    latest = []

    def now(*values):
        waiting.extend(values)
        return values

    def step(kernel, outs, *args, **options):
        after = [v for v in latest + waiting if not any(v is a for a in args)]
        results = run(kernel, outs, *args, after=after, **options)
        waiting.clear()
        latest[:] = results[:1]
        return results

    def phase(*values, after=()):
        after = [v for v in latest + waiting + list(after) if not any(v is a for a in values)]
        waiting.clear()
        count = len(values) + len(after)
        mark, *passed = pl.pallas_call(
            functools.partial(tick_kernel, count),
            out_shape=[jax.ShapeDtypeStruct((8, 128), f32)]
            + [jax.ShapeDtypeStruct(v.shape, v.dtype) for v in values],
            in_specs=[pl.BlockSpec(memory_space=pl.ANY)] * count,
            out_specs=[pl.BlockSpec(memory_space=pltpu.VMEM)]
            + [pl.BlockSpec(memory_space=pl.ANY)] * len(values),
            input_output_aliases={i: i + 1 for i in range(len(values))},
            name="phase",
        )(*values, *after)
        latest[:] = [mark]
        return passed

    gain_one, gain_two = first_gain.reshape(1, width), second_gain.reshape(1, width)
    in_turned = widen(in_proj.transpose(1, 0, 2), 1)
    out_shard, up_shard, down_shard = widen(out_proj, 1), widen(up_proj, 0), widen(down_proj, 1)
    normed, inputs, cot = step(
        rows_kernel, [((rows, width), bf16)] * 3, block_input, cotangent, gain_one, name="rows", micros=0.2
    )
    normed_slots = [normed, ring(normed, -1)]
    in_rows, layer_rows = step(
        weights_kernel,
        [((3 * channels, lane), bf16), ((2 * hidden, lane), bf16)],
        in_turned, up_shard, down_shard,
        name="weights", micros=0.2,
    )
    in_all = gather(in_rows)
    layer_got = swap(layer_rows)

    channel_start = ring_place * channels
    features, times = (jnp.asarray(v) for v in embedding(seq_len))
    last_layer = lax.dynamic_slice_in_dim(filter_out, channel_start, channels, 1)
    tables, turns = spectral_tables(seq_len)
    tables = [jnp.asarray(t) for t in tables]
    turns = jnp.asarray(turns)
    lags = lax.dynamic_slice_in_dim(
        short_filter.reshape(3, 3, width), channel_start, channels, 2
    ).reshape(3, 3 * channels)
    skip = lax.dynamic_slice_in_dim(skip_bias, channel_start, channels, 0)[None]
    pair = ((2, seq_len, channels), f32)
    inner = filter_mid.shape[0]

    def with_width(kernel):
        return lambda info, *refs: kernel(info, width, *refs)

    (filter_hidden,) = step(
        hidden_kernel,
        [((seq_len, 4 * inner), f32)],
        features, filter_in, filter_in_bias[None], filter_mid, filter_mid_bias[None],
        name="hidden", micros=5,
    )
    normed_slots[1], out_shard = phase(normed_slots[1], out_shard)
    normed_slots.append(ring(normed_slots[1], -1))
    out_shards = [out_shard] + [ring(out_shard, -j) for j in range(1, RING)]
    (layer_own,) = step(
        side_by_side, [((2 * hidden // CUBE, width), bf16)], layer_got, name="layer_own", micros=0.2
    )
    (spectrum,) = step(
        with_width(taps_kernel),
        [pair],
        info, filter_hidden, times, last_layer, turns, *tables,
        name="taps", micros=5,
    )
    normed_slots[2], out_shards[0], *out_shards[1:] = phase(normed_slots[2], *out_shards)
    normed_slots.append(ring(normed_slots[2], -1))
    cot_all = gather(cot)
    layer_own, *out_shards = phase(layer_own, *out_shards, after=[normed_slots[3]])
    layer_slots = [layer_own, ring(layer_own, -1)]
    out_all = gather(jnp.concatenate(out_shards, 0))

    projected, long_conv, driven_spectrum, gated, in_full = step(
        conv_kernel,
        [
            ((seq_len, 3 * channels), bf16),
            ((seq_len, channels), f32),
            pair,
            ((seq_len, channels), bf16),
            ((3 * channels, width), bf16),
        ],
        info, *normed_slots, in_all, lags, skip, spectrum, *tables,
        name="conv", micros=14,
    )
    gated, layer_slots[1] = phase(gated, layer_slots[1], after=[cot_all])
    gated = to_rows(gated)
    layer_slots[:2] = phase(*layer_slots[:2], after=[gated, out_all])
    layer_slots += [ring(layer_slots[1], -1), ring(layer_slots[0], 1)]
    residual, second = step(
        out_kernel,
        [((rows, width), f32), ((rows, width), bf16)],
        info, gated, out_all, inputs, gain_two,
        name="out", micros=0.2,
    )

    second_sib, across, along = (hop(second, bit) for bit in (1, 2, 4))
    half = rows // 2
    top, low = hop(along[:half], 2), hop(across[half:], 4)
    across_sib, along_sib, top_sib, low_sib = (hop(v, 1) for v in (across, along, top, low))
    wide = CUBE * rows // 2
    out_kept, out_given, back_kept, back_given, layer_grads = step(
        layer_kernel,
        [((wide, width), bf16)] * 4 + [((hidden, width), bf16)],
        info, second, second_sib, across, across_sib, along, along_sib, top, low, top_sib, low_sib,
        cot_all, *layer_slots,
        scratch=[((hidden // 2, width), f32)] * 2,
        name="layer", micros=22,
    )
    back_given, out_given, layer_grads = phase(back_given, out_given, layer_grads)
    layer_grads = lax.psum_scatter(layer_grads, "pos", scatter_dimension=0, tiled=True)

    block, part = ((rows, width), bf16), ((half, width), bf16)
    turned = []
    shares = [
        step(share_kernel, [block] * 3 + [part] * 2, kept, hop(given, 1), name="share", micros=0.1)
        for kept, given in ((back_kept, back_given), (out_kept, out_given))
    ]
    for own, across, along, top, low in shares:
        across, along = step(
            turn_kernel, [block] * 2, across, along, hop(top, 2), hop(low, 4), name="turn", micros=0.1
        )
        turned.append([own, hop(across, 2), hop(along, 4)])
    back_parts, out_parts = turned
    grad_res, branch, second_gain_grad, grad_gated = step(
        branch_kernel,
        [((rows, width), f32), ((rows, width), bf16), ((1, width), f32), ((seq_len, channels), bf16)],
        info, *back_parts, residual, gain_two, cot, out_all,
        name="branch", micros=0.2,
    )
    (grad_gated,) = phase(grad_gated, after=[layer_grads])
    grad_gated = to_rows(grad_gated)
    (out_grad,) = step(
        out_grad_kernel, [((CUBE * width, lane), bf16)], gated, branch, name="out_grad", micros=0.1
    )
    (layer_sums,) = step(below_kernel, [((2 * hidden, lane), bf16)], layer_grads, name="layer_sum", micros=0.1)
    (out_grad,) = phase(out_grad, after=[grad_gated])
    out_grad = swap(out_grad)

    grad_projected, grad_taps, small = step(
        back_kernel,
        [((seq_len, 3 * channels), bf16), ((seq_len, channels), f32), ((16, channels), f32)],
        info, grad_gated, projected, long_conv, driven_spectrum, lags, skip, spectrum, turns, *tables,
        name="back", micros=15,
    )
    partial, first_gain_grad = step(
        normed_kernel,
        [((seq_len, width), bf16), ((1, width), f32)],
        info, grad_projected, in_full, *normed_slots, gain_one,
        name="normed", micros=0.2,
    )
    partial, layer_sums = phase(partial, layer_sums, after=[out_grad, *out_parts[1:]])
    grad_normed = lax.psum_scatter(partial, "pos", scatter_dimension=0, tiled=True)
    layer_sums = swap(layer_sums)
    (packed,) = step(
        with_width(pack_kernel),
        [((PACKED, channels), f32)],
        info, grad_taps, filter_hidden, features, times, filter_mid, last_layer, small,
        first_gain_grad, second_gain_grad,
        name="pack", micros=0.1,
    )
    if fold > 1:
        packed = lax.psum(packed, "seq", axis_index_groups=bundles)
    (packed,) = phase(packed)
    (in_grad,) = step(
        in_grad_kernel,
        [((3 * CUBE * channels, lane), bf16)],
        info, grad_projected, *normed_slots,
        name="in_grad", micros=0.1,
    )
    out_slots = step(
        out_sum_kernel, [((channels, lane), t) for t in (f32, bf16, bf16, bf16)], info, out_grad,
        name="out_sum", micros=0.1,
    )
    (block_output,) = step(
        finish_kernel, [((rows, width), bf16)], residual, *out_parts, name="finish", micros=0.1
    )
    for bit in (1, 2, 4):
        packed = packed + hop(packed, bit)
    in_grad, packed, *sent = phase(in_grad, packed, *out_slots[1:], after=[layer_sums])
    in_grad = swap(in_grad)
    out_slots = [out_slots[0]] + [ring(v, j) for j, v in enumerate(sent, 1)]
    up_grad, down_grad = step(
        layer_end_kernel, [((lane, hidden), f32), ((hidden, lane), f32)], layer_sums, name="layer_end"
    )
    packed_slots = [packed, near_ring(packed, 1)]
    packed_slots += [near_ring(v, 2) for v in packed_slots]
    small_grads = step(
        unpack_kernel,
        [
            ((1, width), f32),
            ((1, width), f32),
            ((3, 3 * width), f32),
            ((1, width), f32),
            ((EMB, inner), f32),
            ((1, inner), f32),
            ((inner, inner), f32),
            ((1, inner), f32),
            ((inner, width), f32),
        ],
        info, *packed_slots,
        scratch=[((RING, PACKED, channels), f32)],
        name="unpack",
    )
    (input_grad,) = step(
        end_kernel, [((rows, width), bf16)], grad_normed, inputs, gain_one, grad_res, name="end", micros=4
    )
    (out_grad,) = step(out_end_kernel, [((channels, lane), f32)], *out_slots, name="out_end")
    (in_grad,) = step(in_end_kernel, [((3, lane, channels), f32)], in_grad, name="in_end")
    return (
        block_output,
        input_grad,
        settle(in_grad, 1).transpose(1, 0, 2),
        settle(out_grad, 1),
        settle(up_grad, 0),
        settle(down_grad, 1),
        small_grads[0].reshape(width),
        small_grads[1].reshape(width),
        small_grads[2],
        small_grads[3].reshape(width),
        small_grads[4],
        small_grads[5].reshape(inner),
        small_grads[6],
        small_grads[7].reshape(inner),
        small_grads[8],
    )


def solution(mesh):
    rows = P(("seq", "pos"), None)
    in_place, down_place, up_place = P("seq", None, "pos"), P("pos", "seq"), P("seq", "pos")
    return jax.shard_map(
        on_device,
        mesh=mesh,
        in_specs=(rows, rows, P("seq"), in_place, down_place, up_place, down_place) + (P(),) * 9,
        out_specs=(rows, rows, in_place, down_place, up_place, down_place) + (P(),) * 9,
        check_vma=False,
    )
```

```python
import functools
import math

import jax
import jax.numpy as jnp
import ml_dtypes
import numpy as np
from jax import lax
from jax.experimental import pallas as pl
from jax.experimental.pallas import tpu as pltpu
from jax.sharding import PartitionSpec as P

EMB = 33
LSEQ = 1024
RING = 4
CUBE = 8
PLANE = 4
SCALE = 1.0

epsilon = 1e-05
highest = lax.Precision.HIGHEST
f32 = jnp.float32
bf16 = jnp.bfloat16

OWNED = 80
GAINS = 8
SHARED = 64
PACKED = OWNED + GAINS + SHARED


def nt_dot(left, right):
    return lax.dot_general(left, right, (((1,), (1,)), ((), ())), preferred_element_type=f32)


def tn_dot(left, right):
    return lax.dot_general(left, right, (((0,), (0,)), ((), ())), preferred_element_type=f32)


def nn_dot(left, right):
    return jnp.dot(left, right, preferred_element_type=f32)


def full_dot(left, right, dims=((1,), (0,))):
    return lax.dot_general(left, right, (dims, ((), ())), precision=highest, preferred_element_type=f32)


def embedding(seq_len):
    positions = np.concatenate([np.arange(0, seq_len, 2), np.arange(1, seq_len, 2)])
    timeline = positions / (seq_len - 1)
    band_count = (EMB - 1) // 2
    bands = np.linspace(0.0001, band_count - 1, band_count)
    phases = (2.0 * math.pi / seq_len * positions)[:, None] * bands[None, :]
    features = np.concatenate([timeline[:, None], np.cos(phases), -np.sin(phases)], 1)
    return features.astype(np.float32), timeline.astype(np.float32)[:, None]


def spectral_tables(length):
    half = length // 2
    freq = 2 * np.arange(half) + 1
    tables = []
    for offset in (1, 3):
        angle = (freq[:, None] * (4 * np.arange(half) + offset)[None, :]) % (8 * length)
        angle = angle * (math.pi / (4 * length))
        tables.append(np.concatenate([np.cos(angle), np.sin(angle)]))
    tables += [tables[0].T / length, tables[1].T / length]
    split = []
    for table in tables:
        top = table.astype(ml_dtypes.bfloat16)
        split += [top, (table - top.astype(np.float64)).astype(ml_dtypes.bfloat16)]
    order = np.concatenate([np.arange(half), length - 1 - np.arange(half)])
    turn = (2.0 * order + 1.0) * (math.pi / (4 * length))
    turns = np.stack([np.cos(turn), np.sin(turn)]).astype(np.float32)[:, :, None]
    return split, turns


def split_dot(table_top, table_low, value):
    top = value.astype(bf16)
    low = (value - top.astype(f32)).astype(bf16)
    return nn_dot(table_top, top) + nn_dot(table_top, low) + nn_dot(table_low, top)


def transform(tables, even, odd):
    half = even.shape[0]
    even_sums = split_dot(tables[0][...], tables[1][...], even)
    odd_sums = split_dot(tables[2][...], tables[3][...], odd)
    even_cos, even_sin = even_sums[:half], even_sums[half:]
    odd_cos, odd_sin = odd_sums[:half], odd_sums[half:]
    real = jnp.concatenate([even_cos + odd_cos, even_sin - odd_sin], 0)
    imag = jnp.concatenate([-(even_sin + odd_sin), odd_cos - even_cos], 0)
    return real, imag


def restore(tables, real, imag):
    half = real.shape[0] // 2
    real_low, real_up, imag_low, imag_up = real[:half], real[half:], imag[:half], imag[half:]
    even = jnp.concatenate([real_low - imag_up, real_up - imag_low], 0)
    odd = jnp.concatenate([real_low + imag_up, -(real_up + imag_low)], 0)
    return (
        split_dot(tables[4][...], tables[5][...], even),
        split_dot(tables[6][...], tables[7][...], odd),
    )


def later(value):
    row = lax.broadcasted_iota(jnp.int32, value.shape, 0)
    return jnp.where(row == 0, 0.0, pltpu.roll(value, 1, 0))


def sooner(value):
    row = lax.broadcasted_iota(jnp.int32, value.shape, 0)
    last = value.shape[0] - 1
    return jnp.where(row == last, 0.0, pltpu.roll(value, last, 0))


def mix_streams(even, odd, lags):
    mixed_even = lags[0] * even + lags[1] * later(odd) + lags[2] * later(even)
    mixed_odd = lags[0] * odd + lags[1] * even + lags[2] * later(odd)
    return mixed_even, mixed_odd


def valid_rows(length, half, offset):
    place = 2 * lax.broadcasted_iota(jnp.int32, (half, 1), 0) + offset
    return jnp.where(place < length, 1.0, 0.0)


def row_order(rows, dtype):
    left = lax.broadcasted_iota(jnp.int32, (rows, rows), 0)
    right = lax.broadcasted_iota(jnp.int32, (rows, rows), 1)
    half = rows // 2
    source = jnp.where(left < half, 2 * left, 2 * (left - half) + 1)
    return jnp.where(right == source, 1.0, 0.0).astype(dtype)


def standardize(values):
    centred = values - jnp.mean(values, axis=-1, keepdims=True)
    scaling = lax.rsqrt(jnp.mean(centred * centred, axis=-1, keepdims=True) + epsilon)
    return centred * scaling, scaling


def scale_back(unit, scaling, weighted):
    return scaling * (
        weighted
        - jnp.mean(weighted, axis=-1, keepdims=True)
        - unit * jnp.mean(weighted * unit, axis=-1, keepdims=True)
    )


def piece(place, size):
    return pl.ds(pl.multiple_of(place * size, size), size)


def rows_kernel(rows_in, cot_in, gains, normed, inputs, cot):
    order = row_order(rows_in.shape[0], bf16)
    inputs[...] = nn_dot(order, rows_in[...]).astype(bf16)
    cot[...] = nn_dot(order, cot_in[...]).astype(bf16)
    unit, _ = standardize(inputs[...].astype(f32))
    normed[...] = (unit * gains[...]).astype(bf16)


def weights_kernel(in_w, up_w, down_w, o0, o1, o2, o3, in_rows, layer_rows, out_rows):
    streams, channels = in_w.shape[0], in_w.shape[2]
    for k in range(streams):
        in_rows[pl.ds(k * channels, channels), :] = in_w[k].T
    for j, slot in enumerate((o0, o1, o2, o3)):
        out_rows[pl.ds(j * channels, channels), :] = slot[...]
    turned = up_w[...].T
    part = turned.shape[0] // CUBE
    for m in range(CUBE):
        layer_rows[pl.ds(2 * m * part, part), :] = turned[m * part : (m + 1) * part]
        layer_rows[pl.ds((2 * m + 1) * part, part), :] = down_w[pl.ds(m * part, part), :]


def side_by_side(ref, out):
    count, lane = ref.shape[0] // CUBE, ref.shape[1]
    for m in range(CUBE):
        out[:, pl.ds(m * lane, lane)] = ref[pl.ds(m * count, count), :]


def decay_of(info, times, channels, width):
    lanes = lax.broadcasted_iota(jnp.int32, (1, channels), 1) + info[2] * channels
    slowest = math.log(0.01) / 1.5
    fastest = math.log(0.01) / 0.3
    rates = jnp.abs(slowest + (fastest - slowest) * lanes.astype(f32) / (width - 1))
    return jnp.exp(-times[...] * rates)


def pair_dot(left, right):
    half = left.shape[0] // 2
    return jnp.concatenate([full_dot(left[:half], right), full_dot(left[half:], right)], 1)


def unpair(value):
    lanes = value.shape[1] // 2
    return jnp.concatenate([value[:, :lanes], value[:, lanes:]], 0)


def hidden_kernel(features, first, bias_one, middle, bias_two, hidden):
    inner = middle.shape[0]
    twice = lambda ref: jnp.concatenate([ref[...], ref[...]], 1)
    angle = pair_dot(features[...], first[...]) + twice(bias_one)
    one = unpair(jnp.sin(angle))
    hidden[:, pl.ds(0, inner)] = one
    hidden[:, pl.ds(inner, inner)] = unpair(jnp.cos(angle))
    angle = pair_dot(one, middle[...]) + twice(bias_two)
    hidden[:, pl.ds(2 * inner, inner)] = unpair(jnp.sin(angle))
    hidden[:, pl.ds(3 * inner, inner)] = unpair(jnp.cos(angle))


def taps_kernel(info, width, hidden, times, last, turns, *refs):
    tables, (spectrum,) = refs[:8], refs[8:]
    half = hidden.shape[0] // 2
    inner = last.shape[0]
    taps = full_dot(hidden[:, pl.ds(2 * inner, inner)], last[...]) * decay_of(info, times, last.shape[1], width)
    real, imag = transform(tables, taps[:half], taps[half:])
    spectrum[0] = real * turns[0] - imag * turns[1]
    spectrum[1] = real * turns[1] + imag * turns[0]


def ring_blocks(info, count):
    return [piece((info[2] + j) & (RING - 1), count) for j in range(RING)]


def conv_kernel(info, *refs):
    slots, (in_all, lags, skip, spectrum), refs = refs[:4], refs[4:8], refs[8:]
    tables = refs[:8]
    projected, long_conv, driven_spectrum, gated, in_full = refs[8:]
    length = info[3]
    half_rows = slots[0].shape[0] // 2
    half = projected.shape[0] // 2
    channels = skip.shape[1]
    side_by_side(in_all, in_full)
    for j, slot in enumerate(slots):
        total = nt_dot(slot[...], in_full[...]).astype(bf16)
        block = (info[2] + j) & (RING - 1)
        projected[piece(block, half_rows), :] = total[:half_rows]
        projected[pl.ds(pl.multiple_of(half + block * half_rows, half_rows), half_rows), :] = total[half_rows:]
    streams = []
    for k in range(3):
        lanes = pl.ds(k * channels, channels)
        streams.append(
            mix_streams(
                projected[pl.ds(0, half), lanes].astype(f32),
                projected[pl.ds(half, half), lanes].astype(f32),
                [lags[pl.ds(i, 1), lanes] for i in range(3)],
            )
        )
    (outer_even, outer_odd), (inner_even, inner_odd), (value_even, value_odd) = streams
    even = value_even * inner_even * valid_rows(length, half, 0)
    odd = value_odd * inner_odd * valid_rows(length, half, 1)
    real, imag = transform(tables, even, odd)
    driven_spectrum[0] = real
    driven_spectrum[1] = imag
    taps_real, taps_imag = spectrum[0], spectrum[1]
    back_even, back_odd = restore(
        tables, real * taps_real - imag * taps_imag, real * taps_imag + imag * taps_real
    )
    back_even += skip[...] * even
    back_odd += skip[...] * odd
    long_conv[pl.ds(0, half), :] = back_even
    long_conv[pl.ds(half, half), :] = back_odd
    even, odd = (back_even * outer_even).astype(bf16), (back_odd * outer_odd).astype(bf16)
    for z in range(RING):
        here = slice(z * half_rows, (z + 1) * half_rows)
        gated[pl.ds(2 * z * half_rows, half_rows), :] = even[here]
        gated[pl.ds((2 * z + 1) * half_rows, half_rows), :] = odd[here]


def out_kernel(info, gated, out_all, inputs, gains, residual, second):
    rows, width = inputs.shape
    lane = out_all.shape[1]
    wide = jnp.concatenate([gated[block, :] for block in ring_blocks(info, rows)], 1)
    for m in range(CUBE):
        lanes = pl.ds(m * lane, lane)
        residual[:, lanes] = inputs[:, lanes].astype(f32) + nn_dot(wide, out_all[pl.ds(m * width, width), :])
    unit, _ = standardize(residual[...])
    second[...] = (unit * gains[...]).astype(bf16)


def layer_kernel(info, *refs):
    rows_in, (cot_all, *slots), refs = refs[:10], refs[10:15], refs[15:]
    out_kept, out_given, back_kept, back_given, grads, up_sum, down_sum = refs
    own, sib, across, across_sib, along, along_sib, top, low, top_sib, low_sib = rows_in
    rows = own.shape[0]
    part = slots[0].shape[0] // 2
    ups = jnp.concatenate([slot[pl.ds(0, part), :] for slot in slots], 0)
    downs = jnp.concatenate([slot[pl.ds(part, part), :] for slot in slots], 0)
    chips = ((own, sib), (across, across_sib), (along, along_sib), (top, low, top_sib, low_sib))
    for r, parts in enumerate(chips):
        second = jnp.concatenate([ref[...] for ref in parts], 0)
        cot = jnp.concatenate([cot_all[piece(info[1] ^ (2 * r + i), rows), :] for i in range(2)], 0)
        pre_act = nt_dot(second, ups)
        grad_act = nt_dot(cot, downs)
        lower = 0.5 * (1.0 + lax.erf(pre_act * math.sqrt(0.5)))
        density = jnp.exp(-0.5 * pre_act * pre_act) * (1.0 / math.sqrt(2.0 * math.pi))
        activated = (pre_act * lower).astype(bf16)
        grad_pre = (grad_act * (lower + pre_act * density)).astype(bf16)
        here = pl.ds(r * rows, rows)
        out = nn_dot(activated, downs)
        out_kept[here, :] = out[:rows].astype(bf16)
        out_given[here, :] = out[rows:].astype(bf16)
        back = nn_dot(grad_pre, ups)
        back_kept[here, :] = back[:rows].astype(bf16)
        back_given[here, :] = back[rows:].astype(bf16)
        up_grad = tn_dot(grad_pre, second)
        down_grad = tn_dot(activated, cot)
        up_sum[...] = up_grad if r == 0 else up_sum[...] + up_grad
        down_sum[...] = down_grad if r == 0 else down_sum[...] + down_grad
    for j, block in enumerate(ring_blocks(info, 2 * part)):
        here = pl.ds(j * part, part)
        both = jnp.concatenate([up_sum[here, :], down_sum[here, :]], 0)
        grads[block, :] = both.astype(bf16)


def share_kernel(kept, got, own, across, along, top, low):
    rows = own.shape[0]
    for r, ref in enumerate((own, across, along)):
        here = pl.ds(r * rows, rows)
        ref[...] = (kept[here, :].astype(f32) + got[here, :].astype(f32)).astype(bf16)
    for i, ref in enumerate((top, low)):
        here = pl.ds(3 * rows + i * rows // 2, rows // 2)
        ref[...] = (kept[here, :].astype(f32) + got[here, :].astype(f32)).astype(bf16)


def turn_kernel(across, along, top, low, across_sum, along_sum):
    half = top.shape[0]
    first, second = pl.ds(0, half), pl.ds(half, half)
    across_sum[first, :] = across[first, :]
    across_sum[second, :] = (across[second, :].astype(f32) + low[...].astype(f32)).astype(bf16)
    along_sum[first, :] = (along[first, :].astype(f32) + top[...].astype(f32)).astype(bf16)
    along_sum[second, :] = along[second, :]


def branch_kernel(
    info, own, across, along, residual, gains, cot, out_all, grad_res, branch, gain_grad, grad_gated
):
    rows, width = residual.shape
    lane = out_all.shape[1]
    channels = grad_gated.shape[1]
    back = own[...].astype(f32) + across[...].astype(f32) + along[...].astype(f32)
    unit, scaling = standardize(residual[...])
    gain_grad[...] = jnp.sum(back * unit, axis=0, keepdims=True)
    total = cot[...].astype(f32) + scale_back(unit, scaling, back * gains[...])
    grad_res[...] = total
    branch[...] = total.astype(bf16)
    total = None
    for m in range(CUBE):
        part = nt_dot(branch[:, pl.ds(m * lane, lane)], out_all[pl.ds(m * width, width), :])
        total = part if m == 0 else total + part
    total = total.astype(bf16)
    for j, block in enumerate(ring_blocks(info, rows)):
        grad_gated[block, :] = total[:, j * channels : (j + 1) * channels]


def finish_kernel(residual, own, across, along, block_output):
    total = own[...].astype(f32) + across[...].astype(f32) + along[...].astype(f32)
    total = (residual[...] + total).astype(bf16)
    block_output[...] = tn_dot(row_order(total.shape[0], bf16), total).astype(bf16)


def below(total, out):
    count, lane = total.shape[0], total.shape[1] // CUBE
    for m in range(CUBE):
        out[pl.ds(m * count, count), :] = total[:, m * lane : (m + 1) * lane].astype(out.dtype)


def below_kernel(total, out):
    below(total[...], out)


def out_grad_kernel(gated, branch, out_grad):
    rows = branch.shape[0]
    parts = [tn_dot(gated[pl.ds(z * rows, rows), :], branch[...]) for z in range(RING)]
    below(jnp.concatenate(parts, 0).astype(bf16), out_grad)


def back_kernel(
    info, grad_gated, projected, long_conv, driven_spectrum, lags, skip, spectrum, turns, *refs
):
    tables = refs[:8]
    grad_projected, grad_taps, small = refs[8:]
    length = info[3]
    channels = grad_gated.shape[1]
    half = projected.shape[0] // 2
    half_rows = half // RING
    plain, mixed = [], []
    for k in range(3):
        lanes = pl.ds(k * channels, channels)
        even = projected[pl.ds(0, half), lanes].astype(f32)
        odd = projected[pl.ds(half, half), lanes].astype(f32)
        plain.append((even, odd))
        mixed.append(mix_streams(even, odd, [lags[pl.ds(i, 1), lanes] for i in range(3)]))
    (outer_even, outer_odd), (inner_even, inner_odd), (value_even, value_odd) = mixed
    valid_even, valid_odd = valid_rows(length, half, 0), valid_rows(length, half, 1)
    gated_even, gated_odd = (
        jnp.concatenate([grad_gated[pl.ds((2 * z + i) * half_rows, half_rows), :] for z in range(RING)], 0).astype(f32)
        for i in range(2)
    )
    conv_even, conv_odd = gated_even * outer_even, gated_odd * outer_odd
    real, imag = transform(tables, conv_even, conv_odd)
    taps_real, taps_imag = spectrum[0], spectrum[1]
    driven_even, driven_odd = restore(
        tables, real * taps_real + imag * taps_imag, imag * taps_real - real * taps_imag
    )
    driven_even = (driven_even + skip[...] * conv_even) * valid_even
    driven_odd = (driven_odd + skip[...] * conv_odd) * valid_odd
    small[pl.ds(9, 1), :] = jnp.sum(
        conv_even * value_even * inner_even * valid_even + conv_odd * value_odd * inner_odd * valid_odd,
        axis=0,
        keepdims=True,
    )
    small[pl.ds(10, 6), :] = jnp.zeros((6, channels), f32)
    grads = (
        (gated_even * long_conv[pl.ds(0, half), :], gated_odd * long_conv[pl.ds(half, half), :]),
        (driven_even * value_even, driven_odd * value_odd),
        (driven_even * inner_even, driven_odd * inner_odd),
    )
    for k, (even, odd) in enumerate(grads):
        lanes = pl.ds(k * channels, channels)
        lag = [lags[pl.ds(i, 1), lanes] for i in range(3)]
        plain_even, plain_odd = plain[k]
        sums = (
            even * plain_even + odd * plain_odd,
            even * later(plain_odd) + odd * plain_even,
            even * later(plain_even) + odd * later(plain_odd),
        )
        for i in range(3):
            small[pl.ds(3 * i + k, 1), :] = jnp.sum(sums[i], axis=0, keepdims=True)
        next_even, next_odd = sooner(even), sooner(odd)
        stream_even = (lag[0] * even + lag[1] * odd + lag[2] * next_even).astype(bf16)
        stream_odd = (lag[0] * odd + lag[1] * next_even + lag[2] * next_odd).astype(bf16)
        for z in range(RING):
            here = slice(z * half_rows, (z + 1) * half_rows)
            grad_projected[pl.ds(2 * z * half_rows, half_rows), lanes] = stream_even[here]
            grad_projected[pl.ds((2 * z + 1) * half_rows, half_rows), lanes] = stream_odd[here]
    base_real, base_imag = driven_spectrum[0], driven_spectrum[1]
    cross_real = real * base_real + imag * base_imag
    cross_imag = imag * base_real - real * base_imag
    taps_even, taps_odd = restore(
        tables,
        cross_real * turns[0] + cross_imag * turns[1],
        cross_imag * turns[0] - cross_real * turns[1],
    )
    grad_taps[pl.ds(0, half), :] = taps_even
    grad_taps[pl.ds(half, half), :] = taps_odd


def normed_kernel(info, grad_projected, in_full, n0, n1, n2, n3, gains, small, partial, packed):
    rows = n0.shape[0]
    total_gain = None
    for j, (slot, block) in enumerate(zip((n0, n1, n2, n3), ring_blocks(info, rows))):
        total = nn_dot(grad_projected[block, :], in_full[...])
        partial[block, :] = total.astype(bf16)
        part = jnp.sum(total * slot[...].astype(f32), axis=0, keepdims=True)
        total_gain = part if j == 0 else total_gain + part
    total_gain = total_gain / gains[...]
    packed[...] = small[...]
    span = packed.shape[1]
    for r in range(PLANE):
        packed[pl.ds(OWNED + r, 1), :] = total_gain[:, r * span : (r + 1) * span]


def in_grad_kernel(info, grad_projected, n0, n1, n2, n3, in_grad):
    normed = jnp.concatenate([n0[...], n1[...], n2[...], n3[...]], 0)
    grad = jnp.concatenate([grad_projected[block, :] for block in ring_blocks(info, n0.shape[0])], 0)
    below(tn_dot(grad, normed).astype(bf16), in_grad)


def end_kernel(grad_normed, inputs, gains, grad_res, input_grad):
    grad = grad_normed[...].astype(f32)
    unit, scaling = standardize(inputs[...].astype(f32))
    total = (grad_res[...] + scale_back(unit, scaling, grad * gains[...])).astype(bf16)
    input_grad[...] = tn_dot(row_order(total.shape[0], bf16), total).astype(bf16)


def layer_end_kernel(parts, up_grad, down_grad):
    part = parts.shape[0] // CUBE // 2
    for m in range(CUBE):
        here = pl.ds(m * part, part)
        up_grad[:, here] = parts[pl.ds(2 * m * part, part), :].astype(f32).T
        down_grad[here, :] = parts[pl.ds((2 * m + 1) * part, part), :].astype(f32)


def out_end_kernel(own, p1, p2, p3, total):
    total[...] = own[...].astype(f32) + p1[...].astype(f32) + p2[...].astype(f32) + p3[...].astype(f32)


def in_end_kernel(parts, in_grad):
    channels = in_grad.shape[2]
    rows = parts.shape[0] // CUBE
    for k in range(in_grad.shape[0]):
        total = None
        for m in range(CUBE):
            part = parts[pl.ds(m * rows + k * channels, channels), :].astype(f32)
            total = part if m == 0 else total + part
        in_grad[k] = total.T


def pack_kernel(
    info, width, grad_taps, hidden, features, times, middle, last, small, gain_two, packed
):
    inner = middle.shape[0]
    span = packed.shape[1]
    one, slope_one, two, slope_two = (hidden[:, pl.ds(i * inner, inner)] for i in range(4))
    grad_raw = grad_taps[...] * decay_of(info, times, span, width)
    rows = ((0,), (0,))
    packed[pl.ds(0, inner), :] = full_dot(two, grad_raw, rows)
    grad_two = full_dot(grad_raw, last[...], ((1,), (1,))) * slope_two
    grad_one = full_dot(grad_two, middle[...], ((1,), (1,))) * slope_one
    packed[pl.ds(64, 16), :] = small[...]
    for r in range(PLANE):
        lanes = pl.ds(r * span, span)
        packed[pl.ds(OWNED + r, 1), :] = jnp.zeros((1, span), f32)
        packed[pl.ds(OWNED + PLANE + r, 1), :] = gain_two[:, lanes]
    start = OWNED + GAINS
    packed[pl.ds(start, SHARED), :] = jnp.zeros((SHARED, span), f32)
    packed[pl.ds(start, inner), pl.ds(0, inner)] = full_dot(one, grad_two, rows)
    packed[pl.ds(start, EMB), pl.ds(inner, inner)] = full_dot(features[...], grad_one, rows)
    packed[pl.ds(start, 1), pl.ds(2 * inner, inner)] = jnp.sum(grad_one, axis=0, keepdims=True)
    packed[pl.ds(start, 1), pl.ds(3 * inner, inner)] = jnp.sum(grad_two, axis=0, keepdims=True)


def unpack_kernel(
    info, s0, s1, s2, s3, gain_one, gain_two, short, skip, first, bias_one, middle, bias_two, last, slots
):
    place = info[2]
    for j, ref in enumerate((s0, s1, s2, s3)):
        slots[place ^ j] = ref[...]
    channels = s0.shape[1]
    inner = middle.shape[0]
    for z in range(RING):
        lanes = pl.ds(z * channels, channels)
        last[:, lanes] = slots[z, pl.ds(0, 64), :]
        for i in range(3):
            for k in range(3):
                here = pl.ds((k * RING + z) * channels, channels)
                short[pl.ds(i, 1), here] = slots[z, pl.ds(64 + 3 * i + k, 1), :]
        skip[:, lanes] = slots[z, pl.ds(64 + 9, 1), :]
    count = GAINS + SHARED
    total = slots[0, pl.ds(OWNED, count), :] + slots[1, pl.ds(OWNED, count), :]
    total += slots[2, pl.ds(OWNED, count), :] + slots[3, pl.ds(OWNED, count), :]
    for b in range(PLANE):
        lanes = pl.ds(b * channels, channels)
        gain_one[:, lanes] = total[b : b + 1]
        gain_two[:, lanes] = total[PLANE + b : PLANE + b + 1]
    total = total[GAINS:]
    middle[...] = total[:, :inner]
    first[...] = total[:EMB, inner : 2 * inner]
    bias_one[...] = total[:1, 2 * inner : 3 * inner]
    bias_two[...] = total[:1, 3 * inner :]


def tick_kernel(count, *refs):
    refs[count][...] = jnp.zeros_like(refs[count])


def run(kernel, outs, *args, scratch=(), name, micros=2.0, limit=56, after=()):
    place = lambda a: pltpu.SMEM if a.dtype == jnp.int32 else pltpu.VMEM
    shapes = [jax.ShapeDtypeStruct(*o) for o in outs]
    count = len(args)

    def body(*refs):
        kernel(*refs[:count], *refs[count + len(after) :])

    return pl.pallas_call(
        body,
        out_shape=shapes,
        in_specs=[pl.BlockSpec(memory_space=place(a)) for a in args]
        + [pl.BlockSpec(memory_space=pl.ANY) for _ in after],
        out_specs=[pl.BlockSpec(memory_space=pltpu.VMEM)] * len(shapes),
        scratch_shapes=[pltpu.VMEM(*s) for s in scratch],
        compiler_params=pltpu.CompilerParams(vmem_limit_bytes=limit * 2**20),
        cost_estimate=pl.CostEstimate(
            flops=int(SCALE * micros * 1e9), bytes_accessed=int(SCALE * micros * 3e6), transcendentals=0
        ),
        name=name,
    )(*args, *after)


def on_device(
    block_input,
    cotangent,
    lengths,
    in_proj,
    out_proj,
    up_proj,
    down_proj,
    first_gain,
    second_gain,
    short_filter,
    skip_bias,
    filter_in,
    filter_in_bias,
    filter_mid,
    filter_mid_bias,
    filter_out,
):
    seq_size = lax.axis_size("seq")
    fold = seq_size // CUBE
    member = lax.axis_index("seq") // fold
    ring_place = lax.axis_index("pos")
    rows, width = block_input.shape
    channels = width // RING
    lane = width // CUBE
    hidden = up_proj.shape[1]
    seq_len = LSEQ
    members = [[i * fold + o for i in range(CUBE)] for o in range(fold)]
    bundles = [list(range(i * fold, (i + 1) * fold)) for i in range(CUBE)]

    def hop(value, bit):
        pairs = [(i, ((i // fold) ^ bit) * fold + i % fold) for i in range(seq_size)]
        return lax.ppermute(value, "seq", pairs)

    def ring(value, shift):
        return lax.ppermute(value, "pos", [(i, (i + shift) % RING) for i in range(RING)])

    def near_ring(value, bit):
        return lax.ppermute(value, "pos", [(i, i ^ bit) for i in range(RING)])

    def to_rows(value):
        return lax.all_to_all(value, "pos", 0, 0, tiled=True)

    def swap(value):
        return lax.all_to_all(value, "seq", 0, 0, axis_index_groups=members, tiled=True)

    def gather(value):
        return lax.all_gather(value, "seq", axis=0, axis_index_groups=members, tiled=True)

    def scatter(value):
        return lax.psum_scatter(value, "seq", scatter_dimension=0, axis_index_groups=members, tiled=True)

    def settle(value, axis):
        if fold == 1:
            return value
        return lax.psum_scatter(
            value, "seq", scatter_dimension=axis, axis_index_groups=bundles, tiled=True
        )

    def widen(value, axis):
        if fold == 1:
            return value
        return lax.all_gather(value, "seq", axis=axis, axis_index_groups=bundles, tiled=True)

    info = jnp.stack([member % 2, member, ring_place, lengths[0]]).astype(jnp.int32)
    waiting = []
    latest = []

    def now(*values):
        waiting.extend(values)
        return values

    def step(kernel, outs, *args, **options):
        after = [v for v in latest + waiting if not any(v is a for a in args)]
        results = run(kernel, outs, *args, after=after, **options)
        waiting.clear()
        latest[:] = results[:1]
        return results

    def phase(*values, after=()):
        after = [v for v in latest + waiting + list(after) if not any(v is a for a in values)]
        waiting.clear()
        count = len(values) + len(after)
        mark, *passed = pl.pallas_call(
            functools.partial(tick_kernel, count),
            out_shape=[jax.ShapeDtypeStruct((8, 128), f32)]
            + [jax.ShapeDtypeStruct(v.shape, v.dtype) for v in values],
            in_specs=[pl.BlockSpec(memory_space=pl.ANY)] * count,
            out_specs=[pl.BlockSpec(memory_space=pltpu.VMEM)]
            + [pl.BlockSpec(memory_space=pl.ANY)] * len(values),
            input_output_aliases={i: i + 1 for i in range(len(values))},
            name="phase",
        )(*values, *after)
        latest[:] = [mark]
        return passed

    gain_one, gain_two = first_gain, second_gain
    in_turned = widen(in_proj.transpose(1, 0, 2), 1)
    out_shard, up_shard, down_shard = widen(out_proj, 1), widen(up_proj, 0), widen(down_proj, 1)
    out_shards = [out_shard] + [ring(out_shard, -j) for j in range(1, RING)]
    normed, inputs, cot = step(
        rows_kernel, [((rows, width), bf16)] * 3, block_input, cotangent, gain_one, name="rows", micros=0.2
    )
    normed_slots = [normed, ring(normed, -1)]
    in_rows, layer_rows, out_rows = step(
        weights_kernel,
        [((3 * channels, lane), bf16), ((2 * hidden, lane), bf16), ((width, lane), bf16)],
        in_turned, up_shard, down_shard, *out_shards,
        name="weights", micros=0.2,
    )
    in_all = gather(in_rows)
    out_all = gather(out_rows)
    layer_got = swap(layer_rows)

    channel_start = ring_place * channels
    features, times = (jnp.asarray(v) for v in embedding(seq_len))
    last_layer = lax.dynamic_slice_in_dim(filter_out, channel_start, channels, 1)
    tables, turns = spectral_tables(seq_len)
    tables = [jnp.asarray(t) for t in tables]
    turns = jnp.asarray(turns)
    lags = lax.dynamic_slice_in_dim(
        short_filter.reshape(3, 3, width), channel_start, channels, 2
    ).reshape(3, 3 * channels)
    skip = lax.dynamic_slice_in_dim(skip_bias, channel_start, channels, 0)[None]
    pair = ((2, seq_len, channels), f32)
    inner = filter_mid.shape[0]

    def with_width(kernel):
        return lambda info, *refs: kernel(info, width, *refs)

    (filter_hidden,) = step(
        hidden_kernel,
        [((seq_len, 4 * inner), f32)],
        features, filter_in, filter_in_bias[None], filter_mid, filter_mid_bias[None],
        name="hidden", micros=5,
    )
    (normed_slots[1],) = phase(normed_slots[1], after=[layer_got])
    normed_slots.append(ring(normed_slots[1], -1))
    (layer_own,) = step(
        side_by_side, [((2 * hidden // CUBE, width), bf16)], layer_got, name="layer_own", micros=0.2
    )
    (normed_slots[2],) = phase(normed_slots[2], after=[lags, skip])
    normed_slots.append(ring(normed_slots[2], -1))
    (spectrum,) = step(
        with_width(taps_kernel),
        [pair],
        info, filter_hidden, times, last_layer, turns, *tables,
        name="taps", micros=5,
    )
    layer_own, cot = phase(layer_own, cot, after=[normed_slots[3]])
    layer_slots = [layer_own, ring(layer_own, -1)]
    cot_all = gather(cot)

    projected, long_conv, driven_spectrum, gated, in_full = step(
        conv_kernel,
        [
            ((seq_len, 3 * channels), bf16),
            ((seq_len, channels), f32),
            pair,
            ((seq_len, channels), bf16),
            ((3 * channels, width), bf16),
        ],
        info, *normed_slots, in_all, lags, skip, spectrum, *tables,
        name="conv", micros=14,
    )
    gated, layer_slots[1] = phase(gated, layer_slots[1])
    gated = to_rows(gated)
    layer_slots = phase(*layer_slots, after=[gated, out_all])
    layer_slots += [ring(layer_slots[1], -1), ring(layer_slots[0], 1)]
    residual, second = step(
        out_kernel,
        [((rows, width), f32), ((rows, width), bf16)],
        info, gated, out_all, inputs, gain_two,
        name="out", micros=0.2,
    )

    second_sib, across, along = (hop(second, bit) for bit in (1, 2, 4))
    half = rows // 2
    top, low = hop(along[:half], 2), hop(across[half:], 4)
    across_sib, along_sib, top_sib, low_sib = (hop(v, 1) for v in (across, along, top, low))
    wide = CUBE * rows // 2
    out_kept, out_given, back_kept, back_given, layer_grads = step(
        layer_kernel,
        [((wide, width), bf16)] * 4 + [((hidden, width), bf16)],
        info, second, second_sib, across, across_sib, along, along_sib, top, low, top_sib, low_sib,
        cot_all, *layer_slots,
        scratch=[((hidden // 2, width), f32)] * 2,
        name="layer", micros=22,
    )
    back_given, out_given, layer_grads = phase(back_given, out_given, layer_grads)
    layer_grads = lax.psum_scatter(layer_grads, "pos", scatter_dimension=0, tiled=True)

    block, part = ((rows, width), bf16), ((half, width), bf16)
    shares = [
        step(share_kernel, [block] * 3 + [part] * 2, kept, hop(given, 1), name="share", micros=0.1)
        for kept, given in ((back_kept, back_given), (out_kept, out_given))
    ]

    def turn(own, across, along, top, low):
        across, along = step(
            turn_kernel, [block] * 2, across, along, hop(top, 2), hop(low, 4), name="turn", micros=0.1
        )
        return own, hop(across, 2), hop(along, 4)

    back_parts = turn(*shares[0])
    grad_res, branch, second_gain_grad, grad_gated = step(
        branch_kernel,
        [((rows, width), f32), ((rows, width), bf16), ((1, width), f32), ((seq_len, channels), bf16)],
        info, *back_parts, residual, gain_two, cot, out_all,
        name="branch", micros=0.2,
    )
    (grad_gated,) = phase(grad_gated, after=[layer_grads])
    grad_gated = to_rows(grad_gated)
    (out_grad,) = step(
        out_grad_kernel, [((CUBE * width, lane), bf16)], gated, branch, name="out_grad", micros=0.1
    )
    out_parts = turn(*shares[1])
    out_grad = scatter(out_grad)
    (layer_sums,) = step(below_kernel, [((2 * hidden, lane), bf16)], layer_grads, name="layer_sum", micros=0.1)

    grad_projected, grad_taps, small = step(
        back_kernel,
        [((seq_len, 3 * channels), bf16), ((seq_len, channels), f32), ((16, channels), f32)],
        info, grad_gated, projected, long_conv, driven_spectrum, lags, skip, spectrum, turns, *tables,
        name="back", micros=15,
    )
    (packed,) = step(
        with_width(pack_kernel),
        [((PACKED, channels), f32)],
        info, grad_taps, filter_hidden, features, times, filter_mid, last_layer, small, second_gain_grad,
        name="pack", micros=0.1,
    )
    partial, packed = step(
        normed_kernel,
        [((seq_len, width), bf16), ((PACKED, channels), f32)],
        info, grad_projected, in_full, *normed_slots, gain_one, packed,
        name="normed", micros=0.2,
    )
    partial, packed, layer_sums = phase(partial, packed, layer_sums, after=[out_grad])
    grad_normed = lax.psum_scatter(partial, "pos", scatter_dimension=0, tiled=True)
    layer_sums = swap(layer_sums)
    if fold > 1:
        packed = lax.psum(packed, "seq", axis_index_groups=bundles)
    (in_grad,) = step(
        in_grad_kernel,
        [((3 * CUBE * channels, lane), bf16)],
        info, grad_projected, *normed_slots,
        name="in_grad", micros=0.1,
    )
    for bit in (1, 2, 4):
        packed = packed + hop(packed, bit)
    in_grad, packed, out_grad = phase(in_grad, packed, out_grad, after=[layer_sums, *out_parts[1:]])
    in_grad = swap(in_grad)
    out_slots = [
        lax.dynamic_slice_in_dim(out_grad, (ring_place + j) % RING * channels, channels) for j in range(RING)
    ]
    out_slots = [out_slots[0]] + [ring(out_slots[j], j) for j in range(1, RING)]
    packed_slots = [packed, near_ring(packed, 1)]
    packed_slots += [near_ring(v, 2) for v in packed_slots]
    up_grad, down_grad = step(
        layer_end_kernel, [((lane, hidden), f32), ((hidden, lane), f32)], layer_sums, name="layer_end"
    )
    (block_output,) = step(
        finish_kernel, [((rows, width), bf16)], residual, *out_parts, name="finish", micros=0.1
    )
    (out_grad,) = step(out_end_kernel, [((channels, lane), f32)], *out_slots, name="out_end")
    small_grads = step(
        unpack_kernel,
        [
            ((1, width), f32),
            ((1, width), f32),
            ((3, 3 * width), f32),
            ((1, width), f32),
            ((EMB, inner), f32),
            ((1, inner), f32),
            ((inner, inner), f32),
            ((1, inner), f32),
            ((inner, width), f32),
        ],
        info, *packed_slots,
        scratch=[((RING, PACKED, channels), f32)],
        name="unpack",
    )
    (in_grad,) = step(in_end_kernel, [((3, lane, channels), f32)], in_grad, name="in_end")
    (input_grad,) = step(
        end_kernel, [((rows, width), bf16)], grad_normed, inputs, gain_one, grad_res, name="end", micros=1
    )
    return (
        block_output,
        input_grad,
        settle(in_grad, 1).transpose(1, 0, 2),
        settle(out_grad, 1),
        settle(up_grad, 0),
        settle(down_grad, 1),
        small_grads[0].reshape(width),
        small_grads[1].reshape(width),
        small_grads[2],
        small_grads[3].reshape(width),
        small_grads[4],
        small_grads[5].reshape(inner),
        small_grads[6],
        small_grads[7].reshape(inner),
        small_grads[8],
    )


def solution(mesh):
    rows = P(("seq", "pos"), None)
    in_place, down_place, up_place = P("seq", None, "pos"), P("pos", "seq"), P("seq", "pos")
    return jax.shard_map(
        on_device,
        mesh=mesh,
        in_specs=(rows, rows, P("seq"), in_place, down_place, up_place, down_place) + (P(),) * 9,
        out_specs=(rows, rows, in_place, down_place, up_place, down_place) + (P(),) * 9,
        check_vma=False,
    )
```

```python
import functools
import math

import jax
import jax.numpy as jnp
import ml_dtypes
import numpy as np
from jax import lax
from jax.experimental import pallas as pl
from jax.experimental.pallas import tpu as pltpu
from jax.sharding import PartitionSpec as P

EMB = 33
LSEQ = 1024
RING = 4
CUBE = 8
PLANE = 4
SCALE = 1.0

epsilon = 1e-05
highest = lax.Precision.HIGHEST
f32 = jnp.float32
bf16 = jnp.bfloat16

OWNED = 80
GAINS = 8
SHARED = 64
PACKED = OWNED + GAINS + SHARED

SPARE = 16


def nt_dot(left, right):
    return lax.dot_general(left, right, (((1,), (1,)), ((), ())), preferred_element_type=f32)


def tn_dot(left, right):
    return lax.dot_general(left, right, (((0,), (0,)), ((), ())), preferred_element_type=f32)


def nn_dot(left, right):
    return jnp.dot(left, right, preferred_element_type=f32)


def full_dot(left, right, dims=((1,), (0,))):
    return lax.dot_general(left, right, (dims, ((), ())), precision=highest, preferred_element_type=f32)


def embedding(seq_len):
    positions = np.concatenate([np.arange(0, seq_len, 2), np.arange(1, seq_len, 2)])
    timeline = positions / (seq_len - 1)
    band_count = (EMB - 1) // 2
    bands = np.linspace(0.0001, band_count - 1, band_count)
    phases = (2.0 * math.pi / seq_len * positions)[:, None] * bands[None, :]
    features = np.concatenate([timeline[:, None], np.cos(phases), -np.sin(phases)], 1)
    return features.astype(np.float32), timeline.astype(np.float32)[:, None]


def spectral_tables(length):
    half = length // 2
    freq = 2 * np.arange(half) + 1
    tables = []
    for offset in (1, 3):
        angle = (freq[:, None] * (4 * np.arange(half) + offset)[None, :]) % (8 * length)
        angle = angle * (math.pi / (4 * length))
        tables.append(np.concatenate([np.cos(angle), np.sin(angle)]))
    tables += [tables[0].T / length, tables[1].T / length]
    split = []
    for table in tables:
        top = table.astype(ml_dtypes.bfloat16)
        split += [top, (table - top.astype(np.float64)).astype(ml_dtypes.bfloat16)]
    order = np.concatenate([np.arange(half), length - 1 - np.arange(half)])
    turn = (2.0 * order + 1.0) * (math.pi / (4 * length))
    turns = np.stack([np.cos(turn), np.sin(turn)]).astype(np.float32)[:, :, None]
    return split, turns


def split_dot(table_top, table_low, value):
    top = value.astype(bf16)
    low = (value - top.astype(f32)).astype(bf16)
    return nn_dot(table_top, top) + nn_dot(table_top, low) + nn_dot(table_low, top)


def transform(tables, even, odd):
    half = even.shape[0]
    even_sums = split_dot(tables[0][...], tables[1][...], even)
    odd_sums = split_dot(tables[2][...], tables[3][...], odd)
    even_cos, even_sin = even_sums[:half], even_sums[half:]
    odd_cos, odd_sin = odd_sums[:half], odd_sums[half:]
    real = jnp.concatenate([even_cos + odd_cos, even_sin - odd_sin], 0)
    imag = jnp.concatenate([-(even_sin + odd_sin), odd_cos - even_cos], 0)
    return real, imag


def restore(tables, real, imag):
    half = real.shape[0] // 2
    real_low, real_up, imag_low, imag_up = real[:half], real[half:], imag[:half], imag[half:]
    even = jnp.concatenate([real_low - imag_up, real_up - imag_low], 0)
    odd = jnp.concatenate([real_low + imag_up, -(real_up + imag_low)], 0)
    return (
        split_dot(tables[4][...], tables[5][...], even),
        split_dot(tables[6][...], tables[7][...], odd),
    )


def later(value):
    row = lax.broadcasted_iota(jnp.int32, value.shape, 0)
    return jnp.where(row == 0, 0.0, pltpu.roll(value, 1, 0))


def sooner(value):
    row = lax.broadcasted_iota(jnp.int32, value.shape, 0)
    last = value.shape[0] - 1
    return jnp.where(row == last, 0.0, pltpu.roll(value, last, 0))


def mix_streams(even, odd, lags):
    mixed_even = lags[0] * even + lags[1] * later(odd) + lags[2] * later(even)
    mixed_odd = lags[0] * odd + lags[1] * even + lags[2] * later(odd)
    return mixed_even, mixed_odd


def valid_rows(length, half, offset):
    place = 2 * lax.broadcasted_iota(jnp.int32, (half, 1), 0) + offset
    return jnp.where(place < length, 1.0, 0.0)


def row_order(rows, dtype):
    left = lax.broadcasted_iota(jnp.int32, (rows, rows), 0)
    right = lax.broadcasted_iota(jnp.int32, (rows, rows), 1)
    half = rows // 2
    source = jnp.where(left < half, 2 * left, 2 * (left - half) + 1)
    return jnp.where(right == source, 1.0, 0.0).astype(dtype)


def standardize(values):
    centred = values - jnp.mean(values, axis=-1, keepdims=True)
    scaling = lax.rsqrt(jnp.mean(centred * centred, axis=-1, keepdims=True) + epsilon)
    return centred * scaling, scaling


def scale_back(unit, scaling, weighted):
    return scaling * (
        weighted
        - jnp.mean(weighted, axis=-1, keepdims=True)
        - unit * jnp.mean(weighted * unit, axis=-1, keepdims=True)
    )


def piece(place, size):
    return pl.ds(pl.multiple_of(place * size, size), size)


def rows_kernel(rows_in, cot_in, gains, normed, inputs, cot):
    order = row_order(rows_in.shape[0], bf16)
    inputs[...] = nn_dot(order, rows_in[...]).astype(bf16)
    cot[...] = nn_dot(order, cot_in[...]).astype(bf16)
    unit, _ = standardize(inputs[...].astype(f32))
    normed[...] = (unit * gains[...]).astype(bf16)


def weights_kernel(in_w, up_w, down_w, o0, o1, o2, o3, in_rows, layer_rows, out_rows):
    streams, channels = in_w.shape[0], in_w.shape[2]
    for k in range(streams):
        in_rows[pl.ds(k * channels, channels), :] = in_w[k].T
    for j, slot in enumerate((o0, o1, o2, o3)):
        out_rows[pl.ds(j * channels, channels), :] = slot[...]
    turned = up_w[...].T
    part = turned.shape[0] // CUBE
    for m in range(CUBE):
        layer_rows[pl.ds(2 * m * part, part), :] = turned[m * part : (m + 1) * part]
        layer_rows[pl.ds((2 * m + 1) * part, part), :] = down_w[pl.ds(m * part, part), :]


def side_by_side(ref, out):
    count, lane = ref.shape[0] // CUBE, ref.shape[1]
    for m in range(CUBE):
        out[pl.ds(0, count), pl.ds(m * lane, lane)] = ref[pl.ds(m * count, count), :]
    if out.shape[0] > count:
        out[pl.ds(count, out.shape[0] - count), :] = jnp.zeros((out.shape[0] - count, out.shape[1]), out.dtype)


def decay_of(info, times, channels, width):
    lanes = lax.broadcasted_iota(jnp.int32, (1, channels), 1) + info[2] * channels
    slowest = math.log(0.01) / 1.5
    fastest = math.log(0.01) / 0.3
    rates = jnp.abs(slowest + (fastest - slowest) * lanes.astype(f32) / (width - 1))
    return jnp.exp(-times[...] * rates)


def pair_dot(left, right):
    half = left.shape[0] // 2
    return jnp.concatenate([full_dot(left[:half], right), full_dot(left[half:], right)], 1)


def unpair(value):
    lanes = value.shape[1] // 2
    return jnp.concatenate([value[:, :lanes], value[:, lanes:]], 0)


def hidden_kernel(features, first, bias_one, middle, bias_two, hidden):
    inner = middle.shape[0]
    twice = lambda ref: jnp.concatenate([ref[...], ref[...]], 1)
    angle = pair_dot(features[...], first[...]) + twice(bias_one)
    one = unpair(jnp.sin(angle))
    hidden[:, pl.ds(0, inner)] = one
    hidden[:, pl.ds(inner, inner)] = unpair(jnp.cos(angle))
    angle = pair_dot(one, middle[...]) + twice(bias_two)
    hidden[:, pl.ds(2 * inner, inner)] = unpair(jnp.sin(angle))
    hidden[:, pl.ds(3 * inner, inner)] = unpair(jnp.cos(angle))


def taps_kernel(info, width, hidden, times, last, turns, *refs):
    tables, (spectrum,) = refs[:8], refs[8:]
    half = hidden.shape[0] // 2
    inner = last.shape[0]
    taps = full_dot(hidden[:, pl.ds(2 * inner, inner)], last[...]) * decay_of(info, times, last.shape[1], width)
    real, imag = transform(tables, taps[:half], taps[half:])
    spectrum[0] = real * turns[0] - imag * turns[1]
    spectrum[1] = real * turns[1] + imag * turns[0]


def ring_blocks(info, count):
    return [piece((info[2] + j) & (RING - 1), count) for j in range(RING)]


def conv_kernel(info, *refs):
    slots, (in_all, lags, skip, spectrum), refs = refs[:4], refs[4:8], refs[8:]
    tables = refs[:8]
    projected, long_conv, driven_spectrum, gated, in_full = refs[8:]
    length = info[3]
    half_rows = slots[0].shape[0] // 2
    half = projected.shape[0] // 2
    channels = skip.shape[1]
    side_by_side(in_all, in_full)
    for j, slot in enumerate(slots):
        total = nt_dot(slot[...], in_full[...]).astype(bf16)
        block = (info[2] + j) & (RING - 1)
        projected[piece(block, half_rows), :] = total[:half_rows]
        projected[pl.ds(pl.multiple_of(half + block * half_rows, half_rows), half_rows), :] = total[half_rows:]
    streams = []
    for k in range(3):
        lanes = pl.ds(k * channels, channels)
        streams.append(
            mix_streams(
                projected[pl.ds(0, half), lanes].astype(f32),
                projected[pl.ds(half, half), lanes].astype(f32),
                [lags[pl.ds(i, 1), lanes] for i in range(3)],
            )
        )
    (outer_even, outer_odd), (inner_even, inner_odd), (value_even, value_odd) = streams
    even = value_even * inner_even * valid_rows(length, half, 0)
    odd = value_odd * inner_odd * valid_rows(length, half, 1)
    real, imag = transform(tables, even, odd)
    driven_spectrum[0] = real
    driven_spectrum[1] = imag
    taps_real, taps_imag = spectrum[0], spectrum[1]
    back_even, back_odd = restore(
        tables, real * taps_real - imag * taps_imag, real * taps_imag + imag * taps_real
    )
    back_even += skip[...] * even
    back_odd += skip[...] * odd
    long_conv[pl.ds(0, half), :] = back_even
    long_conv[pl.ds(half, half), :] = back_odd
    even, odd = (back_even * outer_even).astype(bf16), (back_odd * outer_odd).astype(bf16)
    for z in range(RING):
        here = slice(z * half_rows, (z + 1) * half_rows)
        gated[pl.ds(2 * z * half_rows, half_rows), :] = even[here]
        gated[pl.ds((2 * z + 1) * half_rows, half_rows), :] = odd[here]


def out_kernel(info, gated, out_all, inputs, gains, residual, second):
    rows, width = inputs.shape
    lane = out_all.shape[1]
    wide = jnp.concatenate([gated[block, :] for block in ring_blocks(info, rows)], 1)
    for m in range(CUBE):
        lanes = pl.ds(m * lane, lane)
        residual[:, lanes] = inputs[:, lanes].astype(f32) + nn_dot(wide, out_all[pl.ds(m * width, width), :])
    unit, _ = standardize(residual[...])
    second[...] = (unit * gains[...]).astype(bf16)


def layer_kernel(info, *refs):
    rows_in, (cot_all, *slots), refs = refs[:10], refs[10:15], refs[15:]
    out_kept, out_given, back_kept, back_given, grads, up_sum, down_sum = refs
    own, sib, across, across_sib, along, along_sib, top, low, top_sib, low_sib = rows_in
    rows = own.shape[0]
    part = (slots[0].shape[0] - SPARE) // 2
    ups = jnp.concatenate([slot[pl.ds(0, part), :] for slot in slots], 0)
    downs = jnp.concatenate([slot[pl.ds(part, part), :] for slot in slots], 0)
    chips = ((own, sib), (across, across_sib), (along, along_sib), (top, low, top_sib, low_sib))
    for r, parts in enumerate(chips):
        second = jnp.concatenate([ref[...] for ref in parts], 0)
        cot = jnp.concatenate([cot_all[piece(info[1] ^ (2 * r + i), rows), :] for i in range(2)], 0)
        pre_act = nt_dot(second, ups)
        grad_act = nt_dot(cot, downs)
        lower = 0.5 * (1.0 + lax.erf(pre_act * math.sqrt(0.5)))
        density = jnp.exp(-0.5 * pre_act * pre_act) * (1.0 / math.sqrt(2.0 * math.pi))
        activated = (pre_act * lower).astype(bf16)
        grad_pre = (grad_act * (lower + pre_act * density)).astype(bf16)
        here = pl.ds(r * rows, rows)
        out = nn_dot(activated, downs)
        out_kept[here, :] = out[:rows].astype(bf16)
        out_given[here, :] = out[rows:].astype(bf16)
        back = nn_dot(grad_pre, ups)
        back_kept[here, :] = back[:rows].astype(bf16)
        back_given[here, :] = back[rows:].astype(bf16)
        up_grad = tn_dot(grad_pre, second)
        down_grad = tn_dot(activated, cot)
        up_sum[...] = up_grad if r == 0 else up_sum[...] + up_grad
        down_sum[...] = down_grad if r == 0 else down_sum[...] + down_grad
    for j, block in enumerate(ring_blocks(info, 2 * part)):
        here = pl.ds(j * part, part)
        both = jnp.concatenate([up_sum[here, :], down_sum[here, :]], 0)
        grads[block, :] = both.astype(bf16)


def share_kernel(kept, got, own, across, along, top, low):
    rows = own.shape[0]
    for r, ref in enumerate((own, across, along)):
        here = pl.ds(r * rows, rows)
        ref[...] = (kept[here, :].astype(f32) + got[here, :].astype(f32)).astype(bf16)
    for i, ref in enumerate((top, low)):
        here = pl.ds(3 * rows + i * rows // 2, rows // 2)
        ref[...] = (kept[here, :].astype(f32) + got[here, :].astype(f32)).astype(bf16)


def turn_kernel(across, along, top, low, across_sum, along_sum):
    half = top.shape[0]
    first, second = pl.ds(0, half), pl.ds(half, half)
    across_sum[first, :] = across[first, :]
    across_sum[second, :] = (across[second, :].astype(f32) + low[...].astype(f32)).astype(bf16)
    along_sum[first, :] = (along[first, :].astype(f32) + top[...].astype(f32)).astype(bf16)
    along_sum[second, :] = along[second, :]


def branch_kernel(
    info, own, across, along, residual, gains, cot, out_all, grad_res, branch, gain_grad, grad_gated
):
    rows, width = residual.shape
    lane = out_all.shape[1]
    channels = grad_gated.shape[1]
    back = own[...].astype(f32) + across[...].astype(f32) + along[...].astype(f32)
    unit, scaling = standardize(residual[...])
    gain_grad[...] = jnp.sum(back * unit, axis=0, keepdims=True)
    total = cot[...].astype(f32) + scale_back(unit, scaling, back * gains[...])
    grad_res[...] = total
    branch[...] = total.astype(bf16)
    total = None
    for m in range(CUBE):
        part = nt_dot(branch[:, pl.ds(m * lane, lane)], out_all[pl.ds(m * width, width), :])
        total = part if m == 0 else total + part
    total = total.astype(bf16)
    for j, block in enumerate(ring_blocks(info, rows)):
        grad_gated[block, :] = total[:, j * channels : (j + 1) * channels]


def finish_kernel(residual, own, across, along, block_output):
    total = own[...].astype(f32) + across[...].astype(f32) + along[...].astype(f32)
    total = (residual[...] + total).astype(bf16)
    block_output[...] = tn_dot(row_order(total.shape[0], bf16), total).astype(bf16)


def below(total, out):
    count, lane = total.shape[0], total.shape[1] // CUBE
    for m in range(CUBE):
        out[pl.ds(m * count, count), :] = total[:, m * lane : (m + 1) * lane].astype(out.dtype)


def below_kernel(total, out):
    below(total[...], out)


def out_grad_kernel(gated, branch, out_grad):
    rows = branch.shape[0]
    parts = [tn_dot(gated[pl.ds(z * rows, rows), :], branch[...]) for z in range(RING)]
    below(jnp.concatenate(parts, 0).astype(bf16), out_grad)


def back_kernel(
    info, grad_gated, projected, long_conv, driven_spectrum, lags, skip, spectrum, turns, *refs
):
    tables = refs[:8]
    grad_projected, grad_taps, small = refs[8:]
    length = info[3]
    channels = grad_gated.shape[1]
    half = projected.shape[0] // 2
    half_rows = half // RING
    plain, mixed = [], []
    for k in range(3):
        lanes = pl.ds(k * channels, channels)
        even = projected[pl.ds(0, half), lanes].astype(f32)
        odd = projected[pl.ds(half, half), lanes].astype(f32)
        plain.append((even, odd))
        mixed.append(mix_streams(even, odd, [lags[pl.ds(i, 1), lanes] for i in range(3)]))
    (outer_even, outer_odd), (inner_even, inner_odd), (value_even, value_odd) = mixed
    valid_even, valid_odd = valid_rows(length, half, 0), valid_rows(length, half, 1)
    gated_even, gated_odd = (
        jnp.concatenate([grad_gated[pl.ds((2 * z + i) * half_rows, half_rows), :] for z in range(RING)], 0).astype(f32)
        for i in range(2)
    )
    conv_even, conv_odd = gated_even * outer_even, gated_odd * outer_odd
    real, imag = transform(tables, conv_even, conv_odd)
    taps_real, taps_imag = spectrum[0], spectrum[1]
    driven_even, driven_odd = restore(
        tables, real * taps_real + imag * taps_imag, imag * taps_real - real * taps_imag
    )
    driven_even = (driven_even + skip[...] * conv_even) * valid_even
    driven_odd = (driven_odd + skip[...] * conv_odd) * valid_odd
    small[pl.ds(9, 1), :] = jnp.sum(
        conv_even * value_even * inner_even * valid_even + conv_odd * value_odd * inner_odd * valid_odd,
        axis=0,
        keepdims=True,
    )
    small[pl.ds(10, 6), :] = jnp.zeros((6, channels), f32)
    grads = (
        (gated_even * long_conv[pl.ds(0, half), :], gated_odd * long_conv[pl.ds(half, half), :]),
        (driven_even * value_even, driven_odd * value_odd),
        (driven_even * inner_even, driven_odd * inner_odd),
    )
    for k, (even, odd) in enumerate(grads):
        lanes = pl.ds(k * channels, channels)
        lag = [lags[pl.ds(i, 1), lanes] for i in range(3)]
        plain_even, plain_odd = plain[k]
        sums = (
            even * plain_even + odd * plain_odd,
            even * later(plain_odd) + odd * plain_even,
            even * later(plain_even) + odd * later(plain_odd),
        )
        for i in range(3):
            small[pl.ds(3 * i + k, 1), :] = jnp.sum(sums[i], axis=0, keepdims=True)
        next_even, next_odd = sooner(even), sooner(odd)
        stream_even = (lag[0] * even + lag[1] * odd + lag[2] * next_even).astype(bf16)
        stream_odd = (lag[0] * odd + lag[1] * next_even + lag[2] * next_odd).astype(bf16)
        for z in range(RING):
            here = slice(z * half_rows, (z + 1) * half_rows)
            grad_projected[pl.ds(2 * z * half_rows, half_rows), lanes] = stream_even[here]
            grad_projected[pl.ds((2 * z + 1) * half_rows, half_rows), lanes] = stream_odd[here]
    base_real, base_imag = driven_spectrum[0], driven_spectrum[1]
    cross_real = real * base_real + imag * base_imag
    cross_imag = imag * base_real - real * base_imag
    taps_even, taps_odd = restore(
        tables,
        cross_real * turns[0] + cross_imag * turns[1],
        cross_imag * turns[0] - cross_real * turns[1],
    )
    grad_taps[pl.ds(0, half), :] = taps_even
    grad_taps[pl.ds(half, half), :] = taps_odd


def normed_kernel(info, grad_projected, in_full, n0, n1, n2, n3, gains, small, partial, packed):
    rows = n0.shape[0]
    total_gain = None
    for j, (slot, block) in enumerate(zip((n0, n1, n2, n3), ring_blocks(info, rows))):
        total = nn_dot(grad_projected[block, :], in_full[...])
        partial[block, :] = total.astype(bf16)
        part = jnp.sum(total * slot[...].astype(f32), axis=0, keepdims=True)
        total_gain = part if j == 0 else total_gain + part
    total_gain = total_gain / gains[...]
    packed[...] = small[...]
    span = packed.shape[1]
    for r in range(PLANE):
        packed[pl.ds(OWNED + r, 1), :] = total_gain[:, r * span : (r + 1) * span]


def in_grad_kernel(info, grad_projected, n0, n1, n2, n3, in_grad):
    normed = jnp.concatenate([n0[...], n1[...], n2[...], n3[...]], 0)
    grad = jnp.concatenate([grad_projected[block, :] for block in ring_blocks(info, n0.shape[0])], 0)
    below(tn_dot(grad, normed).astype(bf16), in_grad)


def end_kernel(grad_normed, inputs, gains, grad_res, input_grad):
    grad = grad_normed[...].astype(f32)
    unit, scaling = standardize(inputs[...].astype(f32))
    total = (grad_res[...] + scale_back(unit, scaling, grad * gains[...])).astype(bf16)
    input_grad[...] = tn_dot(row_order(total.shape[0], bf16), total).astype(bf16)


def layer_end_kernel(parts, up_grad, down_grad):
    part = parts.shape[0] // CUBE // 2
    for m in range(CUBE):
        here = pl.ds(m * part, part)
        up_grad[:, here] = parts[pl.ds(2 * m * part, part), :].astype(f32).T
        down_grad[here, :] = parts[pl.ds((2 * m + 1) * part, part), :].astype(f32)


def out_end_kernel(own, p1, p2, p3, total):
    total[...] = own[...].astype(f32) + p1[...].astype(f32) + p2[...].astype(f32) + p3[...].astype(f32)


def in_end_kernel(parts, in_grad):
    channels = in_grad.shape[2]
    rows = parts.shape[0] // CUBE
    for k in range(in_grad.shape[0]):
        total = None
        for m in range(CUBE):
            part = parts[pl.ds(m * rows + k * channels, channels), :].astype(f32)
            total = part if m == 0 else total + part
        in_grad[k] = total.T


def pack_kernel(
    info, width, grad_taps, hidden, features, times, middle, last, small, gain_two, packed
):
    inner = middle.shape[0]
    span = packed.shape[1]
    one, slope_one, two, slope_two = (hidden[:, pl.ds(i * inner, inner)] for i in range(4))
    grad_raw = grad_taps[...] * decay_of(info, times, span, width)
    rows = ((0,), (0,))
    packed[pl.ds(0, inner), :] = full_dot(two, grad_raw, rows)
    grad_two = full_dot(grad_raw, last[...], ((1,), (1,))) * slope_two
    grad_one = full_dot(grad_two, middle[...], ((1,), (1,))) * slope_one
    packed[pl.ds(64, 16), :] = small[...]
    for r in range(PLANE):
        lanes = pl.ds(r * span, span)
        packed[pl.ds(OWNED + r, 1), :] = jnp.zeros((1, span), f32)
        packed[pl.ds(OWNED + PLANE + r, 1), :] = gain_two[:, lanes]
    start = OWNED + GAINS
    packed[pl.ds(start, SHARED), :] = jnp.zeros((SHARED, span), f32)
    packed[pl.ds(start, inner), pl.ds(0, inner)] = full_dot(one, grad_two, rows)
    packed[pl.ds(start, EMB), pl.ds(inner, inner)] = full_dot(features[...], grad_one, rows)
    packed[pl.ds(start, 1), pl.ds(2 * inner, inner)] = jnp.sum(grad_one, axis=0, keepdims=True)
    packed[pl.ds(start, 1), pl.ds(3 * inner, inner)] = jnp.sum(grad_two, axis=0, keepdims=True)


def unpack_kernel(
    info, s0, s1, s2, s3, gain_one, gain_two, short, skip, first, bias_one, middle, bias_two, last, slots
):
    place = info[2]
    for j, ref in enumerate((s0, s1, s2, s3)):
        slots[place ^ j] = ref[...].astype(f32)
    channels = s0.shape[1]
    inner = middle.shape[0]
    for z in range(RING):
        lanes = pl.ds(z * channels, channels)
        last[:, lanes] = slots[z, pl.ds(0, 64), :]
        for i in range(3):
            for k in range(3):
                here = pl.ds((k * RING + z) * channels, channels)
                short[pl.ds(i, 1), here] = slots[z, pl.ds(64 + 3 * i + k, 1), :]
        skip[:, lanes] = slots[z, pl.ds(64 + 9, 1), :]
    count = GAINS + SHARED
    total = slots[0, pl.ds(OWNED, count), :] + slots[1, pl.ds(OWNED, count), :]
    total += slots[2, pl.ds(OWNED, count), :] + slots[3, pl.ds(OWNED, count), :]
    for b in range(PLANE):
        lanes = pl.ds(b * channels, channels)
        gain_one[:, lanes] = total[b : b + 1]
        gain_two[:, lanes] = total[PLANE + b : PLANE + b + 1]
    total = total[GAINS:]
    middle[...] = total[:, :inner]
    first[...] = total[:EMB, inner : 2 * inner]
    bias_one[...] = total[:1, 2 * inner : 3 * inner]
    bias_two[...] = total[:1, 3 * inner :]


def tick_kernel(count, *refs):
    refs[count][...] = jnp.zeros_like(refs[count])


def run(kernel, outs, *args, scratch=(), name, micros=2.0, limit=62, after=()):
    place = lambda a: pltpu.SMEM if a.dtype == jnp.int32 else pltpu.VMEM
    shapes = [jax.ShapeDtypeStruct(*o) for o in outs]
    count = len(args)

    def body(*refs):
        kernel(*refs[:count], *refs[count + len(after) :])

    return pl.pallas_call(
        body,
        out_shape=shapes,
        in_specs=[pl.BlockSpec(memory_space=place(a)) for a in args]
        + [pl.BlockSpec(memory_space=pl.ANY) for _ in after],
        out_specs=[pl.BlockSpec(memory_space=pltpu.VMEM)] * len(shapes),
        scratch_shapes=[pltpu.VMEM(*s) for s in scratch],
        compiler_params=pltpu.CompilerParams(vmem_limit_bytes=limit * 2**20),
        cost_estimate=pl.CostEstimate(
            flops=int(SCALE * micros * 1e9), bytes_accessed=int(SCALE * micros * 3e6), transcendentals=0
        ),
        name=name,
    )(*args, *after)


def on_device(
    block_input,
    cotangent,
    lengths,
    in_proj,
    out_proj,
    up_proj,
    down_proj,
    first_gain,
    second_gain,
    short_filter,
    skip_bias,
    filter_in,
    filter_in_bias,
    filter_mid,
    filter_mid_bias,
    filter_out,
):
    seq_size = lax.axis_size("seq")
    fold = seq_size // CUBE
    member = lax.axis_index("seq") // fold
    ring_place = lax.axis_index("pos")
    rows, width = block_input.shape
    channels = width // RING
    lane = width // CUBE
    hidden = up_proj.shape[1]
    seq_len = LSEQ
    members = [[i * fold + o for i in range(CUBE)] for o in range(fold)]
    bundles = [list(range(i * fold, (i + 1) * fold)) for i in range(CUBE)]

    def hop(value, bit):
        pairs = [(i, ((i // fold) ^ bit) * fold + i % fold) for i in range(seq_size)]
        return lax.ppermute(value, "seq", pairs)

    def ring(value, shift):
        return lax.ppermute(value, "pos", [(i, (i + shift) % RING) for i in range(RING)])

    def near_ring(value, bit):
        return lax.ppermute(value, "pos", [(i, i ^ bit) for i in range(RING)])

    def to_rows(value):
        return lax.all_to_all(value, "pos", 0, 0, tiled=True)

    def swap(value):
        return lax.all_to_all(value, "seq", 0, 0, axis_index_groups=members, tiled=True)

    def gather(value):
        return lax.all_gather(value, "seq", axis=0, axis_index_groups=members, tiled=True)

    def scatter(value):
        return lax.psum_scatter(value, "seq", scatter_dimension=0, axis_index_groups=members, tiled=True)

    def settle(value, axis):
        if fold == 1:
            return value
        return lax.psum_scatter(
            value, "seq", scatter_dimension=axis, axis_index_groups=bundles, tiled=True
        )

    def widen(value, axis):
        if fold == 1:
            return value
        return lax.all_gather(value, "seq", axis=axis, axis_index_groups=bundles, tiled=True)

    info = jnp.stack([member % 2, member, ring_place, lengths[0]]).astype(jnp.int32)
    waiting = []
    latest = []

    def now(*values):
        waiting.extend(values)
        return values

    def step(kernel, outs, *args, **options):
        after = [v for v in latest + waiting if not any(v is a for a in args)]
        results = run(kernel, outs, *args, after=after, **options)
        waiting.clear()
        latest[:] = results[:1]
        return results

    def phase(*values, after=()):
        after = [v for v in latest + waiting + list(after) if not any(v is a for a in values)]
        waiting.clear()
        count = len(values) + len(after)
        mark, *passed = pl.pallas_call(
            functools.partial(tick_kernel, count),
            out_shape=[jax.ShapeDtypeStruct((8, 128), f32)]
            + [jax.ShapeDtypeStruct(v.shape, v.dtype) for v in values],
            in_specs=[pl.BlockSpec(memory_space=pl.ANY)] * count,
            out_specs=[pl.BlockSpec(memory_space=pltpu.VMEM)]
            + [pl.BlockSpec(memory_space=pl.ANY)] * len(values),
            input_output_aliases={i: i + 1 for i in range(len(values))},
            compiler_params=pltpu.CompilerParams(vmem_limit_bytes=62 * 2**20),
            name="phase",
        )(*values, *after)
        latest[:] = [mark]
        return passed

    gain_one, gain_two = first_gain, second_gain
    in_turned = widen(in_proj.transpose(1, 0, 2), 1)
    out_shard, up_shard, down_shard = widen(out_proj, 1), widen(up_proj, 0), widen(down_proj, 1)
    out_shards = [out_shard] + [ring(out_shard, -j) for j in range(1, RING)]
    normed, inputs, cot = step(
        rows_kernel, [((rows, width), bf16)] * 3, block_input, cotangent, gain_one, name="rows", micros=0.2
    )
    normed_slots = [normed, ring(normed, -1)]
    in_rows, layer_rows, out_rows = step(
        weights_kernel,
        [((3 * channels, lane), bf16), ((2 * hidden, lane), bf16), ((width, lane), bf16)],
        in_turned, up_shard, down_shard, *out_shards,
        name="weights", micros=0.2,
    )
    in_all = gather(in_rows)
    out_all = gather(out_rows)
    layer_got = swap(layer_rows)

    channel_start = ring_place * channels
    features, times = (jnp.asarray(v) for v in embedding(seq_len))
    last_layer = lax.dynamic_slice_in_dim(filter_out, channel_start, channels, 1)
    tables, turns = spectral_tables(seq_len)
    tables = [jnp.asarray(t) for t in tables]
    turns = jnp.asarray(turns)
    lags = lax.dynamic_slice_in_dim(
        short_filter.reshape(3, 3, width), channel_start, channels, 2
    ).reshape(3, 3 * channels)
    skip = lax.dynamic_slice_in_dim(skip_bias, channel_start, channels, 0)[None]
    pair = ((2, seq_len, channels), f32)
    inner = filter_mid.shape[0]

    def with_width(kernel):
        return lambda info, *refs: kernel(info, width, *refs)

    (filter_hidden,) = step(
        hidden_kernel,
        [((seq_len, 4 * inner), f32)],
        features, filter_in, filter_in_bias[None], filter_mid, filter_mid_bias[None],
        name="hidden", micros=5,
    )
    (normed_slots[1],) = phase(normed_slots[1], after=[layer_got])
    normed_slots.append(ring(normed_slots[1], -1))
    (layer_own,) = step(
        side_by_side, [((2 * hidden // CUBE + SPARE, width), bf16)], layer_got, name="layer_own", micros=0.2
    )
    (normed_slots[2],) = phase(normed_slots[2], after=[lags, skip])
    normed_slots.append(ring(normed_slots[2], -1))
    (spectrum,) = step(
        with_width(taps_kernel),
        [pair],
        info, filter_hidden, times, last_layer, turns, *tables,
        name="taps", micros=5,
    )
    layer_own, cot = phase(layer_own, cot, after=[normed_slots[3]])
    layer_slots = [layer_own, ring(layer_own, -1)]
    cot_all = gather(cot)

    projected, long_conv, driven_spectrum, gated, in_full = step(
        conv_kernel,
        [
            ((seq_len, 3 * channels), bf16),
            ((seq_len, channels), f32),
            pair,
            ((seq_len, channels), bf16),
            ((3 * channels, width), bf16),
        ],
        info, *normed_slots, in_all, lags, skip, spectrum, *tables,
        name="conv", micros=14,
    )
    gated, layer_slots[1] = phase(gated, layer_slots[1])
    gated = to_rows(gated)
    layer_slots = phase(*layer_slots, after=[gated, out_all])
    layer_slots += [ring(layer_slots[1], -1), ring(layer_slots[0], 1)]
    residual, second = step(
        out_kernel,
        [((rows, width), f32), ((rows, width), bf16)],
        info, gated, out_all, inputs, gain_two,
        name="out", micros=0.2,
    )

    second_sib, across, along = (hop(second, bit) for bit in (1, 2, 4))
    half = rows // 2
    across, along = phase(across, along, after=[second_sib, *layer_slots[2:]])
    top, low = hop(along[:half], 2), hop(across[half:], 4)
    across_sib, along_sib, top_sib, low_sib = (hop(v, 1) for v in (across, along, top, low))
    wide = CUBE * rows // 2
    out_kept, out_given, back_kept, back_given, layer_grads = step(
        layer_kernel,
        [((wide, width), bf16)] * 4 + [((hidden, width), bf16)],
        info, second, second_sib, across, across_sib, along, along_sib, top, low, top_sib, low_sib,
        cot_all, *layer_slots,
        scratch=[((hidden // 2, width), f32)] * 2,
        name="layer", micros=22,
    )
    back_given, out_given, layer_grads = phase(back_given, out_given, layer_grads)
    layer_grads = lax.psum_scatter(layer_grads, "pos", scatter_dimension=0, tiled=True)

    block, part = ((rows, width), bf16), ((half, width), bf16)
    shares = [
        step(share_kernel, [block] * 3 + [part] * 2, kept, hop(given, 1), name="share", micros=0.1)
        for kept, given in ((back_kept, back_given), (out_kept, out_given))
    ]

    def turn(own, across, along, top, low):
        across, along = step(
            turn_kernel, [block] * 2, across, along, hop(top, 2), hop(low, 4), name="turn", micros=0.1
        )
        return own, hop(across, 2), hop(along, 4)

    back_parts = turn(*shares[0])
    grad_res, branch, second_gain_grad, grad_gated = step(
        branch_kernel,
        [((rows, width), f32), ((rows, width), bf16), ((1, width), f32), ((seq_len, channels), bf16)],
        info, *back_parts, residual, gain_two, cot, out_all,
        name="branch", micros=0.2,
    )
    (grad_gated,) = phase(grad_gated, after=[layer_grads])
    grad_gated = to_rows(grad_gated)
    (out_grad,) = step(
        out_grad_kernel, [((CUBE * width, lane), bf16)], gated, branch, name="out_grad", micros=0.1
    )
    out_parts = turn(*shares[1])
    out_grad = scatter(out_grad)
    (layer_sums,) = step(below_kernel, [((2 * hidden, lane), bf16)], layer_grads, name="layer_sum", micros=0.1)

    grad_projected, grad_taps, small = step(
        back_kernel,
        [((seq_len, 3 * channels), bf16), ((seq_len, channels), f32), ((16, channels), f32)],
        info, grad_gated, projected, long_conv, driven_spectrum, lags, skip, spectrum, turns, *tables,
        name="back", micros=15,
    )
    (packed,) = step(
        with_width(pack_kernel),
        [((PACKED, channels), f32)],
        info, grad_taps, filter_hidden, features, times, filter_mid, last_layer, small, second_gain_grad,
        name="pack", micros=0.1,
    )
    partial, packed = step(
        normed_kernel,
        [((seq_len, width), bf16), ((PACKED, channels), f32)],
        info, grad_projected, in_full, *normed_slots, gain_one, packed,
        name="normed", micros=0.2,
    )
    partial, packed, layer_sums = phase(partial, packed, layer_sums, after=[out_grad])
    grad_normed = lax.psum_scatter(partial, "pos", scatter_dimension=0, tiled=True)
    layer_sums = swap(layer_sums)
    if fold > 1:
        packed = lax.psum(packed, "seq", axis_index_groups=bundles)
    (in_grad,) = step(
        in_grad_kernel,
        [((3 * CUBE * channels, lane), bf16)],
        info, grad_projected, *normed_slots,
        name="in_grad", micros=0.1,
    )
    for bit in (1, 2, 4):
        packed = packed + hop(packed, bit)
    in_grad, packed, out_grad = phase(in_grad, packed, out_grad, after=[layer_sums, *out_parts[1:]])
    in_grad = swap(in_grad)
    out_slots = [
        lax.dynamic_slice_in_dim(out_grad, (ring_place + j) % RING * channels, channels) for j in range(RING)
    ]
    out_slots = [out_slots[0]] + [ring(out_slots[j], j) for j in range(1, RING)]
    packed = packed.astype(bf16)
    packed_slots = [packed, near_ring(packed, 1)]
    packed_slots += [near_ring(v, 2) for v in packed_slots]
    up_grad, down_grad = step(
        layer_end_kernel, [((lane, hidden), f32), ((hidden, lane), f32)], layer_sums, name="layer_end"
    )
    (block_output,) = step(
        finish_kernel, [((rows, width), bf16)], residual, *out_parts, name="finish", micros=0.1
    )
    (input_grad,) = step(
        end_kernel, [((rows, width), bf16)], grad_normed, inputs, gain_one, grad_res, name="end", micros=1
    )
    (out_grad,) = step(out_end_kernel, [((channels, lane), f32)], *out_slots, name="out_end")
    (in_grad,) = step(in_end_kernel, [((3, lane, channels), f32)], in_grad, name="in_end")
    small_grads = step(
        unpack_kernel,
        [
            ((1, width), f32),
            ((1, width), f32),
            ((3, 3 * width), f32),
            ((1, width), f32),
            ((EMB, inner), f32),
            ((1, inner), f32),
            ((inner, inner), f32),
            ((1, inner), f32),
            ((inner, width), f32),
        ],
        info, *packed_slots,
        scratch=[((RING, PACKED, channels), f32)],
        name="unpack",
    )
    return (
        block_output,
        input_grad,
        settle(in_grad, 1).transpose(1, 0, 2),
        settle(out_grad, 1),
        settle(up_grad, 0),
        settle(down_grad, 1),
        small_grads[0].reshape(width),
        small_grads[1].reshape(width),
        small_grads[2],
        small_grads[3].reshape(width),
        small_grads[4],
        small_grads[5].reshape(inner),
        small_grads[6],
        small_grads[7].reshape(inner),
        small_grads[8],
    )


def solution(mesh):
    rows = P(("seq", "pos"), None)
    in_place, down_place, up_place = P("seq", None, "pos"), P("pos", "seq"), P("seq", "pos")
    return jax.shard_map(
        on_device,
        mesh=mesh,
        in_specs=(rows, rows, P("seq"), in_place, down_place, up_place, down_place) + (P(),) * 9,
        out_specs=(rows, rows, in_place, down_place, up_place, down_place) + (P(),) * 9,
        check_vma=False,
    )
```

```python
import functools
import math

import jax
import jax.numpy as jnp
import ml_dtypes
import numpy as np
from jax import lax
from jax.experimental import pallas as pl
from jax.experimental.pallas import tpu as pltpu
from jax.sharding import PartitionSpec as P

EMB = 33
LSEQ = 1024
RING = 4
CUBE = 8
PLANE = 4
SCALE = 1.0
GRANT = 65280 * 1024

epsilon = 1e-05
highest = lax.Precision.HIGHEST
f32 = jnp.float32
bf16 = jnp.bfloat16

OWNED = 80
GAINS = 8
SHARED = 64
PACKED = OWNED + GAINS + SHARED

SPARE = 16


def nt_dot(left, right):
    return lax.dot_general(left, right, (((1,), (1,)), ((), ())), preferred_element_type=f32)


def tn_dot(left, right):
    return lax.dot_general(left, right, (((0,), (0,)), ((), ())), preferred_element_type=f32)


def nn_dot(left, right):
    return jnp.dot(left, right, preferred_element_type=f32)


def full_dot(left, right, dims=((1,), (0,))):
    return lax.dot_general(left, right, (dims, ((), ())), precision=highest, preferred_element_type=f32)


def embedding(seq_len):
    positions = np.concatenate([np.arange(0, seq_len, 2), np.arange(1, seq_len, 2)])
    timeline = positions / (seq_len - 1)
    band_count = (EMB - 1) // 2
    bands = np.linspace(0.0001, band_count - 1, band_count)
    phases = (2.0 * math.pi / seq_len * positions)[:, None] * bands[None, :]
    features = np.concatenate([timeline[:, None], np.cos(phases), -np.sin(phases)], 1)
    return features.astype(np.float32), timeline.astype(np.float32)[:, None]


def spectral_tables(length):
    half = length // 2
    freq = 2 * np.arange(half) + 1
    tables = []
    for offset in (1, 3):
        angle = (freq[:, None] * (4 * np.arange(half) + offset)[None, :]) % (8 * length)
        angle = angle * (math.pi / (4 * length))
        tables.append(np.concatenate([np.cos(angle), np.sin(angle)]))
    tables += [tables[0].T / length, tables[1].T / length]
    split = []
    for table in tables:
        top = table.astype(ml_dtypes.bfloat16)
        split += [top, (table - top.astype(np.float64)).astype(ml_dtypes.bfloat16)]
    order = np.concatenate([np.arange(half), length - 1 - np.arange(half)])
    turn = (2.0 * order + 1.0) * (math.pi / (4 * length))
    turns = np.stack([np.cos(turn), np.sin(turn)]).astype(np.float32)[:, :, None]
    return split, turns


def split_dot(table_top, table_low, value):
    top = value.astype(bf16)
    low = (value - top.astype(f32)).astype(bf16)
    return nn_dot(table_top, top) + nn_dot(table_top, low) + nn_dot(table_low, top)


def transform(tables, even, odd):
    half = even.shape[0]
    even_sums = split_dot(tables[0][...], tables[1][...], even)
    odd_sums = split_dot(tables[2][...], tables[3][...], odd)
    even_cos, even_sin = even_sums[:half], even_sums[half:]
    odd_cos, odd_sin = odd_sums[:half], odd_sums[half:]
    real = jnp.concatenate([even_cos + odd_cos, even_sin - odd_sin], 0)
    imag = jnp.concatenate([-(even_sin + odd_sin), odd_cos - even_cos], 0)
    return real, imag


def restore(tables, real, imag):
    half = real.shape[0] // 2
    real_low, real_up, imag_low, imag_up = real[:half], real[half:], imag[:half], imag[half:]
    even = jnp.concatenate([real_low - imag_up, real_up - imag_low], 0)
    odd = jnp.concatenate([real_low + imag_up, -(real_up + imag_low)], 0)
    return (
        split_dot(tables[4][...], tables[5][...], even),
        split_dot(tables[6][...], tables[7][...], odd),
    )


def later(value):
    row = lax.broadcasted_iota(jnp.int32, value.shape, 0)
    return jnp.where(row == 0, 0.0, pltpu.roll(value, 1, 0))


def sooner(value):
    row = lax.broadcasted_iota(jnp.int32, value.shape, 0)
    last = value.shape[0] - 1
    return jnp.where(row == last, 0.0, pltpu.roll(value, last, 0))


def mix_streams(even, odd, lags):
    mixed_even = lags[0] * even + lags[1] * later(odd) + lags[2] * later(even)
    mixed_odd = lags[0] * odd + lags[1] * even + lags[2] * later(odd)
    return mixed_even, mixed_odd


def valid_rows(length, half, offset):
    place = 2 * lax.broadcasted_iota(jnp.int32, (half, 1), 0) + offset
    return jnp.where(place < length, 1.0, 0.0)


def row_order(rows, dtype):
    left = lax.broadcasted_iota(jnp.int32, (rows, rows), 0)
    right = lax.broadcasted_iota(jnp.int32, (rows, rows), 1)
    half = rows // 2
    source = jnp.where(left < half, 2 * left, 2 * (left - half) + 1)
    return jnp.where(right == source, 1.0, 0.0).astype(dtype)


def standardize(values):
    centred = values - jnp.mean(values, axis=-1, keepdims=True)
    scaling = lax.rsqrt(jnp.mean(centred * centred, axis=-1, keepdims=True) + epsilon)
    return centred * scaling, scaling


def scale_back(unit, scaling, weighted):
    return scaling * (
        weighted
        - jnp.mean(weighted, axis=-1, keepdims=True)
        - unit * jnp.mean(weighted * unit, axis=-1, keepdims=True)
    )


def piece(place, size):
    return pl.ds(pl.multiple_of(place * size, size), size)


def rows_kernel(rows_in, cot_in, gains, normed, inputs, cot):
    order = row_order(rows_in.shape[0], bf16)
    inputs[...] = nn_dot(order, rows_in[...]).astype(bf16)
    cot[...] = nn_dot(order, cot_in[...]).astype(bf16)
    unit, _ = standardize(inputs[...].astype(f32))
    normed[...] = (unit * gains[...]).astype(bf16)


def weights_kernel(in_w, up_w, down_w, in_rows, layer_rows):
    streams, channels = in_w.shape[0], in_w.shape[2]
    for k in range(streams):
        in_rows[pl.ds(k * channels, channels), :] = in_w[k].T
    turned = up_w[...].T
    part = turned.shape[0] // CUBE
    for m in range(CUBE):
        layer_rows[pl.ds(2 * m * part, part), :] = turned[m * part : (m + 1) * part]
        layer_rows[pl.ds((2 * m + 1) * part, part), :] = down_w[pl.ds(m * part, part), :]


def stack_kernel(o0, o1, o2, o3, out_rows):
    count = o0.shape[0]
    for j, slot in enumerate((o0, o1, o2, o3)):
        out_rows[pl.ds(j * count, count), :] = slot[...]


def side_by_side(ref, out):
    count, lane = ref.shape[0] // CUBE, ref.shape[1]
    for m in range(CUBE):
        out[pl.ds(0, count), pl.ds(m * lane, lane)] = ref[pl.ds(m * count, count), :]
    if out.shape[0] > count:
        out[pl.ds(count, out.shape[0] - count), :] = jnp.zeros((out.shape[0] - count, out.shape[1]), out.dtype)


def decay_of(info, times, channels, width):
    lanes = lax.broadcasted_iota(jnp.int32, (1, channels), 1) + info[2] * channels
    slowest = math.log(0.01) / 1.5
    fastest = math.log(0.01) / 0.3
    rates = jnp.abs(slowest + (fastest - slowest) * lanes.astype(f32) / (width - 1))
    return jnp.exp(-times[...] * rates)


def pair_dot(left, right):
    half = left.shape[0] // 2
    return jnp.concatenate([full_dot(left[:half], right), full_dot(left[half:], right)], 1)


def unpair(value):
    lanes = value.shape[1] // 2
    return jnp.concatenate([value[:, :lanes], value[:, lanes:]], 0)


def hidden_kernel(features, first, bias_one, middle, bias_two, hidden):
    inner = middle.shape[0]
    twice = lambda ref: jnp.concatenate([ref[...], ref[...]], 1)
    angle = pair_dot(features[...], first[...]) + twice(bias_one)
    one = unpair(jnp.sin(angle))
    hidden[:, pl.ds(0, inner)] = one
    hidden[:, pl.ds(inner, inner)] = unpair(jnp.cos(angle))
    angle = pair_dot(one, middle[...]) + twice(bias_two)
    hidden[:, pl.ds(2 * inner, inner)] = unpair(jnp.sin(angle))
    hidden[:, pl.ds(3 * inner, inner)] = unpair(jnp.cos(angle))


def taps_kernel(info, width, hidden, times, last, turns, *refs):
    tables, (spectrum,) = refs[:8], refs[8:]
    half = hidden.shape[0] // 2
    inner = last.shape[0]
    taps = full_dot(hidden[:, pl.ds(2 * inner, inner)], last[...]) * decay_of(info, times, last.shape[1], width)
    real, imag = transform(tables, taps[:half], taps[half:])
    spectrum[0] = real * turns[0] - imag * turns[1]
    spectrum[1] = real * turns[1] + imag * turns[0]


def ring_blocks(info, count):
    return [piece((info[2] + j) & (RING - 1), count) for j in range(RING)]


def conv_kernel(info, *refs):
    slots, (in_all, lags, skip, spectrum), refs = refs[:4], refs[4:8], refs[8:]
    tables = refs[:8]
    projected, long_conv, driven_spectrum, gated, in_full = refs[8:]
    length = info[3]
    half_rows = slots[0].shape[0] // 2
    half = projected.shape[0] // 2
    channels = skip.shape[1]
    side_by_side(in_all, in_full)
    for j, slot in enumerate(slots):
        total = nt_dot(slot[...], in_full[...]).astype(bf16)
        block = (info[2] + j) & (RING - 1)
        projected[piece(block, half_rows), :] = total[:half_rows]
        projected[pl.ds(pl.multiple_of(half + block * half_rows, half_rows), half_rows), :] = total[half_rows:]
    streams = []
    for k in range(3):
        lanes = pl.ds(k * channels, channels)
        streams.append(
            mix_streams(
                projected[pl.ds(0, half), lanes].astype(f32),
                projected[pl.ds(half, half), lanes].astype(f32),
                [lags[pl.ds(i, 1), lanes] for i in range(3)],
            )
        )
    (outer_even, outer_odd), (inner_even, inner_odd), (value_even, value_odd) = streams
    even = value_even * inner_even * valid_rows(length, half, 0)
    odd = value_odd * inner_odd * valid_rows(length, half, 1)
    real, imag = transform(tables, even, odd)
    driven_spectrum[0] = real
    driven_spectrum[1] = imag
    taps_real, taps_imag = spectrum[0], spectrum[1]
    back_even, back_odd = restore(
        tables, real * taps_real - imag * taps_imag, real * taps_imag + imag * taps_real
    )
    back_even += skip[...] * even
    back_odd += skip[...] * odd
    long_conv[pl.ds(0, half), :] = back_even
    long_conv[pl.ds(half, half), :] = back_odd
    even, odd = (back_even * outer_even).astype(bf16), (back_odd * outer_odd).astype(bf16)
    for z in range(RING):
        here = slice(z * half_rows, (z + 1) * half_rows)
        gated[pl.ds(2 * z * half_rows, half_rows), :] = even[here]
        gated[pl.ds((2 * z + 1) * half_rows, half_rows), :] = odd[here]


def out_kernel(info, gated, out_all, inputs, gains, residual, second):
    rows, width = inputs.shape
    lane = out_all.shape[1]
    wide = jnp.concatenate([gated[block, :] for block in ring_blocks(info, rows)], 1)
    for m in range(CUBE):
        lanes = pl.ds(m * lane, lane)
        residual[:, lanes] = inputs[:, lanes].astype(f32) + nn_dot(wide, out_all[pl.ds(m * width, width), :])
    unit, _ = standardize(residual[...])
    second[...] = (unit * gains[...]).astype(bf16)


def layer_kernel(info, *refs):
    rows_in, (cot_all, *slots), refs = refs[:10], refs[10:15], refs[15:]
    out_kept, out_given, back_kept, back_given, grads, up_sum, down_sum = refs
    own, sib, across, across_sib, along, along_sib, top, low, top_sib, low_sib = rows_in
    rows = own.shape[0]
    part = (slots[0].shape[0] - SPARE) // 2
    ups = jnp.concatenate([slot[pl.ds(0, part), :] for slot in slots], 0)
    downs = jnp.concatenate([slot[pl.ds(part, part), :] for slot in slots], 0)
    chips = ((own, sib), (across, across_sib), (along, along_sib), (top, low, top_sib, low_sib))
    for r, parts in enumerate(chips):
        second = jnp.concatenate([ref[...] for ref in parts], 0)
        cot = jnp.concatenate([cot_all[piece(info[1] ^ (2 * r + i), rows), :] for i in range(2)], 0)
        pre_act = nt_dot(second, ups)
        grad_act = nt_dot(cot, downs)
        lower = 0.5 * (1.0 + lax.erf(pre_act * math.sqrt(0.5)))
        density = jnp.exp(-0.5 * pre_act * pre_act) * (1.0 / math.sqrt(2.0 * math.pi))
        activated = (pre_act * lower).astype(bf16)
        grad_pre = (grad_act * (lower + pre_act * density)).astype(bf16)
        here = pl.ds(r * rows, rows)
        out = nn_dot(activated, downs)
        out_kept[here, :] = out[:rows].astype(bf16)
        out_given[here, :] = out[rows:].astype(bf16)
        back = nn_dot(grad_pre, ups)
        back_kept[here, :] = back[:rows].astype(bf16)
        back_given[here, :] = back[rows:].astype(bf16)
        up_grad = tn_dot(grad_pre, second)
        down_grad = tn_dot(activated, cot)
        up_sum[...] = up_grad if r == 0 else up_sum[...] + up_grad
        down_sum[...] = down_grad if r == 0 else down_sum[...] + down_grad
    for j, block in enumerate(ring_blocks(info, 2 * part)):
        here = pl.ds(j * part, part)
        both = jnp.concatenate([up_sum[here, :], down_sum[here, :]], 0)
        grads[block, :] = both.astype(bf16)


def share_kernel(kept, got, own, across, along, top, low):
    rows = own.shape[0]
    for r, ref in enumerate((own, across, along)):
        here = pl.ds(r * rows, rows)
        ref[...] = (kept[here, :].astype(f32) + got[here, :].astype(f32)).astype(bf16)
    for i, ref in enumerate((top, low)):
        here = pl.ds(3 * rows + i * rows // 2, rows // 2)
        ref[...] = (kept[here, :].astype(f32) + got[here, :].astype(f32)).astype(bf16)


def turn_kernel(across, along, top, low, across_sum, along_sum):
    half = top.shape[0]
    first, second = pl.ds(0, half), pl.ds(half, half)
    across_sum[first, :] = across[first, :]
    across_sum[second, :] = (across[second, :].astype(f32) + low[...].astype(f32)).astype(bf16)
    along_sum[first, :] = (along[first, :].astype(f32) + top[...].astype(f32)).astype(bf16)
    along_sum[second, :] = along[second, :]


def branch_kernel(
    info, own, across, along, residual, gains, cot, out_all, grad_res, branch, gain_grad, grad_gated
):
    rows, width = residual.shape
    lane = out_all.shape[1]
    channels = grad_gated.shape[1]
    back = own[...].astype(f32) + across[...].astype(f32) + along[...].astype(f32)
    unit, scaling = standardize(residual[...])
    gain_grad[...] = jnp.sum(back * unit, axis=0, keepdims=True)
    total = cot[...].astype(f32) + scale_back(unit, scaling, back * gains[...])
    grad_res[...] = total
    branch[...] = total.astype(bf16)
    total = None
    for m in range(CUBE):
        part = nt_dot(branch[:, pl.ds(m * lane, lane)], out_all[pl.ds(m * width, width), :])
        total = part if m == 0 else total + part
    total = total.astype(bf16)
    for j, block in enumerate(ring_blocks(info, rows)):
        grad_gated[block, :] = total[:, j * channels : (j + 1) * channels]


def finish_kernel(residual, own, across, along, block_output):
    total = own[...].astype(f32) + across[...].astype(f32) + along[...].astype(f32)
    total = (residual[...] + total).astype(bf16)
    block_output[...] = tn_dot(row_order(total.shape[0], bf16), total).astype(bf16)


def below(total, out):
    count, lane = total.shape[0], total.shape[1] // CUBE
    for m in range(CUBE):
        out[pl.ds(m * count, count), :] = total[:, m * lane : (m + 1) * lane].astype(out.dtype)


def below_kernel(total, out):
    below(total[...], out)


def out_grad_kernel(gated, branch, out_grad):
    rows = branch.shape[0]
    parts = [tn_dot(gated[pl.ds(z * rows, rows), :], branch[...]) for z in range(RING)]
    below(jnp.concatenate(parts, 0).astype(bf16), out_grad)


def back_kernel(
    info, grad_gated, projected, long_conv, driven_spectrum, lags, skip, spectrum, turns, *refs
):
    tables = refs[:8]
    grad_projected, grad_taps, small = refs[8:]
    length = info[3]
    channels = grad_gated.shape[1]
    half = projected.shape[0] // 2
    half_rows = half // RING
    plain, mixed = [], []
    for k in range(3):
        lanes = pl.ds(k * channels, channels)
        even = projected[pl.ds(0, half), lanes].astype(f32)
        odd = projected[pl.ds(half, half), lanes].astype(f32)
        plain.append((even, odd))
        mixed.append(mix_streams(even, odd, [lags[pl.ds(i, 1), lanes] for i in range(3)]))
    (outer_even, outer_odd), (inner_even, inner_odd), (value_even, value_odd) = mixed
    valid_even, valid_odd = valid_rows(length, half, 0), valid_rows(length, half, 1)
    gated_even, gated_odd = (
        jnp.concatenate([grad_gated[pl.ds((2 * z + i) * half_rows, half_rows), :] for z in range(RING)], 0).astype(f32)
        for i in range(2)
    )
    conv_even, conv_odd = gated_even * outer_even, gated_odd * outer_odd
    real, imag = transform(tables, conv_even, conv_odd)
    taps_real, taps_imag = spectrum[0], spectrum[1]
    driven_even, driven_odd = restore(
        tables, real * taps_real + imag * taps_imag, imag * taps_real - real * taps_imag
    )
    driven_even = (driven_even + skip[...] * conv_even) * valid_even
    driven_odd = (driven_odd + skip[...] * conv_odd) * valid_odd
    small[pl.ds(9, 1), :] = jnp.sum(
        conv_even * value_even * inner_even * valid_even + conv_odd * value_odd * inner_odd * valid_odd,
        axis=0,
        keepdims=True,
    )
    small[pl.ds(10, 6), :] = jnp.zeros((6, channels), f32)
    grads = (
        (gated_even * long_conv[pl.ds(0, half), :], gated_odd * long_conv[pl.ds(half, half), :]),
        (driven_even * value_even, driven_odd * value_odd),
        (driven_even * inner_even, driven_odd * inner_odd),
    )
    for k, (even, odd) in enumerate(grads):
        lanes = pl.ds(k * channels, channels)
        lag = [lags[pl.ds(i, 1), lanes] for i in range(3)]
        plain_even, plain_odd = plain[k]
        sums = (
            even * plain_even + odd * plain_odd,
            even * later(plain_odd) + odd * plain_even,
            even * later(plain_even) + odd * later(plain_odd),
        )
        for i in range(3):
            small[pl.ds(3 * i + k, 1), :] = jnp.sum(sums[i], axis=0, keepdims=True)
        next_even, next_odd = sooner(even), sooner(odd)
        stream_even = (lag[0] * even + lag[1] * odd + lag[2] * next_even).astype(bf16)
        stream_odd = (lag[0] * odd + lag[1] * next_even + lag[2] * next_odd).astype(bf16)
        for z in range(RING):
            here = slice(z * half_rows, (z + 1) * half_rows)
            grad_projected[pl.ds(2 * z * half_rows, half_rows), lanes] = stream_even[here]
            grad_projected[pl.ds((2 * z + 1) * half_rows, half_rows), lanes] = stream_odd[here]
    base_real, base_imag = driven_spectrum[0], driven_spectrum[1]
    cross_real = real * base_real + imag * base_imag
    cross_imag = imag * base_real - real * base_imag
    taps_even, taps_odd = restore(
        tables,
        cross_real * turns[0] + cross_imag * turns[1],
        cross_imag * turns[0] - cross_real * turns[1],
    )
    grad_taps[pl.ds(0, half), :] = taps_even
    grad_taps[pl.ds(half, half), :] = taps_odd


def normed_kernel(info, grad_projected, in_full, n0, n1, n2, n3, gains, small, partial, packed):
    rows = n0.shape[0]
    total_gain = None
    for j, (slot, block) in enumerate(zip((n0, n1, n2, n3), ring_blocks(info, rows))):
        total = nn_dot(grad_projected[block, :], in_full[...])
        partial[block, :] = total.astype(bf16)
        part = jnp.sum(total * slot[...].astype(f32), axis=0, keepdims=True)
        total_gain = part if j == 0 else total_gain + part
    total_gain = total_gain / gains[...]
    packed[...] = small[...]
    span = packed.shape[1]
    for r in range(PLANE):
        packed[pl.ds(OWNED + r, 1), :] = total_gain[:, r * span : (r + 1) * span]


def in_grad_kernel(info, grad_projected, n0, n1, n2, n3, in_grad):
    normed = jnp.concatenate([n0[...], n1[...], n2[...], n3[...]], 0)
    grad = jnp.concatenate([grad_projected[block, :] for block in ring_blocks(info, n0.shape[0])], 0)
    below(tn_dot(grad, normed).astype(bf16), in_grad)


def end_kernel(grad_normed, inputs, gains, grad_res, input_grad):
    grad = grad_normed[...].astype(f32)
    unit, scaling = standardize(inputs[...].astype(f32))
    total = (grad_res[...] + scale_back(unit, scaling, grad * gains[...])).astype(bf16)
    input_grad[...] = tn_dot(row_order(total.shape[0], bf16), total).astype(bf16)


def layer_end_kernel(parts, up_grad, down_grad):
    part = parts.shape[0] // CUBE // 2
    for m in range(CUBE):
        here = pl.ds(m * part, part)
        up_grad[:, here] = parts[pl.ds(2 * m * part, part), :].astype(f32).T
        down_grad[here, :] = parts[pl.ds((2 * m + 1) * part, part), :].astype(f32)


def out_end_kernel(own, p1, p2, p3, total):
    total[...] = own[...].astype(f32) + p1[...].astype(f32) + p2[...].astype(f32) + p3[...].astype(f32)


def in_end_kernel(parts, in_grad):
    channels = in_grad.shape[2]
    rows = parts.shape[0] // CUBE
    for k in range(in_grad.shape[0]):
        total = None
        for m in range(CUBE):
            part = parts[pl.ds(m * rows + k * channels, channels), :].astype(f32)
            total = part if m == 0 else total + part
        in_grad[k] = total.T


def pack_kernel(
    info, width, grad_taps, hidden, features, times, middle, last, small, gain_two, packed
):
    inner = middle.shape[0]
    span = packed.shape[1]
    one, slope_one, two, slope_two = (hidden[:, pl.ds(i * inner, inner)] for i in range(4))
    grad_raw = grad_taps[...] * decay_of(info, times, span, width)
    rows = ((0,), (0,))
    packed[pl.ds(0, inner), :] = full_dot(two, grad_raw, rows)
    grad_two = full_dot(grad_raw, last[...], ((1,), (1,))) * slope_two
    grad_one = full_dot(grad_two, middle[...], ((1,), (1,))) * slope_one
    packed[pl.ds(64, 16), :] = small[...]
    for r in range(PLANE):
        lanes = pl.ds(r * span, span)
        packed[pl.ds(OWNED + r, 1), :] = jnp.zeros((1, span), f32)
        packed[pl.ds(OWNED + PLANE + r, 1), :] = gain_two[:, lanes]
    start = OWNED + GAINS
    packed[pl.ds(start, SHARED), :] = jnp.zeros((SHARED, span), f32)
    packed[pl.ds(start, inner), pl.ds(0, inner)] = full_dot(one, grad_two, rows)
    packed[pl.ds(start, EMB), pl.ds(inner, inner)] = full_dot(features[...], grad_one, rows)
    packed[pl.ds(start, 1), pl.ds(2 * inner, inner)] = jnp.sum(grad_one, axis=0, keepdims=True)
    packed[pl.ds(start, 1), pl.ds(3 * inner, inner)] = jnp.sum(grad_two, axis=0, keepdims=True)


def unpack_kernel(
    info, s0, s1, s2, s3, gain_one, gain_two, short, skip, first, bias_one, middle, bias_two, last, slots
):
    place = info[2]
    for j, ref in enumerate((s0, s1, s2, s3)):
        slots[place ^ j] = ref[...].astype(f32)
    channels = s0.shape[1]
    inner = middle.shape[0]
    for z in range(RING):
        lanes = pl.ds(z * channels, channels)
        last[:, lanes] = slots[z, pl.ds(0, 64), :]
        for i in range(3):
            for k in range(3):
                here = pl.ds((k * RING + z) * channels, channels)
                short[pl.ds(i, 1), here] = slots[z, pl.ds(64 + 3 * i + k, 1), :]
        skip[:, lanes] = slots[z, pl.ds(64 + 9, 1), :]
    count = GAINS + SHARED
    total = slots[0, pl.ds(OWNED, count), :] + slots[1, pl.ds(OWNED, count), :]
    total += slots[2, pl.ds(OWNED, count), :] + slots[3, pl.ds(OWNED, count), :]
    for b in range(PLANE):
        lanes = pl.ds(b * channels, channels)
        gain_one[:, lanes] = total[b : b + 1]
        gain_two[:, lanes] = total[PLANE + b : PLANE + b + 1]
    total = total[GAINS:]
    middle[...] = total[:, :inner]
    first[...] = total[:EMB, inner : 2 * inner]
    bias_one[...] = total[:1, 2 * inner : 3 * inner]
    bias_two[...] = total[:1, 3 * inner :]


def tick_kernel(count, *refs):
    refs[count][...] = jnp.zeros_like(refs[count])


def run(kernel, outs, *args, scratch=(), name, micros=2.0, after=()):
    place = lambda a: pltpu.SMEM if a.dtype == jnp.int32 else pltpu.VMEM
    shapes = [jax.ShapeDtypeStruct(*o) for o in outs]
    count = len(args)

    def body(*refs):
        kernel(*refs[:count], *refs[count + len(after) :])

    return pl.pallas_call(
        body,
        out_shape=shapes,
        in_specs=[pl.BlockSpec(memory_space=place(a)) for a in args]
        + [pl.BlockSpec(memory_space=pl.ANY) for _ in after],
        out_specs=[pl.BlockSpec(memory_space=pltpu.VMEM)] * len(shapes),
        scratch_shapes=[pltpu.VMEM(*s) for s in scratch],
        compiler_params=pltpu.CompilerParams(vmem_limit_bytes=GRANT),
        cost_estimate=pl.CostEstimate(
            flops=int(SCALE * micros * 1e9), bytes_accessed=int(SCALE * micros * 3e6), transcendentals=0
        ),
        name=name,
    )(*args, *after)


def on_device(
    block_input,
    cotangent,
    lengths,
    in_proj,
    out_proj,
    up_proj,
    down_proj,
    first_gain,
    second_gain,
    short_filter,
    skip_bias,
    filter_in,
    filter_in_bias,
    filter_mid,
    filter_mid_bias,
    filter_out,
):
    seq_size = lax.axis_size("seq")
    fold = seq_size // CUBE
    member = lax.axis_index("seq") // fold
    ring_place = lax.axis_index("pos")
    rows, width = block_input.shape
    channels = width // RING
    lane = width // CUBE
    hidden = up_proj.shape[1]
    seq_len = LSEQ
    members = [[i * fold + o for i in range(CUBE)] for o in range(fold)]
    bundles = [list(range(i * fold, (i + 1) * fold)) for i in range(CUBE)]

    def hop(value, bit):
        pairs = [(i, ((i // fold) ^ bit) * fold + i % fold) for i in range(seq_size)]
        return lax.ppermute(value, "seq", pairs)

    def ring(value, shift):
        return lax.ppermute(value, "pos", [(i, (i + shift) % RING) for i in range(RING)])

    def near_ring(value, bit):
        return lax.ppermute(value, "pos", [(i, i ^ bit) for i in range(RING)])

    def to_rows(value):
        return lax.all_to_all(value, "pos", 0, 0, tiled=True)

    def swap(value):
        return lax.all_to_all(value, "seq", 0, 0, axis_index_groups=members, tiled=True)

    def gather(value):
        return lax.all_gather(value, "seq", axis=0, axis_index_groups=members, tiled=True)

    def scatter(value):
        return lax.psum_scatter(value, "seq", scatter_dimension=0, axis_index_groups=members, tiled=True)

    def settle(value, axis):
        if fold == 1:
            return value
        return lax.psum_scatter(
            value, "seq", scatter_dimension=axis, axis_index_groups=bundles, tiled=True
        )

    def widen(value, axis):
        if fold == 1:
            return value
        return lax.all_gather(value, "seq", axis=axis, axis_index_groups=bundles, tiled=True)

    info = jnp.stack([member % 2, member, ring_place, lengths[0]]).astype(jnp.int32)
    waiting = []
    latest = []

    def now(*values):
        waiting.extend(values)
        return values

    def step(kernel, outs, *args, **options):
        after = [v for v in latest + waiting if not any(v is a for a in args)]
        results = run(kernel, outs, *args, after=after, **options)
        waiting.clear()
        latest[:] = results[:1]
        return results

    def phase(*values, after=()):
        after = [v for v in latest + waiting + list(after) if not any(v is a for a in values)]
        waiting.clear()
        count = len(values) + len(after)
        mark, *passed = pl.pallas_call(
            functools.partial(tick_kernel, count),
            out_shape=[jax.ShapeDtypeStruct((8, 128), f32)]
            + [jax.ShapeDtypeStruct(v.shape, v.dtype) for v in values],
            in_specs=[pl.BlockSpec(memory_space=pl.ANY)] * count,
            out_specs=[pl.BlockSpec(memory_space=pltpu.VMEM)]
            + [pl.BlockSpec(memory_space=pl.ANY)] * len(values),
            input_output_aliases={i: i + 1 for i in range(len(values))},
            compiler_params=pltpu.CompilerParams(vmem_limit_bytes=GRANT),
            name="phase",
        )(*values, *after)
        latest[:] = [mark]
        return passed

    gain_one, gain_two = first_gain, second_gain
    in_turned = widen(in_proj.transpose(1, 0, 2), 1)
    out_shard, up_shard, down_shard = widen(out_proj, 1), widen(up_proj, 0), widen(down_proj, 1)
    out_shards = [out_shard] + [ring(out_shard, -j) for j in range(1, RING)]
    in_rows, layer_rows = step(
        weights_kernel,
        [((3 * channels, lane), bf16), ((2 * hidden, lane), bf16)],
        in_turned, up_shard, down_shard,
        name="weights", micros=0.2,
    )
    in_all = gather(in_rows)
    layer_got = swap(layer_rows)
    normed, inputs, cot = step(
        rows_kernel, [((rows, width), bf16)] * 3, block_input, cotangent, gain_one, name="rows", micros=0.2
    )
    normed_slots = [normed, ring(normed, -1)]

    channel_start = ring_place * channels
    features, times = (jnp.asarray(v) for v in embedding(seq_len))
    last_layer = lax.dynamic_slice_in_dim(filter_out, channel_start, channels, 1)
    tables, turns = spectral_tables(seq_len)
    tables = [jnp.asarray(t) for t in tables]
    turns = jnp.asarray(turns)
    lags = lax.dynamic_slice_in_dim(
        short_filter.reshape(3, 3, width), channel_start, channels, 2
    ).reshape(3, 3 * channels)
    skip = lax.dynamic_slice_in_dim(skip_bias, channel_start, channels, 0)[None]
    pair = ((2, seq_len, channels), f32)
    inner = filter_mid.shape[0]

    def with_width(kernel):
        return lambda info, *refs: kernel(info, width, *refs)

    (filter_hidden,) = step(
        hidden_kernel,
        [((seq_len, 4 * inner), f32)],
        features, filter_in, filter_in_bias[None], filter_mid, filter_mid_bias[None],
        name="hidden", micros=5,
    )
    (normed_slots[1],) = phase(normed_slots[1], after=[layer_got])
    normed_slots.append(ring(normed_slots[1], -1))
    (out_rows,) = step(stack_kernel, [((width, lane), bf16)], *out_shards, name="stack", micros=0.1)
    out_all = gather(out_rows)
    (layer_own,) = step(
        side_by_side, [((2 * hidden // CUBE + SPARE, width), bf16)], layer_got, name="layer_own", micros=0.2
    )
    (normed_slots[2],) = phase(normed_slots[2], after=[lags, skip])
    normed_slots.append(ring(normed_slots[2], -1))
    (spectrum,) = step(
        with_width(taps_kernel),
        [pair],
        info, filter_hidden, times, last_layer, turns, *tables,
        name="taps", micros=5,
    )
    layer_own, cot = phase(layer_own, cot, after=[normed_slots[3]])
    layer_slots = [layer_own, ring(layer_own, -1)]
    cot_all = gather(cot)

    projected, long_conv, driven_spectrum, gated, in_full = step(
        conv_kernel,
        [
            ((seq_len, 3 * channels), bf16),
            ((seq_len, channels), f32),
            pair,
            ((seq_len, channels), bf16),
            ((3 * channels, width), bf16),
        ],
        info, *normed_slots, in_all, lags, skip, spectrum, *tables,
        name="conv", micros=14,
    )
    gated, layer_slots[1] = phase(gated, layer_slots[1])
    gated = to_rows(gated)
    layer_slots = phase(*layer_slots, after=[gated, out_all])
    layer_slots += [ring(layer_slots[1], -1), ring(layer_slots[0], 1)]
    residual, second = step(
        out_kernel,
        [((rows, width), f32), ((rows, width), bf16)],
        info, gated, out_all, inputs, gain_two,
        name="out", micros=0.2,
    )

    second_sib, across, along = (hop(second, bit) for bit in (1, 2, 4))
    half = rows // 2
    across, along = phase(across, along, after=[second_sib, *layer_slots[2:]])
    top, low = hop(along[:half], 2), hop(across[half:], 4)
    across_sib, along_sib, top_sib, low_sib = (hop(v, 1) for v in (across, along, top, low))
    wide = CUBE * rows // 2
    out_kept, out_given, back_kept, back_given, layer_grads = step(
        layer_kernel,
        [((wide, width), bf16)] * 4 + [((hidden, width), bf16)],
        info, second, second_sib, across, across_sib, along, along_sib, top, low, top_sib, low_sib,
        cot_all, *layer_slots,
        scratch=[((hidden // 2, width), f32)] * 2,
        name="layer", micros=22,
    )
    back_given, out_given, layer_grads = phase(back_given, out_given, layer_grads)
    layer_grads = lax.psum_scatter(layer_grads, "pos", scatter_dimension=0, tiled=True)

    block, part = ((rows, width), bf16), ((half, width), bf16)
    shares = [
        step(share_kernel, [block] * 3 + [part] * 2, kept, hop(given, 1), name="share", micros=0.1)
        for kept, given in ((back_kept, back_given), (out_kept, out_given))
    ]

    def turn(own, across, along, top, low):
        across, along = step(
            turn_kernel, [block] * 2, across, along, hop(top, 2), hop(low, 4), name="turn", micros=0.1
        )
        return own, hop(across, 2), hop(along, 4)

    back_parts = turn(*shares[0])
    grad_res, branch, second_gain_grad, grad_gated = step(
        branch_kernel,
        [((rows, width), f32), ((rows, width), bf16), ((1, width), f32), ((seq_len, channels), bf16)],
        info, *back_parts, residual, gain_two, cot, out_all,
        name="branch", micros=0.2,
    )
    (grad_gated,) = phase(grad_gated, after=[layer_grads])
    grad_gated = to_rows(grad_gated)
    (out_grad,) = step(
        out_grad_kernel, [((CUBE * width, lane), bf16)], gated, branch, name="out_grad", micros=0.1
    )
    out_parts = turn(*shares[1])
    out_grad = scatter(out_grad)
    (layer_sums,) = step(below_kernel, [((2 * hidden, lane), bf16)], layer_grads, name="layer_sum", micros=0.1)

    grad_projected, grad_taps, small = step(
        back_kernel,
        [((seq_len, 3 * channels), bf16), ((seq_len, channels), f32), ((16, channels), f32)],
        info, grad_gated, projected, long_conv, driven_spectrum, lags, skip, spectrum, turns, *tables,
        name="back", micros=15,
    )
    (packed,) = step(
        with_width(pack_kernel),
        [((PACKED, channels), f32)],
        info, grad_taps, filter_hidden, features, times, filter_mid, last_layer, small, second_gain_grad,
        name="pack", micros=0.1,
    )
    partial, packed = step(
        normed_kernel,
        [((seq_len, width), bf16), ((PACKED, channels), f32)],
        info, grad_projected, in_full, *normed_slots, gain_one, packed,
        name="normed", micros=0.2,
    )
    partial, packed, layer_sums = phase(partial, packed, layer_sums, after=[out_grad])
    grad_normed = lax.psum_scatter(partial, "pos", scatter_dimension=0, tiled=True)
    layer_sums = swap(layer_sums)
    if fold > 1:
        packed = lax.psum(packed, "seq", axis_index_groups=bundles)
    (in_grad,) = step(
        in_grad_kernel,
        [((3 * CUBE * channels, lane), bf16)],
        info, grad_projected, *normed_slots,
        name="in_grad", micros=0.1,
    )
    for bit in (1, 2, 4):
        packed = packed + hop(packed, bit)
    in_grad, packed, out_grad = phase(in_grad, packed, out_grad, after=[layer_sums, *out_parts[1:]])
    in_grad = swap(in_grad)
    out_slots = [
        lax.dynamic_slice_in_dim(out_grad, (ring_place + j) % RING * channels, channels) for j in range(RING)
    ]
    out_slots = [out_slots[0]] + [ring(out_slots[j], j) for j in range(1, RING)]
    packed = packed.astype(bf16)
    packed_slots = [packed, near_ring(packed, 1)]
    packed_slots += [near_ring(v, 2) for v in packed_slots]
    up_grad, down_grad = step(
        layer_end_kernel, [((lane, hidden), f32), ((hidden, lane), f32)], layer_sums, name="layer_end"
    )
    (block_output,) = step(
        finish_kernel, [((rows, width), bf16)], residual, *out_parts, name="finish", micros=0.1
    )
    (input_grad,) = step(
        end_kernel, [((rows, width), bf16)], grad_normed, inputs, gain_one, grad_res, name="end", micros=1
    )
    (out_grad,) = step(out_end_kernel, [((channels, lane), f32)], *out_slots, name="out_end")
    (in_grad,) = step(in_end_kernel, [((3, lane, channels), f32)], in_grad, name="in_end")
    small_grads = step(
        unpack_kernel,
        [
            ((1, width), f32),
            ((1, width), f32),
            ((3, 3 * width), f32),
            ((1, width), f32),
            ((EMB, inner), f32),
            ((1, inner), f32),
            ((inner, inner), f32),
            ((1, inner), f32),
            ((inner, width), f32),
        ],
        info, *packed_slots,
        scratch=[((RING, PACKED, channels), f32)],
        name="unpack",
    )
    return (
        block_output,
        input_grad,
        settle(in_grad, 1).transpose(1, 0, 2),
        settle(out_grad, 1),
        settle(up_grad, 0),
        settle(down_grad, 1),
        small_grads[0].reshape(width),
        small_grads[1].reshape(width),
        small_grads[2],
        small_grads[3].reshape(width),
        small_grads[4],
        small_grads[5].reshape(inner),
        small_grads[6],
        small_grads[7].reshape(inner),
        small_grads[8],
    )


def solution(mesh):
    rows = P(("seq", "pos"), None)
    in_place, down_place, up_place = P("seq", None, "pos"), P("pos", "seq"), P("seq", "pos")
    return jax.shard_map(
        on_device,
        mesh=mesh,
        in_specs=(rows, rows, P("seq"), in_place, down_place, up_place, down_place) + (P(),) * 9,
        out_specs=(rows, rows, in_place, down_place, up_place, down_place) + (P(),) * 9,
        check_vma=False,
    )
```

```python
import functools
import math

import jax
import jax.numpy as jnp
import ml_dtypes
import numpy as np
from jax import lax
from jax.experimental import pallas as pl
from jax.experimental.pallas import tpu as pltpu
from jax.sharding import PartitionSpec as P

EMB = 33
LSEQ = 1024
RING = 4
CUBE = 8
PLANE = 4
SCALE = 1.0
GRANT = 65280 * 1024

epsilon = 1e-05
highest = lax.Precision.HIGHEST
f32 = jnp.float32
bf16 = jnp.bfloat16

OWNED = 80
GAINS = 8
SHARED = 64
PACKED = OWNED + GAINS + SHARED

SPARE = 16


def nt_dot(left, right):
    return lax.dot_general(left, right, (((1,), (1,)), ((), ())), preferred_element_type=f32)


def tn_dot(left, right):
    return lax.dot_general(left, right, (((0,), (0,)), ((), ())), preferred_element_type=f32)


def nn_dot(left, right):
    return jnp.dot(left, right, preferred_element_type=f32)


def full_dot(left, right, dims=((1,), (0,))):
    return lax.dot_general(left, right, (dims, ((), ())), precision=highest, preferred_element_type=f32)


def embedding(seq_len):
    positions = np.concatenate([np.arange(0, seq_len, 2), np.arange(1, seq_len, 2)])
    timeline = positions / (seq_len - 1)
    band_count = (EMB - 1) // 2
    bands = np.linspace(0.0001, band_count - 1, band_count)
    phases = (2.0 * math.pi / seq_len * positions)[:, None] * bands[None, :]
    features = np.concatenate([timeline[:, None], np.cos(phases), -np.sin(phases)], 1)
    return features.astype(np.float32), timeline.astype(np.float32)[:, None]


def spectral_tables(length):
    half = length // 2
    freq = 2 * np.arange(half) + 1
    tables = []
    for offset in (1, 3):
        angle = (freq[:, None] * (4 * np.arange(half) + offset)[None, :]) % (8 * length)
        angle = angle * (math.pi / (4 * length))
        tables.append(np.concatenate([np.cos(angle), np.sin(angle)]))
    tables += [tables[0].T / length, tables[1].T / length]
    split = []
    for table in tables:
        top = table.astype(ml_dtypes.bfloat16)
        split += [top, (table - top.astype(np.float64)).astype(ml_dtypes.bfloat16)]
    order = np.concatenate([np.arange(half), length - 1 - np.arange(half)])
    turn = (2.0 * order + 1.0) * (math.pi / (4 * length))
    turns = np.stack([np.cos(turn), np.sin(turn)]).astype(np.float32)[:, :, None]
    return split, turns


def split_dot(table_top, table_low, value):
    top = value.astype(bf16)
    low = (value - top.astype(f32)).astype(bf16)
    return nn_dot(table_top, top) + nn_dot(table_top, low) + nn_dot(table_low, top)


def transform(tables, even, odd):
    half = even.shape[0]
    even_sums = split_dot(tables[0][...], tables[1][...], even)
    odd_sums = split_dot(tables[2][...], tables[3][...], odd)
    even_cos, even_sin = even_sums[:half], even_sums[half:]
    odd_cos, odd_sin = odd_sums[:half], odd_sums[half:]
    real = jnp.concatenate([even_cos + odd_cos, even_sin - odd_sin], 0)
    imag = jnp.concatenate([-(even_sin + odd_sin), odd_cos - even_cos], 0)
    return real, imag


def restore(tables, real, imag):
    half = real.shape[0] // 2
    real_low, real_up, imag_low, imag_up = real[:half], real[half:], imag[:half], imag[half:]
    even = jnp.concatenate([real_low - imag_up, real_up - imag_low], 0)
    odd = jnp.concatenate([real_low + imag_up, -(real_up + imag_low)], 0)
    return (
        split_dot(tables[4][...], tables[5][...], even),
        split_dot(tables[6][...], tables[7][...], odd),
    )


def later(value):
    row = lax.broadcasted_iota(jnp.int32, value.shape, 0)
    return jnp.where(row == 0, 0.0, pltpu.roll(value, 1, 0))


def sooner(value):
    row = lax.broadcasted_iota(jnp.int32, value.shape, 0)
    last = value.shape[0] - 1
    return jnp.where(row == last, 0.0, pltpu.roll(value, last, 0))


def mix_streams(even, odd, lags):
    mixed_even = lags[0] * even + lags[1] * later(odd) + lags[2] * later(even)
    mixed_odd = lags[0] * odd + lags[1] * even + lags[2] * later(odd)
    return mixed_even, mixed_odd


def valid_rows(length, half, offset):
    place = 2 * lax.broadcasted_iota(jnp.int32, (half, 1), 0) + offset
    return jnp.where(place < length, 1.0, 0.0)


def row_order(rows, dtype):
    left = lax.broadcasted_iota(jnp.int32, (rows, rows), 0)
    right = lax.broadcasted_iota(jnp.int32, (rows, rows), 1)
    half = rows // 2
    source = jnp.where(left < half, 2 * left, 2 * (left - half) + 1)
    return jnp.where(right == source, 1.0, 0.0).astype(dtype)


def standardize(values):
    centred = values - jnp.mean(values, axis=-1, keepdims=True)
    scaling = lax.rsqrt(jnp.mean(centred * centred, axis=-1, keepdims=True) + epsilon)
    return centred * scaling, scaling


def scale_back(unit, scaling, weighted):
    return scaling * (
        weighted
        - jnp.mean(weighted, axis=-1, keepdims=True)
        - unit * jnp.mean(weighted * unit, axis=-1, keepdims=True)
    )


def piece(place, size):
    return pl.ds(pl.multiple_of(place * size, size), size)


def rows_kernel(rows_in, cot_in, gains, normed, inputs, cot):
    order = row_order(rows_in.shape[0], bf16)
    inputs[...] = nn_dot(order, rows_in[...]).astype(bf16)
    cot[...] = nn_dot(order, cot_in[...]).astype(bf16)
    unit, _ = standardize(inputs[...].astype(f32))
    normed[...] = (unit * gains[...]).astype(bf16)


def weights_kernel(in_w, up_w, down_w, in_rows, layer_rows):
    streams, channels = in_w.shape[0], in_w.shape[2]
    for k in range(streams):
        in_rows[pl.ds(k * channels, channels), :] = in_w[k].T
    turned = up_w[...].T
    part = turned.shape[0] // CUBE
    for m in range(CUBE):
        layer_rows[pl.ds(2 * m * part, part), :] = turned[m * part : (m + 1) * part]
        layer_rows[pl.ds((2 * m + 1) * part, part), :] = down_w[pl.ds(m * part, part), :]


def stack_kernel(o0, o1, o2, o3, out_rows):
    count = o0.shape[0]
    for j, slot in enumerate((o0, o1, o2, o3)):
        out_rows[pl.ds(j * count, count), :] = slot[...]


def side_by_side(ref, out):
    count, lane = ref.shape[0] // CUBE, ref.shape[1]
    for m in range(CUBE):
        out[pl.ds(0, count), pl.ds(m * lane, lane)] = ref[pl.ds(m * count, count), :]
    if out.shape[0] > count:
        out[pl.ds(count, out.shape[0] - count), :] = jnp.zeros((out.shape[0] - count, out.shape[1]), out.dtype)


def decay_of(info, times, channels, width):
    lanes = lax.broadcasted_iota(jnp.int32, (1, channels), 1) + info[2] * channels
    slowest = math.log(0.01) / 1.5
    fastest = math.log(0.01) / 0.3
    rates = jnp.abs(slowest + (fastest - slowest) * lanes.astype(f32) / (width - 1))
    return jnp.exp(-times[...] * rates)


def pair_dot(left, right):
    half = left.shape[0] // 2
    return jnp.concatenate([full_dot(left[:half], right), full_dot(left[half:], right)], 1)


def unpair(value):
    lanes = value.shape[1] // 2
    return jnp.concatenate([value[:, :lanes], value[:, lanes:]], 0)


def hidden_kernel(features, first, bias_one, middle, bias_two, hidden):
    inner = middle.shape[0]
    twice = lambda ref: jnp.concatenate([ref[...], ref[...]], 1)
    angle = pair_dot(features[...], first[...]) + twice(bias_one)
    one = unpair(jnp.sin(angle))
    hidden[:, pl.ds(0, inner)] = one
    hidden[:, pl.ds(inner, inner)] = unpair(jnp.cos(angle))
    angle = pair_dot(one, middle[...]) + twice(bias_two)
    hidden[:, pl.ds(2 * inner, inner)] = unpair(jnp.sin(angle))
    hidden[:, pl.ds(3 * inner, inner)] = unpair(jnp.cos(angle))


def taps_kernel(info, width, hidden, times, last, turns, *refs):
    tables, (spectrum,) = refs[:8], refs[8:]
    half = hidden.shape[0] // 2
    inner = last.shape[0]
    taps = full_dot(hidden[:, pl.ds(2 * inner, inner)], last[...]) * decay_of(info, times, last.shape[1], width)
    real, imag = transform(tables, taps[:half], taps[half:])
    spectrum[0] = real * turns[0] - imag * turns[1]
    spectrum[1] = real * turns[1] + imag * turns[0]


def ring_blocks(info, count):
    return [piece((info[2] + j) & (RING - 1), count) for j in range(RING)]


def conv_kernel(info, *refs):
    slots, (in_all, lags, skip, spectrum), refs = refs[:4], refs[4:8], refs[8:]
    tables = refs[:8]
    projected, long_conv, driven_spectrum, gated, in_full = refs[8:]
    length = info[3]
    half_rows = slots[0].shape[0] // 2
    half = projected.shape[0] // 2
    channels = skip.shape[1]
    side_by_side(in_all, in_full)
    for j, slot in enumerate(slots):
        total = nt_dot(slot[...], in_full[...]).astype(bf16)
        block = (info[2] + j) & (RING - 1)
        projected[piece(block, half_rows), :] = total[:half_rows]
        projected[pl.ds(pl.multiple_of(half + block * half_rows, half_rows), half_rows), :] = total[half_rows:]
    streams = []
    for k in range(3):
        lanes = pl.ds(k * channels, channels)
        streams.append(
            mix_streams(
                projected[pl.ds(0, half), lanes].astype(f32),
                projected[pl.ds(half, half), lanes].astype(f32),
                [lags[pl.ds(i, 1), lanes] for i in range(3)],
            )
        )
    (outer_even, outer_odd), (inner_even, inner_odd), (value_even, value_odd) = streams
    even = value_even * inner_even * valid_rows(length, half, 0)
    odd = value_odd * inner_odd * valid_rows(length, half, 1)
    real, imag = transform(tables, even, odd)
    driven_spectrum[0] = real
    driven_spectrum[1] = imag
    taps_real, taps_imag = spectrum[0], spectrum[1]
    back_even, back_odd = restore(
        tables, real * taps_real - imag * taps_imag, real * taps_imag + imag * taps_real
    )
    back_even += skip[...] * even
    back_odd += skip[...] * odd
    long_conv[pl.ds(0, half), :] = back_even
    long_conv[pl.ds(half, half), :] = back_odd
    even, odd = (back_even * outer_even).astype(bf16), (back_odd * outer_odd).astype(bf16)
    for z in range(RING):
        here = slice(z * half_rows, (z + 1) * half_rows)
        gated[pl.ds(2 * z * half_rows, half_rows), :] = even[here]
        gated[pl.ds((2 * z + 1) * half_rows, half_rows), :] = odd[here]


def out_kernel(info, gated, out_all, inputs, gains, residual, second):
    rows, width = inputs.shape
    lane = out_all.shape[1]
    wide = jnp.concatenate([gated[block, :] for block in ring_blocks(info, rows)], 1)
    for m in range(CUBE):
        lanes = pl.ds(m * lane, lane)
        residual[:, lanes] = inputs[:, lanes].astype(f32) + nn_dot(wide, out_all[pl.ds(m * width, width), :])
    unit, _ = standardize(residual[...])
    second[...] = (unit * gains[...]).astype(bf16)


def halves_kernel(across, along, top, low):
    half = top.shape[0]
    top[...] = along[pl.ds(0, half), :]
    low[...] = across[pl.ds(half, half), :]


def layer_kernel(info, *refs):
    rows_in, (cot_all, *slots), refs = refs[:10], refs[10:15], refs[15:]
    out_kept, out_given, back_kept, back_given, grads, up_sum, down_sum = refs
    own, sib, across, across_sib, along, along_sib, top, low, top_sib, low_sib = rows_in
    rows = own.shape[0]
    part = (slots[0].shape[0] - SPARE) // 2
    ups = jnp.concatenate([slot[pl.ds(0, part), :] for slot in slots], 0)
    downs = jnp.concatenate([slot[pl.ds(part, part), :] for slot in slots], 0)
    chips = ((own, sib), (across, across_sib), (along, along_sib), (top, low, top_sib, low_sib))
    for r, parts in enumerate(chips):
        second = jnp.concatenate([ref[...] for ref in parts], 0)
        cot = jnp.concatenate([cot_all[piece(info[1] ^ (2 * r + i), rows), :] for i in range(2)], 0)
        pre_act = nt_dot(second, ups)
        grad_act = nt_dot(cot, downs)
        lower = 0.5 * (1.0 + lax.erf(pre_act * math.sqrt(0.5)))
        density = jnp.exp(-0.5 * pre_act * pre_act) * (1.0 / math.sqrt(2.0 * math.pi))
        activated = (pre_act * lower).astype(bf16)
        grad_pre = (grad_act * (lower + pre_act * density)).astype(bf16)
        here = pl.ds(r * rows, rows)
        out = nn_dot(activated, downs)
        out_kept[here, :] = out[:rows].astype(bf16)
        out_given[here, :] = out[rows:].astype(bf16)
        back = nn_dot(grad_pre, ups)
        back_kept[here, :] = back[:rows].astype(bf16)
        back_given[here, :] = back[rows:].astype(bf16)
        up_grad = tn_dot(grad_pre, second)
        down_grad = tn_dot(activated, cot)
        up_sum[...] = up_grad if r == 0 else up_sum[...] + up_grad
        down_sum[...] = down_grad if r == 0 else down_sum[...] + down_grad
    for j, block in enumerate(ring_blocks(info, 2 * part)):
        here = pl.ds(j * part, part)
        both = jnp.concatenate([up_sum[here, :], down_sum[here, :]], 0)
        grads[block, :] = both.astype(bf16)


def share_kernel(kept, got, own, across, along, top, low):
    rows = own.shape[0]
    for r, ref in enumerate((own, across, along)):
        here = pl.ds(r * rows, rows)
        ref[...] = (kept[here, :].astype(f32) + got[here, :].astype(f32)).astype(bf16)
    for i, ref in enumerate((top, low)):
        here = pl.ds(3 * rows + i * rows // 2, rows // 2)
        ref[...] = (kept[here, :].astype(f32) + got[here, :].astype(f32)).astype(bf16)


def turn_kernel(across, along, top, low, across_sum, along_sum):
    half = top.shape[0]
    first, second = pl.ds(0, half), pl.ds(half, half)
    across_sum[first, :] = across[first, :]
    across_sum[second, :] = (across[second, :].astype(f32) + low[...].astype(f32)).astype(bf16)
    along_sum[first, :] = (along[first, :].astype(f32) + top[...].astype(f32)).astype(bf16)
    along_sum[second, :] = along[second, :]


def branch_kernel(
    info, own, across, along, residual, gains, cot, out_all, grad_res, branch, gain_grad, grad_gated
):
    rows, width = residual.shape
    lane = out_all.shape[1]
    channels = grad_gated.shape[1]
    back = own[...].astype(f32) + across[...].astype(f32) + along[...].astype(f32)
    unit, scaling = standardize(residual[...])
    gain_grad[...] = jnp.sum(back * unit, axis=0, keepdims=True)
    total = cot[...].astype(f32) + scale_back(unit, scaling, back * gains[...])
    grad_res[...] = total
    branch[...] = total.astype(bf16)
    total = None
    for m in range(CUBE):
        part = nt_dot(branch[:, pl.ds(m * lane, lane)], out_all[pl.ds(m * width, width), :])
        total = part if m == 0 else total + part
    total = total.astype(bf16)
    for j, block in enumerate(ring_blocks(info, rows)):
        grad_gated[block, :] = total[:, j * channels : (j + 1) * channels]


def finish_kernel(residual, own, across, along, block_output):
    total = own[...].astype(f32) + across[...].astype(f32) + along[...].astype(f32)
    total = (residual[...] + total).astype(bf16)
    block_output[...] = tn_dot(row_order(total.shape[0], bf16), total).astype(bf16)


def below(total, out):
    count, lane = total.shape[0], total.shape[1] // CUBE
    for m in range(CUBE):
        out[pl.ds(m * count, count), :] = total[:, m * lane : (m + 1) * lane].astype(out.dtype)


def below_kernel(total, out):
    below(total[...], out)


def out_grad_kernel(gated, branch, out_grad):
    rows = branch.shape[0]
    parts = [tn_dot(gated[pl.ds(z * rows, rows), :], branch[...]) for z in range(RING)]
    below(jnp.concatenate(parts, 0).astype(bf16), out_grad)


def back_kernel(
    info, grad_gated, projected, long_conv, driven_spectrum, lags, skip, spectrum, turns, *refs
):
    tables = refs[:8]
    grad_projected, grad_taps, small = refs[8:]
    length = info[3]
    channels = grad_gated.shape[1]
    half = projected.shape[0] // 2
    half_rows = half // RING
    plain, mixed = [], []
    for k in range(3):
        lanes = pl.ds(k * channels, channels)
        even = projected[pl.ds(0, half), lanes].astype(f32)
        odd = projected[pl.ds(half, half), lanes].astype(f32)
        plain.append((even, odd))
        mixed.append(mix_streams(even, odd, [lags[pl.ds(i, 1), lanes] for i in range(3)]))
    (outer_even, outer_odd), (inner_even, inner_odd), (value_even, value_odd) = mixed
    valid_even, valid_odd = valid_rows(length, half, 0), valid_rows(length, half, 1)
    gated_even, gated_odd = (
        jnp.concatenate([grad_gated[pl.ds((2 * z + i) * half_rows, half_rows), :] for z in range(RING)], 0).astype(f32)
        for i in range(2)
    )
    conv_even, conv_odd = gated_even * outer_even, gated_odd * outer_odd
    real, imag = transform(tables, conv_even, conv_odd)
    taps_real, taps_imag = spectrum[0], spectrum[1]
    driven_even, driven_odd = restore(
        tables, real * taps_real + imag * taps_imag, imag * taps_real - real * taps_imag
    )
    driven_even = (driven_even + skip[...] * conv_even) * valid_even
    driven_odd = (driven_odd + skip[...] * conv_odd) * valid_odd
    small[pl.ds(9, 1), :] = jnp.sum(
        conv_even * value_even * inner_even * valid_even + conv_odd * value_odd * inner_odd * valid_odd,
        axis=0,
        keepdims=True,
    )
    small[pl.ds(10, 6), :] = jnp.zeros((6, channels), f32)
    grads = (
        (gated_even * long_conv[pl.ds(0, half), :], gated_odd * long_conv[pl.ds(half, half), :]),
        (driven_even * value_even, driven_odd * value_odd),
        (driven_even * inner_even, driven_odd * inner_odd),
    )
    for k, (even, odd) in enumerate(grads):
        lanes = pl.ds(k * channels, channels)
        lag = [lags[pl.ds(i, 1), lanes] for i in range(3)]
        plain_even, plain_odd = plain[k]
        sums = (
            even * plain_even + odd * plain_odd,
            even * later(plain_odd) + odd * plain_even,
            even * later(plain_even) + odd * later(plain_odd),
        )
        for i in range(3):
            small[pl.ds(3 * i + k, 1), :] = jnp.sum(sums[i], axis=0, keepdims=True)
        next_even, next_odd = sooner(even), sooner(odd)
        stream_even = (lag[0] * even + lag[1] * odd + lag[2] * next_even).astype(bf16)
        stream_odd = (lag[0] * odd + lag[1] * next_even + lag[2] * next_odd).astype(bf16)
        for z in range(RING):
            here = slice(z * half_rows, (z + 1) * half_rows)
            grad_projected[pl.ds(2 * z * half_rows, half_rows), lanes] = stream_even[here]
            grad_projected[pl.ds((2 * z + 1) * half_rows, half_rows), lanes] = stream_odd[here]
    base_real, base_imag = driven_spectrum[0], driven_spectrum[1]
    cross_real = real * base_real + imag * base_imag
    cross_imag = imag * base_real - real * base_imag
    taps_even, taps_odd = restore(
        tables,
        cross_real * turns[0] + cross_imag * turns[1],
        cross_imag * turns[0] - cross_real * turns[1],
    )
    grad_taps[pl.ds(0, half), :] = taps_even
    grad_taps[pl.ds(half, half), :] = taps_odd


def normed_kernel(info, grad_projected, in_full, n0, n1, n2, n3, gains, small, partial, packed):
    rows = n0.shape[0]
    total_gain = None
    for j, (slot, block) in enumerate(zip((n0, n1, n2, n3), ring_blocks(info, rows))):
        total = nn_dot(grad_projected[block, :], in_full[...])
        partial[block, :] = total.astype(bf16)
        part = jnp.sum(total * slot[...].astype(f32), axis=0, keepdims=True)
        total_gain = part if j == 0 else total_gain + part
    total_gain = total_gain / gains[...]
    packed[...] = small[...]
    span = packed.shape[1]
    for r in range(PLANE):
        packed[pl.ds(OWNED + r, 1), :] = total_gain[:, r * span : (r + 1) * span]


def in_grad_kernel(info, grad_projected, n0, n1, n2, n3, in_grad):
    normed = jnp.concatenate([n0[...], n1[...], n2[...], n3[...]], 0)
    grad = jnp.concatenate([grad_projected[block, :] for block in ring_blocks(info, n0.shape[0])], 0)
    below(tn_dot(grad, normed).astype(bf16), in_grad)


def end_kernel(grad_normed, inputs, gains, grad_res, input_grad):
    grad = grad_normed[...].astype(f32)
    unit, scaling = standardize(inputs[...].astype(f32))
    total = (grad_res[...] + scale_back(unit, scaling, grad * gains[...])).astype(bf16)
    input_grad[...] = tn_dot(row_order(total.shape[0], bf16), total).astype(bf16)


def layer_end_kernel(parts, up_grad, down_grad):
    part = parts.shape[0] // CUBE // 2
    for m in range(CUBE):
        here = pl.ds(m * part, part)
        up_grad[:, here] = parts[pl.ds(2 * m * part, part), :].astype(f32).T
        down_grad[here, :] = parts[pl.ds((2 * m + 1) * part, part), :].astype(f32)


def out_end_kernel(own, p1, p2, p3, total):
    total[...] = own[...].astype(f32) + p1[...].astype(f32) + p2[...].astype(f32) + p3[...].astype(f32)


def in_end_kernel(parts, in_grad):
    channels = in_grad.shape[2]
    rows = parts.shape[0] // CUBE
    for k in range(in_grad.shape[0]):
        total = None
        for m in range(CUBE):
            part = parts[pl.ds(m * rows + k * channels, channels), :].astype(f32)
            total = part if m == 0 else total + part
        in_grad[k] = total.T


def pack_kernel(
    info, width, grad_taps, hidden, features, times, middle, last, small, gain_two, packed
):
    inner = middle.shape[0]
    span = packed.shape[1]
    one, slope_one, two, slope_two = (hidden[:, pl.ds(i * inner, inner)] for i in range(4))
    grad_raw = grad_taps[...] * decay_of(info, times, span, width)
    rows = ((0,), (0,))
    packed[pl.ds(0, inner), :] = full_dot(two, grad_raw, rows)
    grad_two = full_dot(grad_raw, last[...], ((1,), (1,))) * slope_two
    grad_one = full_dot(grad_two, middle[...], ((1,), (1,))) * slope_one
    packed[pl.ds(64, 16), :] = small[...]
    for r in range(PLANE):
        lanes = pl.ds(r * span, span)
        packed[pl.ds(OWNED + r, 1), :] = jnp.zeros((1, span), f32)
        packed[pl.ds(OWNED + PLANE + r, 1), :] = gain_two[:, lanes]
    start = OWNED + GAINS
    packed[pl.ds(start, SHARED), :] = jnp.zeros((SHARED, span), f32)
    packed[pl.ds(start, inner), pl.ds(0, inner)] = full_dot(one, grad_two, rows)
    packed[pl.ds(start, EMB), pl.ds(inner, inner)] = full_dot(features[...], grad_one, rows)
    packed[pl.ds(start, 1), pl.ds(2 * inner, inner)] = jnp.sum(grad_one, axis=0, keepdims=True)
    packed[pl.ds(start, 1), pl.ds(3 * inner, inner)] = jnp.sum(grad_two, axis=0, keepdims=True)


def unpack_kernel(
    info, s0, s1, s2, s3, gain_one, gain_two, short, skip, first, bias_one, middle, bias_two, last, slots
):
    place = info[2]
    for j, ref in enumerate((s0, s1, s2, s3)):
        slots[place ^ j] = ref[...].astype(f32)
    channels = s0.shape[1]
    inner = middle.shape[0]
    for z in range(RING):
        lanes = pl.ds(z * channels, channels)
        last[:, lanes] = slots[z, pl.ds(0, 64), :]
        for i in range(3):
            for k in range(3):
                here = pl.ds((k * RING + z) * channels, channels)
                short[pl.ds(i, 1), here] = slots[z, pl.ds(64 + 3 * i + k, 1), :]
        skip[:, lanes] = slots[z, pl.ds(64 + 9, 1), :]
    count = GAINS + SHARED
    total = slots[0, pl.ds(OWNED, count), :] + slots[1, pl.ds(OWNED, count), :]
    total += slots[2, pl.ds(OWNED, count), :] + slots[3, pl.ds(OWNED, count), :]
    for b in range(PLANE):
        lanes = pl.ds(b * channels, channels)
        gain_one[:, lanes] = total[b : b + 1]
        gain_two[:, lanes] = total[PLANE + b : PLANE + b + 1]
    total = total[GAINS:]
    middle[...] = total[:, :inner]
    first[...] = total[:EMB, inner : 2 * inner]
    bias_one[...] = total[:1, 2 * inner : 3 * inner]
    bias_two[...] = total[:1, 3 * inner :]


def tick_kernel(count, *refs):
    refs[count][...] = jnp.zeros_like(refs[count])


def run(kernel, outs, *args, scratch=(), name, micros=2.0, after=()):
    place = lambda a: pltpu.SMEM if a.dtype == jnp.int32 else pltpu.VMEM
    shapes = [jax.ShapeDtypeStruct(*o) for o in outs]
    count = len(args)

    def body(*refs):
        kernel(*refs[:count], *refs[count + len(after) :])

    return pl.pallas_call(
        body,
        out_shape=shapes,
        in_specs=[pl.BlockSpec(memory_space=place(a)) for a in args]
        + [pl.BlockSpec(memory_space=pl.ANY) for _ in after],
        out_specs=[pl.BlockSpec(memory_space=pltpu.VMEM)] * len(shapes),
        scratch_shapes=[pltpu.VMEM(*s) for s in scratch],
        compiler_params=pltpu.CompilerParams(vmem_limit_bytes=GRANT),
        cost_estimate=pl.CostEstimate(
            flops=int(SCALE * micros * 1e9), bytes_accessed=int(SCALE * micros * 3e6), transcendentals=0
        ),
        name=name,
    )(*args, *after)


def on_device(
    block_input,
    cotangent,
    lengths,
    in_proj,
    out_proj,
    up_proj,
    down_proj,
    first_gain,
    second_gain,
    short_filter,
    skip_bias,
    filter_in,
    filter_in_bias,
    filter_mid,
    filter_mid_bias,
    filter_out,
):
    seq_size = lax.axis_size("seq")
    fold = seq_size // CUBE
    member = lax.axis_index("seq") // fold
    ring_place = lax.axis_index("pos")
    rows, width = block_input.shape
    channels = width // RING
    lane = width // CUBE
    hidden = up_proj.shape[1]
    seq_len = LSEQ
    members = [[i * fold + o for i in range(CUBE)] for o in range(fold)]
    bundles = [list(range(i * fold, (i + 1) * fold)) for i in range(CUBE)]

    def hop(value, bit):
        pairs = [(i, ((i // fold) ^ bit) * fold + i % fold) for i in range(seq_size)]
        return lax.ppermute(value, "seq", pairs)

    def ring(value, shift):
        return lax.ppermute(value, "pos", [(i, (i + shift) % RING) for i in range(RING)])

    def near_ring(value, bit):
        return lax.ppermute(value, "pos", [(i, i ^ bit) for i in range(RING)])

    def to_rows(value):
        return lax.all_to_all(value, "pos", 0, 0, tiled=True)

    def swap(value):
        return lax.all_to_all(value, "seq", 0, 0, axis_index_groups=members, tiled=True)

    def gather(value):
        return lax.all_gather(value, "seq", axis=0, axis_index_groups=members, tiled=True)

    def scatter(value):
        return lax.psum_scatter(value, "seq", scatter_dimension=0, axis_index_groups=members, tiled=True)

    def settle(value, axis):
        if fold == 1:
            return value
        return lax.psum_scatter(
            value, "seq", scatter_dimension=axis, axis_index_groups=bundles, tiled=True
        )

    def widen(value, axis):
        if fold == 1:
            return value
        return lax.all_gather(value, "seq", axis=axis, axis_index_groups=bundles, tiled=True)

    info = jnp.stack([member % 2, member, ring_place, lengths[0]]).astype(jnp.int32)
    waiting = []
    latest = []

    def now(*values):
        waiting.extend(values)
        return values

    def step(kernel, outs, *args, **options):
        after = [v for v in latest + waiting if not any(v is a for a in args)]
        results = run(kernel, outs, *args, after=after, **options)
        waiting.clear()
        latest[:] = results[:1]
        return results

    def phase(*values, after=()):
        after = [v for v in latest + waiting + list(after) if not any(v is a for a in values)]
        waiting.clear()
        count = len(values) + len(after)
        mark, *passed = pl.pallas_call(
            functools.partial(tick_kernel, count),
            out_shape=[jax.ShapeDtypeStruct((8, 128), f32)]
            + [jax.ShapeDtypeStruct(v.shape, v.dtype) for v in values],
            in_specs=[pl.BlockSpec(memory_space=pl.ANY)] * count,
            out_specs=[pl.BlockSpec(memory_space=pltpu.VMEM)]
            + [pl.BlockSpec(memory_space=pl.ANY)] * len(values),
            input_output_aliases={i: i + 1 for i in range(len(values))},
            compiler_params=pltpu.CompilerParams(vmem_limit_bytes=GRANT),
            name="phase",
        )(*values, *after)
        latest[:] = [mark]
        return passed

    gain_one, gain_two = first_gain, second_gain
    in_turned = widen(in_proj.transpose(1, 0, 2), 1)
    out_shard, up_shard, down_shard = widen(out_proj, 1), widen(up_proj, 0), widen(down_proj, 1)
    out_shards = [out_shard] + [ring(out_shard, -j) for j in range(1, RING)]
    in_rows, layer_rows = step(
        weights_kernel,
        [((3 * channels, lane), bf16), ((2 * hidden, lane), bf16)],
        in_turned, up_shard, down_shard,
        name="weights", micros=0.2,
    )
    in_all = gather(in_rows)
    layer_got = swap(layer_rows)
    normed, inputs, cot = step(
        rows_kernel, [((rows, width), bf16)] * 3, block_input, cotangent, gain_one, name="rows", micros=0.2
    )
    normed_slots = [normed, ring(normed, -1)]

    channel_start = ring_place * channels
    features, times = (jnp.asarray(v) for v in embedding(seq_len))
    last_layer = lax.dynamic_slice_in_dim(filter_out, channel_start, channels, 1)
    tables, turns = spectral_tables(seq_len)
    tables = [jnp.asarray(t) for t in tables]
    turns = jnp.asarray(turns)
    lags = lax.dynamic_slice_in_dim(
        short_filter.reshape(3, 3, width), channel_start, channels, 2
    ).reshape(3, 3 * channels)
    skip = lax.dynamic_slice_in_dim(skip_bias, channel_start, channels, 0)[None]
    pair = ((2, seq_len, channels), f32)
    inner = filter_mid.shape[0]

    def with_width(kernel):
        return lambda info, *refs: kernel(info, width, *refs)

    (filter_hidden,) = step(
        hidden_kernel,
        [((seq_len, 4 * inner), f32)],
        features, filter_in, filter_in_bias[None], filter_mid, filter_mid_bias[None],
        name="hidden", micros=5,
    )
    (normed_slots[1],) = phase(normed_slots[1], after=[layer_got])
    normed_slots.append(ring(normed_slots[1], -1))
    (out_rows,) = step(stack_kernel, [((width, lane), bf16)], *out_shards, name="stack", micros=0.1)
    out_all = gather(out_rows)
    (layer_own,) = step(
        side_by_side, [((2 * hidden // CUBE + SPARE, width), bf16)], layer_got, name="layer_own", micros=0.2
    )
    (normed_slots[2],) = phase(normed_slots[2], after=[lags, skip])
    normed_slots.append(ring(normed_slots[2], -1))
    (spectrum,) = step(
        with_width(taps_kernel),
        [pair],
        info, filter_hidden, times, last_layer, turns, *tables,
        name="taps", micros=5,
    )
    layer_own, cot = phase(layer_own, cot, after=[normed_slots[3]])
    layer_slots = [layer_own, ring(layer_own, -1)]
    cot_all = gather(cot)

    projected, long_conv, driven_spectrum, gated, in_full = step(
        conv_kernel,
        [
            ((seq_len, 3 * channels), bf16),
            ((seq_len, channels), f32),
            pair,
            ((seq_len, channels), bf16),
            ((3 * channels, width), bf16),
        ],
        info, *normed_slots, in_all, lags, skip, spectrum, *tables,
        name="conv", micros=14,
    )
    gated, layer_slots[1] = phase(gated, layer_slots[1])
    gated = to_rows(gated)
    layer_slots = phase(*layer_slots, after=[gated, out_all])
    layer_slots += [ring(layer_slots[1], -1), ring(layer_slots[0], 1)]
    residual, second = step(
        out_kernel,
        [((rows, width), f32), ((rows, width), bf16)],
        info, gated, out_all, inputs, gain_two,
        name="out", micros=0.2,
    )

    second_sib, across, along = (hop(second, bit) for bit in (1, 2, 4))
    half = rows // 2
    now(second_sib, *layer_slots[2:])
    top, low = step(halves_kernel, [((half, width), bf16)] * 2, across, along, name="halves", micros=0.1)
    top, low = hop(top, 2), hop(low, 4)
    across_sib, along_sib, top_sib, low_sib = (hop(v, 1) for v in (across, along, top, low))
    wide = CUBE * rows // 2
    out_kept, out_given, back_kept, back_given, layer_grads = step(
        layer_kernel,
        [((wide, width), bf16)] * 4 + [((hidden, width), bf16)],
        info, second, second_sib, across, across_sib, along, along_sib, top, low, top_sib, low_sib,
        cot_all, *layer_slots,
        scratch=[((hidden // 2, width), f32)] * 2,
        name="layer", micros=22,
    )
    back_given, out_given, layer_grads = phase(back_given, out_given, layer_grads)
    layer_grads = lax.psum_scatter(layer_grads, "pos", scatter_dimension=0, tiled=True)

    block, part = ((rows, width), bf16), ((half, width), bf16)
    shares = [
        step(share_kernel, [block] * 3 + [part] * 2, kept, hop(given, 1), name="share", micros=0.1)
        for kept, given in ((back_kept, back_given), (out_kept, out_given))
    ]

    def turn(own, across, along, top, low):
        across, along = step(
            turn_kernel, [block] * 2, across, along, hop(top, 2), hop(low, 4), name="turn", micros=0.1
        )
        return own, hop(across, 2), hop(along, 4)

    back_parts = turn(*shares[0])
    grad_res, branch, second_gain_grad, grad_gated = step(
        branch_kernel,
        [((rows, width), f32), ((rows, width), bf16), ((1, width), f32), ((seq_len, channels), bf16)],
        info, *back_parts, residual, gain_two, cot, out_all,
        name="branch", micros=0.2,
    )
    (grad_gated,) = phase(grad_gated, after=[layer_grads])
    grad_gated = to_rows(grad_gated)
    (out_grad,) = step(
        out_grad_kernel, [((CUBE * width, lane), bf16)], gated, branch, name="out_grad", micros=0.1
    )
    out_parts = turn(*shares[1])
    out_grad = scatter(out_grad)
    (layer_sums,) = step(below_kernel, [((2 * hidden, lane), bf16)], layer_grads, name="layer_sum", micros=0.1)

    grad_projected, grad_taps, small = step(
        back_kernel,
        [((seq_len, 3 * channels), bf16), ((seq_len, channels), f32), ((16, channels), f32)],
        info, grad_gated, projected, long_conv, driven_spectrum, lags, skip, spectrum, turns, *tables,
        name="back", micros=15,
    )
    (packed,) = step(
        with_width(pack_kernel),
        [((PACKED, channels), f32)],
        info, grad_taps, filter_hidden, features, times, filter_mid, last_layer, small, second_gain_grad,
        name="pack", micros=0.1,
    )
    partial, packed = step(
        normed_kernel,
        [((seq_len, width), bf16), ((PACKED, channels), f32)],
        info, grad_projected, in_full, *normed_slots, gain_one, packed,
        name="normed", micros=0.2,
    )
    partial, packed, layer_sums = phase(partial, packed, layer_sums, after=[out_grad])
    grad_normed = lax.psum_scatter(partial, "pos", scatter_dimension=0, tiled=True)
    layer_sums = swap(layer_sums)
    if fold > 1:
        packed = lax.psum(packed, "seq", axis_index_groups=bundles)
    (in_grad,) = step(
        in_grad_kernel,
        [((3 * CUBE * channels, lane), bf16)],
        info, grad_projected, *normed_slots,
        name="in_grad", micros=0.1,
    )
    for bit in (1, 2, 4):
        packed = packed + hop(packed, bit)
    in_grad, packed, out_grad = phase(in_grad, packed, out_grad, after=[layer_sums, *out_parts[1:]])
    in_grad = swap(in_grad)
    out_slots = [
        lax.dynamic_slice_in_dim(out_grad, (ring_place + j) % RING * channels, channels) for j in range(RING)
    ]
    out_slots = [out_slots[0]] + [ring(out_slots[j], j) for j in range(1, RING)]
    packed = packed.astype(bf16)
    packed_slots = [packed, near_ring(packed, 1)]
    packed_slots += [near_ring(v, 2) for v in packed_slots]
    up_grad, down_grad = step(
        layer_end_kernel, [((lane, hidden), f32), ((hidden, lane), f32)], layer_sums, name="layer_end"
    )
    (block_output,) = step(
        finish_kernel, [((rows, width), bf16)], residual, *out_parts, name="finish", micros=0.1
    )
    (input_grad,) = step(
        end_kernel, [((rows, width), bf16)], grad_normed, inputs, gain_one, grad_res, name="end", micros=1
    )
    (out_grad,) = step(out_end_kernel, [((channels, lane), f32)], *out_slots, name="out_end")
    small_grads = step(
        unpack_kernel,
        [
            ((1, width), f32),
            ((1, width), f32),
            ((3, 3 * width), f32),
            ((1, width), f32),
            ((EMB, inner), f32),
            ((1, inner), f32),
            ((inner, inner), f32),
            ((1, inner), f32),
            ((inner, width), f32),
        ],
        info, *packed_slots,
        scratch=[((RING, PACKED, channels), f32)],
        name="unpack",
    )
    (in_grad,) = step(in_end_kernel, [((3, lane, channels), f32)], in_grad, name="in_end")
    return (
        block_output,
        input_grad,
        settle(in_grad, 1).transpose(1, 0, 2),
        settle(out_grad, 1),
        settle(up_grad, 0),
        settle(down_grad, 1),
        small_grads[0].reshape(width),
        small_grads[1].reshape(width),
        small_grads[2],
        small_grads[3].reshape(width),
        small_grads[4],
        small_grads[5].reshape(inner),
        small_grads[6],
        small_grads[7].reshape(inner),
        small_grads[8],
    )


def solution(mesh):
    rows = P(("seq", "pos"), None)
    in_place, down_place, up_place = P("seq", None, "pos"), P("pos", "seq"), P("seq", "pos")
    return jax.shard_map(
        on_device,
        mesh=mesh,
        in_specs=(rows, rows, P("seq"), in_place, down_place, up_place, down_place) + (P(),) * 9,
        out_specs=(rows, rows, in_place, down_place, up_place, down_place) + (P(),) * 9,
        check_vma=False,
    )
```
